128 devices in a mesh: gx: 16 (over z, x_hi, core), gy: 8 (over y, x_lo).
Axes of the slice: x: 4 (x_hi: 2, x_lo: 2; x = x_hi * 2 + x_lo), y: 4, z: 4, core: 2. Of those that a mesh axis runs over, the one named last changes fastest.
Arguments:
- rhs: float32 [3, 25, 64, 64, 128], P(None, None, 'gx', 'gy'), may hold values from -6 to 6
- kappa: float32 [64, 64, 128], P('gx', 'gy'), may hold values from 0.1 to 10
- mass: float32 [64, 64, 128], P('gx', 'gy'), may hold values from 0.05 to 2
- stiffness: float32 [150, 150], replicated, as said below
- mass_matrix: float32 [150, 150], replicated, as said below
- prolong: float32 [3, 25], replicated, may hold values from 0.5 to 1.5
Outputs:
- solution: float32 [3, 25, 64, 64, 128], P(None, None, 'gx', 'gy')
- residual: float32 [3, 25, 64, 64, 128], P(None, None, 'gx', 'gy')
- coarse: float32 [16, 64, 128], P('gx', 'gy')
The draws below stay inside these ranges and needn't reach their ends.
Inputs may be any that keep to these rules, and one draw needn't show every extreme that they name: `stiffness`: symmetric, with a diagonal larger than the sum of magnitudes of the rest of its row. `mass_matrix`: symmetric, with a diagonal larger than the sum of magnitudes of the rest of its row.
All inputs are finite; a program needn't handle non-finite values.
Results may differ from the reference program's by a relative error of at most 0.0035.
Values sent between devices are 32-bit elements; how exact they have to be, the bound alone decides.
No kernel may reach another device: no remote copies, remote signals or barrier semaphores. Data moves between devices by JAX's collectives and lax.ppermute only.
A program may use at most 64 MiB of HBM per device.

```python
import math
import jax
import jax.numpy as jnp
from jax import lax

NODES = 25
LOCAL = 150
EX = 4
EZ = 128
ITERS = 3
SWEEPS = 8
NX = 64
NY = 64
N_GX = 16


def dominant_matrix(key):
    entries = jax.random.uniform(key, (LOCAL, LOCAL), jnp.float32, -1.0, 1.0)
    symmetric = 0.5 * (entries + entries.T)
    extra = jax.random.uniform(jax.random.fold_in(key, 7), (LOCAL,), jnp.float32, 0.0, 20.0)
    eye_mask = jnp.eye(LOCAL, dtype=jnp.float32)
    diagonal = 160.0 + extra
    return (symmetric * (1.0 - eye_mask) + eye_mask * diagonal[:, None]) / 160.0


def draw_stiffness(key, part):
    return dominant_matrix(jax.random.fold_in(key, 11))


def draw_mass_matrix(key, part):
    return dominant_matrix(jax.random.fold_in(key, 23))


def steps_of(key, dims, shards, least, high):
    level = 1.0
    for position, blocks in shards:
        heights = jax.random.uniform(jax.random.fold_in(jax.random.fold_in(key, 6), position), (blocks,), jnp.float32, least / len(shards), high / len(shards))
        level = level * jnp.repeat(jnp.exp(heights), dims[position] // blocks).reshape((-1,) + (1,) * (len(dims) - 1 - position))
    return level


def gaussian(rng, extent, scale, most, cuts=(), held_as=jnp.bfloat16):
    level = steps_of(rng, extent, cuts, -0.22, 0.18) if cuts else 1.0
    result = jax.random.normal(rng, extent, jnp.float32) * scale * level
    return jnp.minimum(jnp.maximum(result, -most), most).astype(held_as)


def setup_inputs(seed: int = 0) -> dict:
    keys = jax.random.split(jax.random.key(seed), 7)
    return {
        "rhs": gaussian(keys[0], (3, NODES, NX, NY, EZ), 1.0, 6.0, ((2, 16), (3, 8)), jnp.float32),
        "kappa": jnp.clip(jnp.exp(math.log(10.0) - 4.6051702 * jax.random.uniform(keys[1], (NX, NY, EZ), jnp.float32) ** steps_of(keys[1], (NX, NY, EZ), ((0, 16), (1, 8)), -0.2, 0.2)), 0.1, 10.0),
        "mass": jnp.clip(jnp.exp(math.log(2.0) - 3.6888794 * jax.random.uniform(keys[2], (NX, NY, EZ), jnp.float32) ** steps_of(keys[2], (NX, NY, EZ), ((0, 16), (1, 8)), -0.2, 0.2)), 0.05, 2.0),
        "stiffness": draw_stiffness(jax.random.fold_in(keys[6], 71), 0),
        "mass_matrix": draw_mass_matrix(jax.random.fold_in(keys[6], 71), 0),
        "prolong": jnp.clip(jax.random.uniform(keys[5], (3, NODES), jnp.float32, 0.5, 1.5), 0.5, 1.5),
    }


def operate(field, kappa, mass, stacked):
    trace_x, trace_y, trace_z = field[0], field[1], field[2]
    local = jnp.concatenate([trace_x, jnp.roll(trace_x, -1, axis=1), trace_y, jnp.roll(trace_y, -1, axis=2), trace_z, jnp.roll(trace_z, -1, axis=3)], 0)
    prod = jnp.einsum("ij,jxyz->ixyz", stacked, local, precision=lax.Precision.HIGHEST)
    half = prod.shape[0] // 2
    weighted = kappa[None] * prod[:half] + mass[None] * prod[half:]
    nodes = trace_x.shape[0]
    parts = weighted.reshape((6, nodes) + kappa.shape)
    out_x = parts[0] + jnp.roll(parts[1], 1, axis=1)
    out_y = parts[2] + jnp.roll(parts[3], 1, axis=2)
    out_z = parts[4] + jnp.roll(parts[5], 1, axis=3)
    return jnp.stack([out_x, out_y, out_z], 0)


def reference(rhs, kappa, mass, stiffness, mass_matrix, prolong):
    stacked = jnp.concatenate([stiffness, mass_matrix], 0)
    iterate = jnp.zeros_like(rhs)
    residual, direction = rhs, rhs
    norm_now = jnp.sum(residual * residual)
    for step in range(ITERS):
        image = operate(direction, kappa, mass, stacked)
        alpha = norm_now / jnp.sum(direction * image)
        iterate = iterate + alpha * direction
        residual = residual - alpha * image
        norm_next = jnp.sum(residual * residual)
        direction = residual + (norm_next / norm_now) * direction
        norm_now = norm_next
    slabs = residual.reshape((3, NODES, N_GX, EX) + residual.shape[3:])
    load = jnp.sum(slabs, axis=(0, 1, 3)) / 75.0
    coarse = jnp.zeros_like(load)
    for sweep in range(SWEEPS):
        coarse = (load + jnp.roll(coarse, 1, axis=0) + jnp.roll(coarse, -1, axis=0)) / 2.2
    spread = jnp.repeat(coarse, EX, axis=0)
    solution = iterate + prolong[:, :, None, None, None] * spread[None, None]
    return solution, residual, coarse
```

```python
import jax
import jax.numpy as jnp
import numpy as np
from jax import lax
from jax.experimental import pallas as pl
from jax.experimental.pallas import tpu as pltpu
from jax.sharding import PartitionSpec as P

ITERS = 3
SWEEPS = 8
F, A, AP = 3, 25, 32
LX, LY, LZ = 4, 8, 128
CELLS = LX * LY
FACE = A * CELLS
ROWS = F * FACE
PADDED = ROWS + (AP - A) * CELLS
f32, bf16 = jnp.float32, jnp.bfloat16
VM = pl.BlockSpec(memory_space=pltpu.VMEM)
SM = pl.BlockSpec(memory_space=pltpu.SMEM)


def shifted(value, axis, by):
    n = lax.axis_size(axis)
    return lax.ppermute(value, axis, [(i, (i + by) % n) for i in range(n)])


def near_swap(value, axis):
    n = lax.axis_size(axis)
    return lax.ppermute(value, axis, [(i, i ^ 1) for i in range(n)])


def far_swap(value, axis):
    n = lax.axis_size(axis)
    pairs = [(i, (i + 1) % n) if i % 2 else (i, (i - 1) % n) for i in range(n)]
    return lax.ppermute(value, axis, pairs)


def halves(v):
    hi = v.astype(bf16)
    lo = (v - hi.astype(f32)).astype(bf16)
    return hi, lo


def apply_operator(v_ref, ux_ref, uy_ref, k_ref, m_ref, scale, wh_ref, wl_ref, out_ref, up_x, low_x, up_y, low_y):
    wh = wh_ref[...]
    wl = wl_ref[...]

    def face(f, x, y):
        if f == 0 and x == LX:
            return ux_ref[pl.ds(y, AP, stride=LY), :]
        if f == 1 and y == LY:
            return uy_ref[pl.ds(x, AP, stride=LX), :]
        return v_ref[pl.ds(f * FACE + x * LY + y, AP, stride=CELLS), :]

    def put(f, x, y, value):
        out_ref[pl.ds(f * FACE + x * LY + y, A, stride=CELLS), :] = value[:A]

    t0 = [halves(face(0, 0, y)) for y in range(LY)]
    carry = None
    for x in range(LX):
        t0_next = [halves(face(0, x + 1, y)) for y in range(LY)]
        t1 = [halves(face(1, x, y)) for y in range(LY + 1)]
        his, los = [], []
        for y in range(LY):
            z = face(2, x, y)
            t2 = halves(z)
            t2u = halves(pltpu.roll(z, LZ - 1, 1))
            six = (t0[y], t0_next[y], t1[y], t1[y + 1], t2, t2u)
            his.append(jnp.concatenate([b[0] for b in six], 0))
            los.append(jnp.concatenate([b[1] for b in six], 0))
        t0 = t0_next
        hi = jnp.concatenate(his, 1)
        lo = jnp.concatenate(los, 1)
        prod = jnp.dot(wh, hi, preferred_element_type=f32)
        prod += jnp.dot(wh, lo, preferred_element_type=f32)
        prod += jnp.dot(wl, hi, preferred_element_type=f32)
        parts = []
        for y in range(LY):
            k = k_ref[x * LY + y : x * LY + y + 1, :] * scale
            m = m_ref[x * LY + y : x * LY + y + 1, :] * scale
            cols = slice(y * LZ, (y + 1) * LZ)
            w = prod[: 6 * AP, cols] * k + prod[6 * AP :, cols] * m
            parts.append([w[b * AP : (b + 1) * AP] for b in range(6)])
        for y in range(LY):
            wlx, wux, wly, wuy, wlz, wuz = parts[y]
            put(0, x, y, wlx if x == 0 else wlx + carry[y])
            put(1, x, y, wly if y == 0 else wly + parts[y - 1][3])
            put(2, x, y, wlz + pltpu.roll(wuz, 1, 1))
            if x == 0 and low_x is not None:
                low_x[pl.ds(y, A, stride=LY), :] = wlx[:A]
            if x == LX - 1:
                up_x[pl.ds(y, A, stride=LY), :] = wux[:A]
        if low_y is not None:
            low_y[pl.ds(x, A, stride=LX), :] = parts[0][2][:A]
        up_y[pl.ds(x, A, stride=LX), :] = parts[LY - 1][3][:A]
        carry = [parts[y][1] for y in range(LY)]


def route(even, up, low, near, far):
    near[...] = jnp.where(even, up[...], low[...])
    far[...] = jnp.where(even, low[...], up[...])


def mean_eigenvalue(st_ref, traces_ref, total):
    st = st_ref[...].reshape(-1, 2, LZ)
    sums = jnp.sum(jnp.sum(st, 0), axis=1, keepdims=True)
    return (sums[0:1] * traces_ref[0] + sums[1:2] * traces_ref[1]) * (1.0 / (75.0 * total))


def first_kernel(even_ref, rhs_ref, hx_ref, hy_ref, k_ref, m_ref, wh_ref, wl_ref,
                 p_ref, snx, sfx, sny, sfy, v, ux, uy, upx, lowx, upy, lowy):
    v[:ROWS] = rhs_ref[...]
    v[ROWS:] = jnp.zeros((PADDED - ROWS, LZ), f32)
    ux[: A * LY] = hx_ref[...]
    ux[A * LY :] = jnp.zeros(((AP - A) * LY, LZ), f32)
    uy[: A * LX] = hy_ref[...]
    uy[A * LX :] = jnp.zeros(((AP - A) * LX, LZ), f32)
    apply_operator(v, ux, uy, k_ref, m_ref, 1.0, wh_ref, wl_ref, p_ref, upx, lowx, upy, lowy)
    route(even_ref[0] == 0, upx, lowx, snx, sfx)
    route(even_ref[1] == 0, upy, lowy, sny, sfy)


def next_vector(even_ref, p_ref, prev_ref, hx_ref, hy_ref, snx, sfx, sny, sfy, rnx, rfx, rny, rfy, scale, v, ux, uy):
    even_x = even_ref[0] == 0
    even_y = even_ref[1] == 0
    v[:ROWS] = p_ref[...] * scale - prev_ref[...]
    v[ROWS:] = jnp.zeros((PADDED - ROWS, LZ), f32)
    below_x = jnp.where(even_x, rfx[...], rnx[...]) * scale
    for a in range(A):
        rows = slice(a * CELLS, a * CELLS + LY)
        v[rows, :] = v[rows, :] + below_x[a * LY : (a + 1) * LY]
    below_y = jnp.where(even_y, rfy[...], rny[...]) * scale
    first = pl.ds(FACE, A * LX, stride=LY)
    v[first, :] = v[first, :] + below_y
    above_x = jnp.where(even_x, snx[...] + rnx[...], sfx[...] + rfx[...])
    ux[: A * LY] = above_x * scale - hx_ref[...]
    ux[A * LY :] = jnp.zeros(((AP - A) * LY, LZ), f32)
    above_y = jnp.where(even_y, sny[...] + rny[...], sfy[...] + rfy[...])
    uy[: A * LX] = above_y * scale - hy_ref[...]
    uy[A * LX :] = jnp.zeros(((AP - A) * LX, LZ), f32)


def node_sum(value):
    return jnp.sum(value.reshape(-1, LY, LZ), 0)


def second_kernel(even_ref, traces_ref, p_ref, rhs_ref, hx_ref, hy_ref, snx, sfx, sny, sfy, rnx, rfx, rny, rfy,
                  st_ref, k_ref, m_ref, wh_ref, wl_ref,
                  v1_ref, ux1_ref, uy1_ref, p1_ref, tnx, tfx, tny, tfy, sums_ref, inv_ref,
                  v, ux, uy, upx, lowx, upy, lowy, *, total):
    inv = 1.0 / mean_eigenvalue(st_ref, traces_ref, total)
    inv_ref[...] = jnp.broadcast_to(inv, (8, LZ))
    next_vector(even_ref, p_ref, rhs_ref, hx_ref, hy_ref, snx, sfx, sny, sfy, rnx, rfx, rny, rfy, inv, v, ux, uy)
    v0 = rhs_ref[...]
    v1 = v[:ROWS]
    v1_ref[...] = v1
    ux1_ref[...] = ux[: A * LY]
    uy1_ref[...] = uy[: A * LX]
    sums_ref[0:8] = node_sum(v0)
    sums_ref[8:16] = node_sum(v1)
    sums_ref[16:24] = node_sum(v0 * v0)
    sums_ref[24:32] = node_sum(v0 * v1)
    sums_ref[32:40] = node_sum(v1 * v1)
    apply_operator(v, ux, uy, k_ref, m_ref, inv, wh_ref, wl_ref, p1_ref, upx, lowx, upy, lowy)
    route(even_ref[0] == 0, upx, lowx, tnx, tfx)
    route(even_ref[1] == 0, upy, lowy, tny, tfy)


def third_kernel(even_ref, p_ref, prev_ref, hx_ref, hy_ref, snx, sfx, sny, sfy, rnx, rfx, rny, rfy,
                 inv_ref, sums1_ref, k_ref, m_ref, wh_ref, wl_ref,
                 v2_ref, p2_ref, upx, upy, loads_ref, mom_ref, v, ux, uy):
    one = jnp.float32(1.0)
    next_vector(even_ref, p_ref, prev_ref, hx_ref, hy_ref, snx, sfx, sny, sfy, rnx, rfx, rny, rfy, one, v, ux, uy)
    v1 = prev_ref[...]
    v2 = v[:ROWS]
    v2_ref[...] = v2
    loads_ref[0:16] = sums1_ref[0:16]
    loads_ref[16:24] = node_sum(v2)
    m3 = node_sum(v1 * v2)
    m4 = node_sum(v2 * v2)
    apply_operator(v, ux, uy, k_ref, m_ref, inv_ref[0:1], wh_ref, wl_ref, p2_ref, upx, None, upy, None)
    p2 = p2_ref[...]
    loads_ref[24:32] = node_sum(p2)
    loads_ref[32:40] = node_sum(upx[...])
    energy = node_sum(v[:ROWS] * p2) + node_sum(ux[: A * LY] * upx[...])
    tail = jnp.sum(uy[: A * LX] * upy[...], 0, keepdims=True)

    def row(tile):
        return jnp.sum(tile, 0, keepdims=True)

    mom_ref[0:1] = row(sums1_ref[16:24])
    mom_ref[1:2] = row(sums1_ref[24:32])
    mom_ref[2:3] = row(sums1_ref[32:40])
    mom_ref[3:4] = row(m3)
    mom_ref[4:5] = row(m4)
    mom_ref[5:6] = row(energy) + tail
    mom_ref[6:7] = jnp.sum(upy[...], 0, keepdims=True)
    mom_ref[7:8] = jnp.zeros((1, LZ), f32)


def middle_kernel(me_ref, g_ref, mom_ref, loads_ref, out_ref, *, nx, ny):
    below = lax.rem(me_ref[1] + ny - 1, ny)
    tiles = mom_ref[...].reshape(ny, 8, LZ)
    total = jnp.sum(tiles, 0)
    edge = mom_ref[pl.ds(below * 8 + 6, 1), :]
    image = loads_ref[24:32]
    at_first = lax.broadcasted_iota(jnp.int32, (8, LZ), 0) == 0
    image = image + jnp.where(at_first, jnp.broadcast_to(edge, (8, LZ)), 0.0)
    own = [loads_ref[0:8], loads_ref[8:16], loads_ref[16:24], image]
    above = loads_ref[32:40]
    for to in range(nx):
        g = g_ref[to]
        for k in range(4):
            piece = own[k] * g
            if k == 3:
                piece = piece + above * g_ref[nx + to]
            out_ref[to * 40 + k * 8 : to * 40 + (k + 1) * 8] = piece
        out_ref[to * 40 + 32 : to * 40 + 40] = total


def conjugate_gradient(m):
    def dot(a, b):
        s = None
        for i, ai in enumerate(a):
            for j, bj in enumerate(b):
                t = ai * bj * m[i + j]
                s = t if s is None else s + t
        return s

    def add(a, b, factor):
        longer = []
        for i in range(max(len(a), len(b))):
            if i >= len(b):
                longer.append(a[i])
            elif i >= len(a):
                longer.append(factor * b[i])
            else:
                longer.append(a[i] + factor * b[i])
        return longer

    def image(a):
        return [a[0]] + [a[i] + a[i - 1] for i in range(1, len(a))] + [a[-1]]

    one = jnp.ones((1, 1), f32)
    iterate, residual, direction = [], [one], [one]
    norm = m[0]
    for step in range(ITERS):
        img = image(direction)
        alpha = norm / dot(direction, img)
        iterate = add(iterate, direction, alpha)
        residual = add(residual, img, -alpha)
        if step < ITERS - 1:
            norm_next = dot(residual, residual)
            direction = add(residual, direction, norm_next / norm)
            norm = norm_next
    return iterate, residual


def last_kernel(prolong_ref, got_ref, inv_ref, rhs_ref, v1_ref, v2_ref, p2_ref, rx_ref, ry_ref,
                sol_ref, res_ref, coarse_ref, *, nx):
    got = jnp.sum(got_ref[...].reshape(nx, 5, 8, LZ), 0)
    sums = jnp.sum(got[4], axis=1, keepdims=True)
    m = [sums[k : k + 1] for k in range(6)]
    m[5] = m[5] - m[4]
    x, d = conjugate_gradient(m)
    inv = inv_ref[0:1, 0:1]
    x = [t * inv for t in x]
    coarse = d[0] * got[0] + d[1] * got[1] + (d[2] - d[3]) * got[2] + d[3] * got[3]
    coarse_ref[...] = coarse
    d2 = d[2] - d[3]
    for f in range(F):
        for a in range(A):
            at = (f * A + a) * CELLS
            spread = coarse * prolong_ref[f * A + a]
            for c in range(LX):
                rows = slice(at + c * LY, at + (c + 1) * LY)
                v0, v1, v2 = rhs_ref[rows, :], v1_ref[rows, :], v2_ref[rows, :]
                img = p2_ref[rows, :]
                if f == 0 and c == 0:
                    img = img + rx_ref[a * LY : (a + 1) * LY, :]
                sol_ref[rows, :] = x[0] * v0 + x[1] * v1 + x[2] * v2 + spread
                res_ref[rows, :] = d[0] * v0 + d[1] * v1 + d2 * v2 + d[3] * img
    first = pl.ds(FACE, A * LX, stride=LY)
    res_ref[first, :] = res_ref[first, :] + d[3] * ry_ref[...]


def jacobi_weights(n):
    coarse = np.zeros(n)
    load = np.zeros(n)
    load[0] = 1.0
    for _ in range(SWEEPS):
        coarse = (load + np.roll(coarse, 1) + np.roll(coarse, -1)) / 2.2
    return coarse / 75.0


def struct(*shape):
    return jax.ShapeDtypeStruct(shape, f32)


PARAMS = pltpu.CompilerParams(vmem_limit_bytes=40 * 1024 * 1024)


def shards(rhs, kappa, mass, stiffness, mass_matrix, prolong):
    nx, ny = lax.axis_size("gx"), lax.axis_size("gy")
    me_x, me_y = lax.axis_index("gx"), lax.axis_index("gy")
    both = ("gx", "gy")
    vx, vy = A * LY, A * LX

    hx = shifted(rhs[0, :, 0].reshape(vx, LZ), "gx", -1)
    hy = shifted(rhs[1, :, :, 0].reshape(vy, LZ), "gy", -1)

    stats = jnp.stack([jnp.sum(kappa, (0, 1)), jnp.sum(mass, (0, 1))], 0)
    stats = lax.all_to_all(jnp.broadcast_to(stats[None], (nx * ny, 2, LZ)), both, 0, 0, tiled=True)
    stats = stats.reshape(nx * ny * 2, LZ)
    traces = jnp.stack([jnp.trace(stiffness), jnp.trace(mass_matrix)])

    def padded(matrix):
        blocks = jnp.pad(matrix.reshape(6, A, 6, A), ((0, 0), (0, AP - A), (0, 0), (0, AP - A)))
        return blocks.reshape(6 * AP, 6 * AP)

    weights = jnp.concatenate([padded(stiffness), padded(mass_matrix)], 0)
    wh = lax.reduce_precision(weights, 8, 7)
    wl = (weights - wh).astype(bf16)
    wh = wh.astype(bf16)

    even = jnp.stack([me_x % 2, me_y % 2])
    me = jnp.stack([me_x, me_y])
    table = jacobi_weights(nx)
    index = np.arange(nx)
    rows = np.stack([np.concatenate([table[(index - p) % nx], table[(index - p - 1) % nx]]) for p in range(nx)])
    g = lax.dynamic_index_in_dim(jnp.asarray(rows, f32), me_x, 0, keepdims=False)

    rhs2 = rhs.reshape(ROWS, LZ)
    k2 = kappa.reshape(CELLS, LZ)
    m2 = mass.reshape(CELLS, LZ)
    sends = [struct(vx, LZ), struct(vx, LZ), struct(vy, LZ), struct(vy, LZ)]
    field = [pltpu.VMEM((PADDED, LZ), f32), pltpu.VMEM((AP * LY, LZ), f32), pltpu.VMEM((AP * LX, LZ), f32)]
    edges = [pltpu.VMEM((vx, LZ), f32)] * 2 + [pltpu.VMEM((vy, LZ), f32)] * 2

    def swap(s):
        far_x = far_swap(s[1], "gx")
        far_y = far_swap(s[3], "gy")
        near_y = near_swap(s[2], "gy")
        near_x = near_swap(s[0], "gx")
        return [near_x, far_x, near_y, far_y]

    p0, *s = pl.pallas_call(
        first_kernel,
        out_shape=[struct(ROWS, LZ)] + sends,
        in_specs=[SM] + [VM] * 7,
        out_specs=[VM] * 5,
        scratch_shapes=field + edges,
        compiler_params=PARAMS,
        name="first",
    )(even, rhs2, hx, hy, k2, m2, wh, wl)
    r = swap(s)

    def second(*refs):
        second_kernel(*refs, total=float(nx * ny * CELLS * LZ))

    v1, ux1, uy1, p1, *rest = pl.pallas_call(
        second,
        out_shape=[struct(ROWS, LZ), struct(vx, LZ), struct(vy, LZ), struct(ROWS, LZ)] + sends + [struct(40, LZ), struct(8, LZ)],
        in_specs=[SM, SM] + [VM] * 17,
        out_specs=[VM] * 10,
        scratch_shapes=field + edges,
        compiler_params=PARAMS,
        name="second",
    )(even, traces, p0, rhs2, hx, hy, *s, *r, stats, k2, m2, wh, wl)
    s, (sums, inv) = rest[:4], rest[4:]
    r = swap(s)

    v2, p2, upx, upy, loads, mom = pl.pallas_call(
        third_kernel,
        out_shape=[struct(ROWS, LZ), struct(ROWS, LZ), struct(vx, LZ), struct(vy, LZ), struct(40, LZ), struct(8, LZ)],
        in_specs=[SM] + [VM] * 18,
        out_specs=[VM] * 6,
        scratch_shapes=field,
        compiler_params=PARAMS,
        name="third",
    )(even, p1, v1, ux1, uy1, *s, *r, inv, sums, k2, m2, wh, wl)
    rx = shifted(upx, "gx", 1)
    ry = shifted(upy, "gy", 1)
    mom = lax.all_to_all(jnp.broadcast_to(mom[None], (ny, 8, LZ)), "gy", 0, 0, tiled=True)

    def middle(*refs):
        middle_kernel(*refs, nx=nx, ny=ny)

    pieces = pl.pallas_call(
        middle,
        out_shape=struct(nx * 40, LZ),
        in_specs=[SM, SM, VM, VM],
        out_specs=VM,
        compiler_params=PARAMS,
        name="middle",
    )(me, g, mom.reshape(ny * 8, LZ), loads)
    got = lax.all_to_all(pieces.reshape(nx, 40, LZ), "gx", 0, 0, tiled=True)

    def last(*refs):
        last_kernel(*refs, nx=nx)

    sol, res, coarse = pl.pallas_call(
        last,
        out_shape=[struct(ROWS, LZ), struct(ROWS, LZ), struct(LY, LZ)],
        in_specs=[SM] + [VM] * 8,
        out_specs=[VM] * 3,
        compiler_params=PARAMS,
        name="last",
    )(prolong.reshape(-1), got.reshape(nx * 40, LZ), inv, rhs2, v1, v2, p2, rx, ry)
    return sol.reshape(rhs.shape), res.reshape(rhs.shape), coarse[None]


def solution(mesh):
    placed = (
        P(None, None, "gx", "gy", None),
        P("gx", "gy", None),
        P("gx", "gy", None),
        P(),
        P(),
        P(),
    )
    return jax.shard_map(
        shards,
        mesh=mesh,
        in_specs=placed,
        out_specs=(
            P(None, None, "gx", "gy", None),
            P(None, None, "gx", "gy", None),
            P("gx", "gy", None),
        ),
        check_vma=False,
    )
```

```python
import jax
import jax.numpy as jnp
import numpy as np
from jax import lax
from jax.experimental import pallas as pl
from jax.experimental.pallas import tpu as pltpu
from jax.sharding import PartitionSpec as P

ITERS = 3
SWEEPS = 8
F, A, AP = 3, 25, 32
LX, LY, LZ = 4, 8, 128
CELLS = LX * LY
FACE = A * CELLS
ROWS = F * FACE
PADDED = ROWS + (AP - A) * CELLS
f32, bf16 = jnp.float32, jnp.bfloat16
VM = pl.BlockSpec(memory_space=pltpu.VMEM)
SM = pl.BlockSpec(memory_space=pltpu.SMEM)
ANY = pl.BlockSpec(memory_space=pl.ANY)


def shifted(value, axis, by):
    n = lax.axis_size(axis)
    return lax.ppermute(value, axis, [(i, (i + by) % n) for i in range(n)])


def near_swap(value, axis):
    n = lax.axis_size(axis)
    return lax.ppermute(value, axis, [(i, i ^ 1) for i in range(n)])


def far_swap(value, axis):
    n = lax.axis_size(axis)
    pairs = [(i, (i + 1) % n) if i % 2 else (i, (i - 1) % n) for i in range(n)]
    return lax.ppermute(value, axis, pairs)


def halves(v):
    hi = v.astype(bf16)
    lo = (v - hi.astype(f32)).astype(bf16)
    return hi, lo


def apply_operator(v_ref, ux_ref, uy_ref, k_ref, m_ref, scale, wh_ref, wl_ref, out_ref, up_x, low_x, up_y, low_y):
    wh = wh_ref[...]
    wl = wl_ref[...]

    def face(f, x, y):
        if f == 0 and x == LX:
            return ux_ref[pl.ds(y, AP, stride=LY), :]
        if f == 1 and y == LY:
            return uy_ref[pl.ds(x, AP, stride=LX), :]
        return v_ref[pl.ds(f * FACE + x * LY + y, AP, stride=CELLS), :]

    def put(f, x, y, value):
        out_ref[pl.ds(f * FACE + x * LY + y, A, stride=CELLS), :] = value[:A]

    t0 = [halves(face(0, 0, y)) for y in range(LY)]
    carry = None
    for x in range(LX):
        t0_next = [halves(face(0, x + 1, y)) for y in range(LY)]
        t1 = [halves(face(1, x, y)) for y in range(LY + 1)]
        his, los = [], []
        for y in range(LY):
            z = face(2, x, y)
            t2 = halves(z)
            t2u = halves(pltpu.roll(z, LZ - 1, 1))
            six = (t0[y], t0_next[y], t1[y], t1[y + 1], t2, t2u)
            his.append(jnp.concatenate([b[0] for b in six], 0))
            los.append(jnp.concatenate([b[1] for b in six], 0))
        t0 = t0_next
        hi = jnp.concatenate(his, 1)
        lo = jnp.concatenate(los, 1)
        prod = jnp.dot(wh, hi, preferred_element_type=f32)
        prod += jnp.dot(wh, lo, preferred_element_type=f32)
        prod += jnp.dot(wl, hi, preferred_element_type=f32)
        parts = []
        for y in range(LY):
            k = k_ref[x * LY + y : x * LY + y + 1, :] * scale
            m = m_ref[x * LY + y : x * LY + y + 1, :] * scale
            cols = slice(y * LZ, (y + 1) * LZ)
            w = prod[: 6 * AP, cols] * k + prod[6 * AP :, cols] * m
            parts.append([w[b * AP : (b + 1) * AP] for b in range(6)])
        for y in range(LY):
            wlx, wux, wly, wuy, wlz, wuz = parts[y]
            put(0, x, y, wlx if x == 0 else wlx + carry[y])
            put(1, x, y, wly if y == 0 else wly + parts[y - 1][3])
            put(2, x, y, wlz + pltpu.roll(wuz, 1, 1))
            if x == 0 and low_x is not None:
                low_x[pl.ds(y, A, stride=LY), :] = wlx[:A]
            if x == LX - 1:
                up_x[pl.ds(y, A, stride=LY), :] = wux[:A]
        if low_y is not None:
            low_y[pl.ds(x, A, stride=LX), :] = parts[0][2][:A]
        up_y[pl.ds(x, A, stride=LX), :] = parts[LY - 1][3][:A]
        carry = [parts[y][1] for y in range(LY)]


def is_even(axis):
    return lax.rem(lax.axis_index(axis), 2) == 0


def route(even, up, low, near, far):
    near[...] = jnp.where(even, up[...], low[...])
    far[...] = jnp.where(even, low[...], up[...])


def mean_eigenvalue(st_ref, traces_ref, total):
    st = st_ref[...].reshape(-1, 2, LZ)
    sums = jnp.sum(jnp.sum(st, 0), axis=1, keepdims=True)
    return (sums[0:1] * traces_ref[0:1, 0:1] + sums[1:2] * traces_ref[1:2, 0:1]) * (1.0 / (75.0 * total))


def edge_kernel(rhs_ref, k_ref, m_ref, fx_ref, fy_ref, st_ref, sem_x, sem_y, *, devices):
    face_x = pltpu.make_async_copy(rhs_ref.at[0, :, 0], fx_ref, sem_x)
    face_y = pltpu.make_async_copy(rhs_ref.at[1, :, :, 0], fy_ref, sem_y)
    face_x.start()
    face_y.start()
    both = jnp.concatenate([jnp.sum(k_ref[...], 0, keepdims=True), jnp.sum(m_ref[...], 0, keepdims=True)], 0)
    st_ref[...] = jnp.broadcast_to(both[None], (devices, 2, LZ))
    face_x.wait()
    face_y.wait()


def weight_kernel(s_ref, m_ref, wh_ref, wl_ref, traces_ref):
    n, padded = 6 * A, 6 * AP
    r = lax.broadcasted_iota(jnp.int32, (padded, n), 0)
    c = lax.broadcasted_iota(jnp.int32, (padded, n), 1)
    node = lax.rem(r, AP)
    place = jnp.where((node < A) & (lax.div(r, AP) * A + node == c), 1.0, 0.0).astype(bf16)
    diagonal = lax.broadcasted_iota(jnp.int32, (n, n), 0) == lax.broadcasted_iota(jnp.int32, (n, n), 1)
    for i, ref in enumerate((s_ref, m_ref)):
        v = ref[...]
        for part, out in zip(halves(v), (wh_ref, wl_ref)):
            rows = jnp.dot(place, part, preferred_element_type=f32).astype(bf16)
            full = lax.dot_general(rows, place, (((1,), (1,)), ((), ())), preferred_element_type=f32)
            out[i * padded : (i + 1) * padded] = full.astype(bf16)
        trace = jnp.sum(jnp.sum(jnp.where(diagonal, v, 0.0), 0, keepdims=True), 1, keepdims=True)
        traces_ref[i : i + 1] = jnp.broadcast_to(trace, (1, LZ))


def first_kernel(rhs_ref, hx_ref, hy_ref, k_ref, m_ref, wh_ref, wl_ref,
                 p_ref, snx, sfx, sny, sfy, v, ux, uy, upx, lowx, upy, lowy):
    v[:ROWS] = rhs_ref[...]
    v[ROWS:] = jnp.zeros((PADDED - ROWS, LZ), f32)
    ux[: A * LY] = hx_ref[...]
    ux[A * LY :] = jnp.zeros(((AP - A) * LY, LZ), f32)
    uy[: A * LX] = hy_ref[...]
    uy[A * LX :] = jnp.zeros(((AP - A) * LX, LZ), f32)
    apply_operator(v, ux, uy, k_ref, m_ref, 1.0, wh_ref, wl_ref, p_ref, upx, lowx, upy, lowy)
    route(is_even("gx"), upx, lowx, snx, sfx)
    route(is_even("gy"), upy, lowy, sny, sfy)


def next_vector(p_ref, prev_ref, hx_ref, hy_ref, snx, sfx, sny, sfy, rnx, rfx, rny, rfy, scale, v, ux, uy):
    even_x = is_even("gx")
    even_y = is_even("gy")
    v[:ROWS] = p_ref[...] * scale - prev_ref[...]
    v[ROWS:] = jnp.zeros((PADDED - ROWS, LZ), f32)
    below_x = jnp.where(even_x, rfx[...], rnx[...]) * scale
    for a in range(A):
        rows = slice(a * CELLS, a * CELLS + LY)
        v[rows, :] = v[rows, :] + below_x[a * LY : (a + 1) * LY]
    below_y = jnp.where(even_y, rfy[...], rny[...]) * scale
    first = pl.ds(FACE, A * LX, stride=LY)
    v[first, :] = v[first, :] + below_y
    above_x = jnp.where(even_x, snx[...] + rnx[...], sfx[...] + rfx[...])
    ux[: A * LY] = above_x * scale - hx_ref[...]
    ux[A * LY :] = jnp.zeros(((AP - A) * LY, LZ), f32)
    above_y = jnp.where(even_y, sny[...] + rny[...], sfy[...] + rfy[...])
    uy[: A * LX] = above_y * scale - hy_ref[...]
    uy[A * LX :] = jnp.zeros(((AP - A) * LX, LZ), f32)


def node_sum(value):
    return jnp.sum(value.reshape(-1, LY, LZ), 0)


def second_kernel(p_ref, rhs_ref, hx_ref, hy_ref, snx, sfx, sny, sfy, rnx, rfx, rny, rfy,
                  st_ref, traces_ref, k_ref, m_ref, wh_ref, wl_ref,
                  v1_ref, ux1_ref, uy1_ref, p1_ref, tnx, tfx, tny, tfy, sums_ref, inv_ref,
                  v, ux, uy, upx, lowx, upy, lowy, *, total):
    inv = 1.0 / mean_eigenvalue(st_ref, traces_ref, total)
    inv_ref[...] = jnp.broadcast_to(inv, (8, LZ))
    next_vector(p_ref, rhs_ref, hx_ref, hy_ref, snx, sfx, sny, sfy, rnx, rfx, rny, rfy, inv, v, ux, uy)
    v0 = rhs_ref[...]
    v1 = v[:ROWS]
    v1_ref[...] = v1
    ux1_ref[...] = ux[: A * LY]
    uy1_ref[...] = uy[: A * LX]
    sums_ref[0:8] = node_sum(v0)
    sums_ref[8:16] = node_sum(v1)
    sums_ref[16:24] = node_sum(v0 * v0)
    sums_ref[24:32] = node_sum(v0 * v1)
    sums_ref[32:40] = node_sum(v1 * v1)
    apply_operator(v, ux, uy, k_ref, m_ref, inv, wh_ref, wl_ref, p1_ref, upx, lowx, upy, lowy)
    route(is_even("gx"), upx, lowx, tnx, tfx)
    route(is_even("gy"), upy, lowy, tny, tfy)


def third_kernel(p_ref, prev_ref, hx_ref, hy_ref, snx, sfx, sny, sfy, rnx, rfx, rny, rfy,
                 inv_ref, sums1_ref, k_ref, m_ref, wh_ref, wl_ref,
                 v2_ref, p2_ref, upx, upy, loads_ref, mom_ref, v, ux, uy):
    one = jnp.float32(1.0)
    next_vector(p_ref, prev_ref, hx_ref, hy_ref, snx, sfx, sny, sfy, rnx, rfx, rny, rfy, one, v, ux, uy)
    v1 = prev_ref[...]
    v2 = v[:ROWS]
    v2_ref[...] = v2
    loads_ref[0:16] = sums1_ref[0:16]
    loads_ref[16:24] = node_sum(v2)
    m3 = node_sum(v1 * v2)
    m4 = node_sum(v2 * v2)
    apply_operator(v, ux, uy, k_ref, m_ref, inv_ref[0:1], wh_ref, wl_ref, p2_ref, upx, None, upy, None)
    p2 = p2_ref[...]
    loads_ref[24:32] = node_sum(p2)
    energy = node_sum(v[:ROWS] * p2) + node_sum(ux[: A * LY] * upx[...])
    tail = jnp.sum(uy[: A * LX] * upy[...], 0, keepdims=True)

    def row(tile):
        return jnp.sum(tile, 0, keepdims=True)

    tile = [row(sums1_ref[16 + 8 * k : 24 + 8 * k]) for k in range(3)]
    tile += [row(m3), row(m4), row(energy) + tail, jnp.zeros((2, LZ), f32)]
    mom_ref[...] = jnp.broadcast_to(jnp.concatenate(tile, 0)[None], mom_ref.shape)


def middle_kernel(mom_ref, loads_ref, rx_ref, ry_ref, out_ref, *, table):
    nx = len(table)
    me = lax.axis_index("gx")
    total = jnp.sum(mom_ref[...], 0)
    edge = jnp.broadcast_to(jnp.sum(ry_ref[...], 0, keepdims=True), (LY, LZ))
    at_first = lax.broadcasted_iota(jnp.int32, (LY, LZ), 0) == 0
    image = loads_ref[24:32] + node_sum(rx_ref[...]) + jnp.where(at_first, edge, 0.0)
    own = [loads_ref[0:8], loads_ref[8:16], loads_ref[16:24], image]
    for offset, weight in enumerate(table):
        to = lax.rem(me + offset, nx)
        for k in range(4):
            out_ref[to, k] = own[k] * weight
        out_ref[to, 4] = total


def conjugate_gradient(m):
    def dot(a, b):
        s = None
        for i, ai in enumerate(a):
            for j, bj in enumerate(b):
                t = ai * bj * m[i + j]
                s = t if s is None else s + t
        return s

    def add(a, b, factor):
        longer = []
        for i in range(max(len(a), len(b))):
            if i >= len(b):
                longer.append(a[i])
            elif i >= len(a):
                longer.append(factor * b[i])
            else:
                longer.append(a[i] + factor * b[i])
        return longer

    def image(a):
        return [a[0]] + [a[i] + a[i - 1] for i in range(1, len(a))] + [a[-1]]

    one = jnp.ones((1, 1), f32)
    iterate, residual, direction = [], [one], [one]
    norm = m[0]
    for step in range(ITERS):
        img = image(direction)
        alpha = norm / dot(direction, img)
        iterate = add(iterate, direction, alpha)
        residual = add(residual, img, -alpha)
        if step < ITERS - 1:
            norm_next = dot(residual, residual)
            direction = add(residual, direction, norm_next / norm)
            norm = norm_next
    return iterate, residual


def last_kernel(prolong_ref, got_ref, inv_ref, rhs_ref, v1_ref, v2_ref, p2_ref, rx_ref, ry_ref,
                sol_ref, res_ref, coarse_ref):
    got = jnp.sum(got_ref[...], 0)
    sums = jnp.sum(got[4], axis=1, keepdims=True)
    m = [sums[k : k + 1] for k in range(6)]
    m[5] = m[5] - m[4]
    x, d = conjugate_gradient(m)
    inv = inv_ref[0:1, 0:1]
    x = [t * inv for t in x]
    coarse = d[0] * got[0] + d[1] * got[1] + (d[2] - d[3]) * got[2] + d[3] * got[3]
    coarse_ref[...] = coarse
    d2 = d[2] - d[3]
    for f in range(F):
        for a in range(A):
            at = (f * A + a) * CELLS
            spread = coarse * prolong_ref[f * A + a]
            for c in range(LX):
                rows = slice(at + c * LY, at + (c + 1) * LY)
                v0, v1, v2 = rhs_ref[rows, :], v1_ref[rows, :], v2_ref[rows, :]
                img = p2_ref[rows, :]
                if f == 0 and c == 0:
                    img = img + rx_ref[a * LY : (a + 1) * LY, :]
                sol_ref[rows, :] = x[0] * v0 + x[1] * v1 + x[2] * v2 + spread
                res_ref[rows, :] = d[0] * v0 + d[1] * v1 + d2 * v2 + d[3] * img
    first = pl.ds(FACE, A * LX, stride=LY)
    res_ref[first, :] = res_ref[first, :] + d[3] * ry_ref[...]


def jacobi_weights(n):
    coarse = np.zeros(n)
    load = np.zeros(n)
    load[0] = 1.0
    for _ in range(SWEEPS):
        coarse = (load + np.roll(coarse, 1) + np.roll(coarse, -1)) / 2.2
    return coarse / 75.0


def struct(*shape):
    return jax.ShapeDtypeStruct(shape, f32)


PARAMS = pltpu.CompilerParams(vmem_limit_bytes=16 * 1024 * 1024)


def shards(rhs, kappa, mass, stiffness, mass_matrix, prolong):
    nx, ny = lax.axis_size("gx"), lax.axis_size("gy")
    vx, vy = A * LY, A * LX
    rhs2 = rhs.reshape(ROWS, LZ)
    k2 = kappa.reshape(CELLS, LZ)
    m2 = mass.reshape(CELLS, LZ)
    sends = [struct(vx, LZ), struct(vx, LZ), struct(vy, LZ), struct(vy, LZ)]
    field = [pltpu.VMEM((PADDED, LZ), f32), pltpu.VMEM((AP * LY, LZ), f32), pltpu.VMEM((AP * LX, LZ), f32)]
    edges = [pltpu.VMEM((vx, LZ), f32)] * 2 + [pltpu.VMEM((vy, LZ), f32)] * 2

    def call(kernel, name, ins, outs, scratch=(), **static):
        specs = [i[1] if isinstance(i, tuple) else VM for i in ins]
        ins = [i[0] if isinstance(i, tuple) else i for i in ins]

        def bound(*refs):
            kernel(*refs, **static)

        return pl.pallas_call(
            bound,
            out_shape=outs,
            in_specs=specs,
            out_specs=[VM] * len(outs),
            scratch_shapes=list(scratch),
            compiler_params=PARAMS,
            name=name,
        )(*ins)

    def swap(s):
        far_x = far_swap(s[1], "gx")
        far_y = far_swap(s[3], "gy")
        near_y = near_swap(s[2], "gy")
        near_x = near_swap(s[0], "gx")
        return [near_x, far_x, near_y, far_y]

    fx, fy, stats = call(
        edge_kernel, "edges", [(rhs, ANY), k2, m2], [struct(A, LY, LZ), struct(A, LX, LZ), struct(nx * ny, 2, LZ)],
        [pltpu.SemaphoreType.DMA, pltpu.SemaphoreType.DMA], devices=nx * ny,
    )
    hx = shifted(fx.reshape(vx, LZ), "gx", -1)
    hy = shifted(fy.reshape(vy, LZ), "gy", -1)
    stats = lax.all_to_all(stats, ("gx", "gy"), 0, 0, tiled=True).reshape(nx * ny * 2, LZ)
    half = jax.ShapeDtypeStruct((12 * AP, 6 * AP), bf16)
    wh, wl, traces = call(weight_kernel, "weights", [stiffness, mass_matrix], [half, half, struct(8, LZ)])

    p0, *s = call(
        first_kernel, "first", [rhs2, hx, hy, k2, m2, wh, wl], [struct(ROWS, LZ)] + sends, field + edges,
    )
    r = swap(s)
    v1, ux1, uy1, p1, *rest = call(
        second_kernel, "second", [p0, rhs2, hx, hy, *s, *r, stats, traces, k2, m2, wh, wl],
        [struct(ROWS, LZ), struct(vx, LZ), struct(vy, LZ), struct(ROWS, LZ)] + sends + [struct(40, LZ), struct(8, LZ)],
        field + edges, total=float(nx * ny * CELLS * LZ),
    )
    s, (sums, inv) = rest[:4], rest[4:]
    r = swap(s)
    v2, p2, upx, upy, loads, mom = call(
        third_kernel, "third", [p1, v1, ux1, uy1, *s, *r, inv, sums, k2, m2, wh, wl],
        [struct(ROWS, LZ), struct(ROWS, LZ), struct(vx, LZ), struct(vy, LZ), struct(32, LZ), struct(ny, 8, LZ)], field,
    )
    rx = shifted(upx, "gx", 1)
    ry = shifted(upy, "gy", 1)
    mom = lax.all_to_all(mom, "gy", 0, 0, tiled=True)
    pieces, = call(
        middle_kernel, "middle", [mom, loads, rx, ry], [struct(nx, 5, 8, LZ)], table=[float(t) for t in jacobi_weights(nx)],
    )
    got = lax.all_to_all(pieces, "gx", 0, 0, tiled=True)
    sol, res, coarse = call(
        last_kernel, "last", [(prolong.reshape(-1), SM), got, inv, rhs2, v1, v2, p2, rx, ry],
        [struct(ROWS, LZ), struct(ROWS, LZ), struct(LY, LZ)],
    )
    return sol.reshape(rhs.shape), res.reshape(rhs.shape), coarse[None]


def solution(mesh):
    placed = (
        P(None, None, "gx", "gy", None),
        P("gx", "gy", None),
        P("gx", "gy", None),
        P(),
        P(),
        P(),
    )
    return jax.shard_map(
        shards,
        mesh=mesh,
        in_specs=placed,
        out_specs=(
            P(None, None, "gx", "gy", None),
            P(None, None, "gx", "gy", None),
            P("gx", "gy", None),
        ),
        check_vma=False,
    )
```

```python
import jax
import jax.numpy as jnp
import numpy as np
from jax import lax
from jax.experimental import pallas as pl
from jax.experimental.pallas import tpu as pltpu
from jax.sharding import PartitionSpec as P

ITERS = 3
SWEEPS = 8
F, A, AP = 3, 25, 32
LX, LY, LZ = 4, 8, 128
CELLS = LX * LY
FACE = A * CELLS
ROWS = F * FACE
PADDED = ROWS + (AP - A) * CELLS
f32, bf16 = jnp.float32, jnp.bfloat16
VM = pl.BlockSpec(memory_space=pltpu.VMEM)
SM = pl.BlockSpec(memory_space=pltpu.SMEM)
ANY = pl.BlockSpec(memory_space=pl.ANY)


def shifted(value, axis, by):
    n = lax.axis_size(axis)
    return lax.ppermute(value, axis, [(i, (i + by) % n) for i in range(n)])


def near_swap(value, axis):
    n = lax.axis_size(axis)
    return lax.ppermute(value, axis, [(i, i ^ 1) for i in range(n)])


def far_swap(value, axis):
    n = lax.axis_size(axis)
    pairs = [(i, (i + 1) % n) if i % 2 else (i, (i - 1) % n) for i in range(n)]
    return lax.ppermute(value, axis, pairs)


def halves(v):
    hi = v.astype(bf16)
    lo = (v - hi.astype(f32)).astype(bf16)
    return hi, lo


def apply_operator(v_ref, ux_ref, uy_ref, k_ref, m_ref, wh_ref, wl_ref, out_ref, up_x, low_x, up_y, low_y):
    wh = wh_ref[...]
    wl = wl_ref[...]

    def face(f, x, y):
        if f == 0 and x == LX:
            return ux_ref[pl.ds(y, AP, stride=LY), :]
        if f == 1 and y == LY:
            return uy_ref[pl.ds(x, AP, stride=LX), :]
        return v_ref[pl.ds(f * FACE + x * LY + y, AP, stride=CELLS), :]

    def put(f, x, y, value):
        out_ref[pl.ds(f * FACE + x * LY + y, A, stride=CELLS), :] = value[:A]

    t0 = [halves(face(0, 0, y)) for y in range(LY)]
    carry = None
    for x in range(LX):
        t0_next = [halves(face(0, x + 1, y)) for y in range(LY)]
        t1 = [halves(face(1, x, y)) for y in range(LY + 1)]
        his, los = [], []
        for y in range(LY):
            z = face(2, x, y)
            t2 = halves(z)
            t2u = halves(pltpu.roll(z, LZ - 1, 1))
            six = (t0[y], t0_next[y], t1[y], t1[y + 1], t2, t2u)
            his.append(jnp.concatenate([b[0] for b in six], 0))
            los.append(jnp.concatenate([b[1] for b in six], 0))
        t0 = t0_next
        hi = jnp.concatenate(his, 1)
        lo = jnp.concatenate(los, 1)
        prod = jnp.dot(wh, hi, preferred_element_type=f32)
        prod += jnp.dot(wh, lo, preferred_element_type=f32)
        prod += jnp.dot(wl, hi, preferred_element_type=f32)
        parts = []
        for y in range(LY):
            k = k_ref[x * LY + y : x * LY + y + 1, :]
            m = m_ref[x * LY + y : x * LY + y + 1, :]
            cols = slice(y * LZ, (y + 1) * LZ)
            w = prod[: 6 * AP, cols] * k + prod[6 * AP :, cols] * m
            parts.append([w[b * AP : (b + 1) * AP] for b in range(6)])
        for y in range(LY):
            wlx, wux, wly, wuy, wlz, wuz = parts[y]
            put(0, x, y, wlx if x == 0 else wlx + carry[y])
            put(1, x, y, wly if y == 0 else wly + parts[y - 1][3])
            put(2, x, y, wlz + pltpu.roll(wuz, 1, 1))
            if x == 0 and low_x is not None:
                low_x[pl.ds(y, A, stride=LY), :] = wlx[:A]
            if x == LX - 1:
                up_x[pl.ds(y, A, stride=LY), :] = wux[:A]
        if low_y is not None:
            low_y[pl.ds(x, A, stride=LX), :] = parts[0][2][:A]
        up_y[pl.ds(x, A, stride=LX), :] = parts[LY - 1][3][:A]
        carry = [parts[y][1] for y in range(LY)]


def is_even(axis):
    return lax.rem(lax.axis_index(axis), 2) == 0


def route(even, up, low, near, far):
    near[...] = jnp.where(even, up[...], low[...])
    far[...] = jnp.where(even, low[...], up[...])


def edge_kernel(rhs_ref, fx_ref, fy_ref, sem_x, sem_y):
    face_x = pltpu.make_async_copy(rhs_ref.at[0, :, 0], fx_ref, sem_x)
    face_y = pltpu.make_async_copy(rhs_ref.at[1, :, :, 0], fy_ref, sem_y)
    face_x.start()
    face_y.start()
    face_x.wait()
    face_y.wait()


def weight_kernel(s_ref, m_ref, wh_ref, wl_ref, inv_ref):
    n, padded = 6 * A, 6 * AP
    r = lax.broadcasted_iota(jnp.int32, (padded, n), 0)
    c = lax.broadcasted_iota(jnp.int32, (padded, n), 1)
    node = lax.rem(r, AP)
    place = jnp.where((node < A) & (lax.div(r, AP) * A + node == c), 1.0, 0.0).astype(bf16)
    diagonal = lax.broadcasted_iota(jnp.int32, (n, n), 0) == lax.broadcasted_iota(jnp.int32, (n, n), 1)

    def largest(v):
        return jnp.max(jnp.max(jnp.where(diagonal, v, 0.0), 0, keepdims=True), 1, keepdims=True)

    inv = 1.0 / (10.0 * largest(s_ref[...]) + 2.0 * largest(m_ref[...]))
    inv_ref[...] = jnp.broadcast_to(inv, (8, LZ))
    for i, ref in enumerate((s_ref, m_ref)):
        for part, out in zip(halves(ref[...] * inv), (wh_ref, wl_ref)):
            rows = jnp.dot(place, part, preferred_element_type=f32).astype(bf16)
            full = lax.dot_general(rows, place, (((1,), (1,)), ((), ())), preferred_element_type=f32)
            out[i * padded : (i + 1) * padded] = full.astype(bf16)


def pad(ref, rows):
    ref[rows:] = jnp.zeros((ref.shape[0] - rows, LZ), f32)


def first_kernel(rhs_ref, hx_ref, hy_ref, k_ref, m_ref, wh_ref, wl_ref,
                 p_ref, snx, sfx, sny, sfy, v, ux, uy, upx, lowx, upy, lowy):
    v[:ROWS] = rhs_ref[...]
    pad(v, ROWS)
    ux[: A * LY] = hx_ref[...]
    pad(ux, A * LY)
    uy[: A * LX] = hy_ref[...]
    pad(uy, A * LX)
    apply_operator(v, ux, uy, k_ref, m_ref, wh_ref, wl_ref, p_ref, upx, lowx, upy, lowy)
    route(is_even("gx"), upx, lowx, snx, sfx)
    route(is_even("gy"), upy, lowy, sny, sfy)


def assemble(p_ref, snx, sfx, sny, sfy, rnx, rfx, rny, rfy, v, ux, uy):
    even_x = is_even("gx")
    even_y = is_even("gy")
    v[:ROWS] = p_ref[...]
    pad(v, ROWS)
    below_x = jnp.where(even_x, rfx[...], rnx[...])
    for a in range(A):
        rows = slice(a * CELLS, a * CELLS + LY)
        v[rows, :] = v[rows, :] + below_x[a * LY : (a + 1) * LY]
    below_y = jnp.where(even_y, rfy[...], rny[...])
    first = pl.ds(FACE, A * LX, stride=LY)
    v[first, :] = v[first, :] + below_y
    ux[: A * LY] = jnp.where(even_x, snx[...] + rnx[...], sfx[...] + rfx[...])
    pad(ux, A * LY)
    uy[: A * LX] = jnp.where(even_y, sny[...] + rny[...], sfy[...] + rfy[...])
    pad(uy, A * LX)


def node_sum(value):
    return jnp.sum(value.reshape(-1, LY, LZ), 0)


def row(tile):
    return jnp.sum(tile, 0, keepdims=True)


def second_kernel(p_ref, rhs_ref, snx, sfx, sny, sfy, rnx, rfx, rny, rfy, k_ref, m_ref, wh_ref, wl_ref,
                  v1_ref, p1_ref, tnx, tfx, tny, tfy, sums_ref, ux, uy, upx, lowx, upy, lowy):
    assemble(p_ref, snx, sfx, sny, sfy, rnx, rfx, rny, rfy, v1_ref, ux, uy)
    v0 = rhs_ref[...]
    v1 = v1_ref[:ROWS]
    sums_ref[0:8] = node_sum(v0)
    sums_ref[8:16] = node_sum(v1)
    sums_ref[16:24] = node_sum(v0 * v0)
    sums_ref[24:32] = node_sum(v0 * v1)
    sums_ref[32:40] = node_sum(v1 * v1)
    apply_operator(v1_ref, ux, uy, k_ref, m_ref, wh_ref, wl_ref, p1_ref, upx, lowx, upy, lowy)
    route(is_even("gx"), upx, lowx, tnx, tfx)
    route(is_even("gy"), upy, lowy, tny, tfy)


def third_kernel(p_ref, v1_ref, snx, sfx, sny, sfy, rnx, rfx, rny, rfy, sums_ref, k_ref, m_ref, wh_ref, wl_ref,
                 v2_ref, p2_ref, upx, upy, loads_ref, mom_ref, ux, uy):
    assemble(p_ref, snx, sfx, sny, sfy, rnx, rfx, rny, rfy, v2_ref, ux, uy)
    v1 = v1_ref[:ROWS]
    v2 = v2_ref[:ROWS]
    loads_ref[0:16] = sums_ref[0:16]
    loads_ref[16:24] = node_sum(v2)
    m3 = node_sum(v1 * v2)
    m4 = node_sum(v2 * v2)
    apply_operator(v2_ref, ux, uy, k_ref, m_ref, wh_ref, wl_ref, p2_ref, upx, None, upy, None)
    p2 = p2_ref[...]
    above = upx[...]
    loads_ref[24:32] = node_sum(p2)
    loads_ref[32:40] = node_sum(above)
    energy = node_sum(v2_ref[:ROWS] * p2) + node_sum(ux[: A * LY] * above)
    tail = row(uy[: A * LX] * upy[...])
    tile = [row(sums_ref[16 + 8 * k : 24 + 8 * k]) for k in range(3)]
    tile = jnp.concatenate(tile + [row(m3), row(m4), row(energy) + tail, jnp.zeros((2, LZ), f32)], 0)
    for lanes in (64, 32, 16):
        tile = tile + pltpu.roll(tile, lanes, 1)
    lane = lax.broadcasted_iota(jnp.int32, (8, LZ), 1)
    moment = lax.broadcasted_iota(jnp.int32, (8, LZ), 0)
    packed = row(jnp.where(lax.div(lane, 16) == moment, tile, 0.0))
    pair = jnp.concatenate([packed, row(upy[...])] * 4, 0)
    for at in range(0, mom_ref.shape[0], 8):
        mom_ref[at : at + 8] = pair


def weigh_kernel(own, near, far, both, *outs, table):
    nx = len(table)
    q = lax.rem(lax.axis_index("gx"), 4)
    low, high = lax.rem(q, 2) == 0, q < 2
    one, two = jnp.where(low, 1, -1), jnp.where(high, 2, -2)

    def pick(at, shift, span):
        value = jnp.float32(table[(at - span[0]) % nx])
        for s in span[1:]:
            value = jnp.where(shift == s, table[(at - s) % nx], value)
        return value

    for z, out in enumerate(outs):
        total = [0.0] * 4
        for ref, shift, span in ((own, 0, (0,)), (near, one, (1, -1)), (far, two, (2, -2)), (both, one + two, (3, 1, -1, -3))):
            w = pick(4 * z, shift, span)
            for k in range(4):
                total[k] = total[k] + ref[k * 8 : k * 8 + 8] * w
            total[3] = total[3] + ref[32:40] * pick(4 * z - 1, shift, span)
        for k in range(4):
            out[k * 8 : k * 8 + 8] = total[k]


def two_sum(a, b):
    s = a + b
    t = s - a
    return s, (a - (s - t)) + (b - t)


def pair_add(a, b):
    s, e = two_sum(a[0], b[0])
    e = e + (a[1] + b[1])
    h = s + e
    return h, e - (h - s)


def split(a):
    t = a * 4097.0
    h = t - (t - a)
    return h, a - h


def pair_times(a, c):
    p = a[0] * c
    ah, al = split(a[0])
    ch, cl = split(c)
    return p, ((ah * ch - p) + ah * cl + al * ch) + al * cl + a[1] * c


def moments(got):
    pairs = [(got[at : at + 8], jnp.zeros((8, LZ), f32)) for at in range(0, got.shape[0], 8)]
    while len(pairs) > 1:
        pairs = [pair_add(a, b) for a, b in zip(pairs[::2], pairs[1::2])]
    t = pairs[0]
    for rows in (4, 2):
        t = pair_add(t, tuple(pltpu.roll(p, rows, 0) for p in t))
    for lanes in (8, 4, 2, 1):
        t = pair_add(t, tuple(pltpu.roll(p, LZ - lanes, 1) for p in t))
    c = t[0][0:1, 16:17] / t[0][0:1, 0:1]
    wide = jnp.broadcast_to(c, (8, LZ))
    m = [t[0][0:1, 0:1]]
    for _ in range(5):
        up = tuple(pltpu.roll(p, LZ - 16, 1) for p in t)
        t = pair_add(up, pair_times(t, -wide))
        m.append(t[0][0:1, 0:1])
    return c, m


def conjugate_gradient(c, m):
    def dot(a, b):
        s = None
        for i, ai in enumerate(a):
            for j, bj in enumerate(b):
                t = ai * bj * m[i + j]
                s = t if s is None else s + t
        return s

    def add(a, b, factor):
        longer = []
        for i in range(max(len(a), len(b))):
            if i >= len(b):
                longer.append(a[i])
            elif i >= len(a):
                longer.append(factor * b[i])
            else:
                longer.append(a[i] + factor * b[i])
        return longer

    def times(a, shift):
        return [a[0] * shift] + [a[i] * shift + a[i - 1] for i in range(1, len(a))] + [a[-1]]

    def plain(a):
        out = [a[-1]]
        for coefficient in a[-2::-1]:
            out = times(out, -c)
            out[0] = out[0] + coefficient
        return out

    one = jnp.ones((1, 1), f32)
    iterate, residual, direction = [], [one], [one]
    norm = m[0]
    for step in range(ITERS):
        img = times(direction, c)
        alpha = norm / dot(direction, img)
        iterate = add(iterate, direction, alpha)
        residual = add(residual, img, -alpha)
        if step < ITERS - 1:
            norm_next = dot(residual, residual)
            direction = add(residual, direction, norm_next / norm)
            norm = norm_next
    return plain(iterate), plain(residual)


def last_kernel(prolong_ref, got_ref, c0, c1, c2, c3, inv_ref, rhs_ref, v1_ref, v2_ref, p2_ref, rx_ref, ry_ref,
                sol_ref, res_ref, coarse_ref, *, table, ny):
    nx = len(table)
    x, d = conjugate_gradient(*moments(got_ref[...]))
    inv = inv_ref[0:1, 0:1]
    x = [t * inv for t in x]
    me = lax.axis_index("gx")
    below = lax.rem(lax.axis_index("gy") + ny - 1, ny)
    edge = jnp.zeros((1, LZ), f32)
    for offset, weight in enumerate(table):
        slab = lax.rem(me + nx - offset, nx)
        edge = edge + got_ref[pl.ds(2 * (slab * ny + below) + 1, 1), :] * weight
    circ = [c0[k * 8 : k * 8 + 8] + c1[k * 8 : k * 8 + 8] + c2[k * 8 : k * 8 + 8] + c3[k * 8 : k * 8 + 8] for k in range(4)]
    at_first = lax.broadcasted_iota(jnp.int32, (LY, LZ), 0) == 0
    circ[3] = circ[3] + jnp.where(at_first, jnp.broadcast_to(edge, (LY, LZ)), 0.0)
    coarse = d[0] * circ[0] + d[1] * circ[1] + d[2] * circ[2] + d[3] * circ[3]
    coarse_ref[...] = coarse
    x = [jnp.broadcast_to(t, (LY, LZ)) for t in x]
    d = [jnp.broadcast_to(t, (LY, LZ)) for t in d]
    for f in range(F):
        for a in range(A):
            at = (f * A + a) * CELLS
            spread = coarse * prolong_ref[f, a]
            for cell in range(LX):
                rows = slice(at + cell * LY, at + (cell + 1) * LY)
                v0, v1, v2 = rhs_ref[rows, :], v1_ref[rows, :], v2_ref[rows, :]
                img = p2_ref[rows, :]
                if f == 0 and cell == 0:
                    img = img + rx_ref[a * LY : (a + 1) * LY, :]
                sol_ref[rows, :] = x[0] * v0 + x[1] * v1 + x[2] * v2 + spread
                res_ref[rows, :] = d[0] * v0 + d[1] * v1 + d[2] * v2 + d[3] * img
    first = pl.ds(FACE, A * LX, stride=LY)
    res_ref[first, :] = res_ref[first, :] + d[3][0:1] * ry_ref[...]


def jacobi_weights(n):
    coarse = np.zeros(n)
    load = np.zeros(n)
    load[0] = 1.0
    for _ in range(SWEEPS):
        coarse = (load + np.roll(coarse, 1) + np.roll(coarse, -1)) / 2.2
    return coarse / 75.0


def struct(*shape):
    return jax.ShapeDtypeStruct(shape, f32)


PARAMS = pltpu.CompilerParams(vmem_limit_bytes=16 * 1024 * 1024)


def shards(rhs, kappa, mass, stiffness, mass_matrix, prolong):
    nx, ny = lax.axis_size("gx"), lax.axis_size("gy")
    vx, vy = A * LY, A * LX
    rhs2 = rhs.reshape(ROWS, LZ)
    k2 = kappa.reshape(CELLS, LZ)
    m2 = mass.reshape(CELLS, LZ)
    sends = [struct(vx, LZ), struct(vx, LZ), struct(vy, LZ), struct(vy, LZ)]
    upper = [pltpu.VMEM((AP * LY, LZ), f32), pltpu.VMEM((AP * LX, LZ), f32)]
    field = [pltpu.VMEM((PADDED, LZ), f32)] + upper
    edges = [pltpu.VMEM((vx, LZ), f32)] * 2 + [pltpu.VMEM((vy, LZ), f32)] * 2

    def call(kernel, name, ins, outs, scratch=(), **static):
        specs = [i[1] if isinstance(i, tuple) else VM for i in ins]
        ins = [i[0] if isinstance(i, tuple) else i for i in ins]

        def bound(*refs):
            kernel(*refs, **static)

        return pl.pallas_call(
            bound,
            out_shape=outs,
            in_specs=specs,
            out_specs=[VM] * len(outs),
            scratch_shapes=list(scratch),
            compiler_params=PARAMS,
            name=name,
        )(*ins)

    def swap(s):
        far_x = far_swap(s[1], "gx")
        far_y = far_swap(s[3], "gy")
        near_y = near_swap(s[2], "gy")
        near_x = near_swap(s[0], "gx")
        return [near_x, far_x, near_y, far_y]

    hbm = pltpu.with_memory_space_constraint(rhs, pltpu.HBM)
    fx, fy = call(
        edge_kernel, "edges", [(hbm, ANY)], [struct(A, LY, LZ), struct(A, LX, LZ)],
        [pltpu.SemaphoreType.DMA, pltpu.SemaphoreType.DMA],
    )
    hx = shifted(fx.reshape(vx, LZ), "gx", -1)
    hy = shifted(fy.reshape(vy, LZ), "gy", -1)
    half = jax.ShapeDtypeStruct((12 * AP, 6 * AP), bf16)
    wh, wl, inv = call(weight_kernel, "weights", [stiffness, mass_matrix], [half, half, struct(8, LZ)])

    p0, *s = call(
        first_kernel, "first", [rhs2, hx, hy, k2, m2, wh, wl], [struct(ROWS, LZ)] + sends, field + edges,
    )
    r = swap(s)
    v1, p1, *s, sums = call(
        second_kernel, "second", [p0, rhs2, *s, *r, k2, m2, wh, wl],
        [struct(PADDED, LZ), struct(ROWS, LZ)] + sends + [struct(40, LZ)], upper + edges,
    )
    r = swap(s)
    v2, p2, upx, upy, loads, mom = call(
        third_kernel, "third", [p1, v1, *s, *r, sums, k2, m2, wh, wl],
        [struct(PADDED, LZ), struct(ROWS, LZ), struct(vx, LZ), struct(vy, LZ), struct(40, LZ), struct(nx * ny * 2, LZ)],
        upper,
    )
    got = lax.all_to_all(mom.reshape(nx * ny, 2, LZ), ("gx", "gy"), 0, 0, tiled=True).reshape(nx * ny * 2, LZ)
    group = [lax.ppermute(loads, "gx", [(i, i ^ b) for i in range(nx)]) for b in (1, 2, 3)]
    rx = shifted(upx, "gx", 1)
    ry = shifted(upy, "gy", 1)
    table = [float(t) for t in jacobi_weights(nx)]
    pieces = call(weigh_kernel, "weigh", [loads, *group], [struct(32, LZ)] * (nx // 4), table=table)
    coarse = [pieces[0]] + [shifted(p, "gx", 4 * z) for z, p in enumerate(pieces) if z]
    sol, res, coarse = call(
        last_kernel, "last", [(prolong, SM), got, *coarse, inv, rhs2, v1, v2, p2, rx, ry],
        [struct(ROWS, LZ), struct(ROWS, LZ), struct(LY, LZ)], table=table, ny=ny,
    )
    return sol.reshape(rhs.shape), res.reshape(rhs.shape), coarse[None]


def solution(mesh):
    placed = (
        P(None, None, "gx", "gy", None),
        P("gx", "gy", None),
        P("gx", "gy", None),
        P(),
        P(),
        P(),
    )
    return jax.shard_map(
        shards,
        mesh=mesh,
        in_specs=placed,
        out_specs=(
            P(None, None, "gx", "gy", None),
            P(None, None, "gx", "gy", None),
            P("gx", "gy", None),
        ),
        check_vma=False,
    )
```

```python
import jax
import jax.numpy as jnp
import numpy as np
from jax import lax
from jax.experimental import pallas as pl
from jax.experimental.pallas import tpu as pltpu
from jax.sharding import PartitionSpec as P

ITERS = 3
SWEEPS = 8
F, A, AP = 3, 25, 32
LX, LY, LZ = 4, 8, 128
CELLS = LX * LY
FACE = A * CELLS
ROWS = F * FACE
PADDED = ROWS + (AP - A) * CELLS
f32, bf16 = jnp.float32, jnp.bfloat16
VM = pl.BlockSpec(memory_space=pltpu.VMEM)
SM = pl.BlockSpec(memory_space=pltpu.SMEM)
ANY = pl.BlockSpec(memory_space=pl.ANY)


def shifted(value, axis, by):
    n = lax.axis_size(axis)
    return lax.ppermute(value, axis, [(i, (i + by) % n) for i in range(n)])


def near_swap(value, axis):
    n = lax.axis_size(axis)
    return lax.ppermute(value, axis, [(i, i ^ 1) for i in range(n)])


def far_swap(value, axis):
    n = lax.axis_size(axis)
    pairs = [(i, (i + 1) % n) if i % 2 else (i, (i - 1) % n) for i in range(n)]
    return lax.ppermute(value, axis, pairs)


def halves(v):
    hi = v.astype(bf16)
    lo = (v - hi.astype(f32)).astype(bf16)
    return hi, lo


def apply_operator(v_ref, ux_ref, uy_ref, k_ref, m_ref, wh_ref, wl_ref, out_ref, up_x, low_x, up_y, low_y):
    wh = wh_ref[...]
    wl = wl_ref[...]

    def face(f, x, y):
        if f == 0 and x == LX:
            return ux_ref[pl.ds(y, AP, stride=LY), :]
        if f == 1 and y == LY:
            return uy_ref[pl.ds(x, AP, stride=LX), :]
        return v_ref[pl.ds(f * FACE + x * LY + y, AP, stride=CELLS), :]

    def put(f, x, y, value):
        out_ref[pl.ds(f * FACE + x * LY + y, A, stride=CELLS), :] = value[:A]

    t0 = [halves(face(0, 0, y)) for y in range(LY)]
    carry = None
    for x in range(LX):
        t0_next = [halves(face(0, x + 1, y)) for y in range(LY)]
        t1 = [halves(face(1, x, y)) for y in range(LY + 1)]
        his, los = [], []
        for y in range(LY):
            z = face(2, x, y)
            t2 = halves(z)
            t2u = halves(pltpu.roll(z, LZ - 1, 1))
            six = (t0[y], t0_next[y], t1[y], t1[y + 1], t2, t2u)
            his.append(jnp.concatenate([b[0] for b in six], 0))
            los.append(jnp.concatenate([b[1] for b in six], 0))
        t0 = t0_next
        hi = jnp.concatenate(his, 1)
        lo = jnp.concatenate(los, 1)
        prod = jnp.dot(wh, hi, preferred_element_type=f32)
        prod += jnp.dot(wh, lo, preferred_element_type=f32)
        prod += jnp.dot(wl, hi, preferred_element_type=f32)
        parts = []
        for y in range(LY):
            k = k_ref[x * LY + y : x * LY + y + 1, :]
            m = m_ref[x * LY + y : x * LY + y + 1, :]
            cols = slice(y * LZ, (y + 1) * LZ)
            w = prod[: 6 * AP, cols] * k + prod[6 * AP :, cols] * m
            parts.append([w[b * AP : (b + 1) * AP] for b in range(6)])
        for y in range(LY):
            wlx, wux, wly, wuy, wlz, wuz = parts[y]
            put(0, x, y, wlx if x == 0 else wlx + carry[y])
            put(1, x, y, wly if y == 0 else wly + parts[y - 1][3])
            put(2, x, y, wlz + pltpu.roll(wuz, 1, 1))
            if x == 0 and low_x is not None:
                low_x[pl.ds(y, A, stride=LY), :] = wlx[:A]
            if x == LX - 1:
                up_x[pl.ds(y, A, stride=LY), :] = wux[:A]
        if low_y is not None:
            low_y[pl.ds(x, A, stride=LX), :] = parts[0][2][:A]
        up_y[pl.ds(x, A, stride=LX), :] = parts[LY - 1][3][:A]
        carry = [parts[y][1] for y in range(LY)]


def is_even(axis):
    return lax.rem(lax.axis_index(axis), 2) == 0


def route(even, up, low, near, far):
    near[...] = jnp.where(even, up[...], low[...])
    far[...] = jnp.where(even, low[...], up[...])


def edge_kernel(rhs_ref, fx_ref, fy_ref, sem_x, sem_y):
    face_x = pltpu.make_async_copy(rhs_ref.at[0, :, 0], fx_ref, sem_x)
    face_y = pltpu.make_async_copy(rhs_ref.at[1, :, :, 0], fy_ref, sem_y)
    face_x.start()
    face_y.start()
    face_x.wait()
    face_y.wait()


def weight_kernel(s_ref, m_ref, wh_ref, wl_ref, inv_ref):
    n, padded = 6 * A, 6 * AP
    r = lax.broadcasted_iota(jnp.int32, (padded, n), 0)
    c = lax.broadcasted_iota(jnp.int32, (padded, n), 1)
    node = lax.rem(r, AP)
    place = jnp.where((node < A) & (lax.div(r, AP) * A + node == c), 1.0, 0.0).astype(bf16)
    diagonal = lax.broadcasted_iota(jnp.int32, (n, n), 0) == lax.broadcasted_iota(jnp.int32, (n, n), 1)

    def largest(v):
        return jnp.max(jnp.max(jnp.where(diagonal, v, 0.0), 0, keepdims=True), 1, keepdims=True)

    inv = 1.0 / (10.0 * largest(s_ref[...]) + 2.0 * largest(m_ref[...]))
    inv_ref[...] = jnp.broadcast_to(inv, (8, LZ))
    for i, ref in enumerate((s_ref, m_ref)):
        for part, out in zip(halves(ref[...] * inv), (wh_ref, wl_ref)):
            rows = jnp.dot(place, part, preferred_element_type=f32).astype(bf16)
            full = lax.dot_general(rows, place, (((1,), (1,)), ((), ())), preferred_element_type=f32)
            out[i * padded : (i + 1) * padded] = full.astype(bf16)


def pad(ref, rows):
    ref[rows:] = jnp.zeros((ref.shape[0] - rows, LZ), f32)


def first_kernel(rhs_ref, hx_ref, hy_ref, k_ref, m_ref, wh_ref, wl_ref,
                 p_ref, snx, sfx, sny, sfy, v, ux, uy, upx, lowx, upy, lowy):
    v[:ROWS] = rhs_ref[...]
    pad(v, ROWS)
    ux[: A * LY] = hx_ref[...]
    pad(ux, A * LY)
    uy[: A * LX] = hy_ref[...]
    pad(uy, A * LX)
    apply_operator(v, ux, uy, k_ref, m_ref, wh_ref, wl_ref, p_ref, upx, lowx, upy, lowy)
    route(is_even("gx"), upx, lowx, snx, sfx)
    route(is_even("gy"), upy, lowy, sny, sfy)


def assemble(p_ref, snx, sfx, sny, sfy, rnx, rfx, rny, rfy, v, ux, uy):
    even_x = is_even("gx")
    even_y = is_even("gy")
    v[:ROWS] = p_ref[...]
    pad(v, ROWS)
    below_x = jnp.where(even_x, rfx[...], rnx[...])
    for a in range(A):
        rows = slice(a * CELLS, a * CELLS + LY)
        v[rows, :] = v[rows, :] + below_x[a * LY : (a + 1) * LY]
    below_y = jnp.where(even_y, rfy[...], rny[...])
    first = pl.ds(FACE, A * LX, stride=LY)
    v[first, :] = v[first, :] + below_y
    ux[: A * LY] = jnp.where(even_x, snx[...] + rnx[...], sfx[...] + rfx[...])
    pad(ux, A * LY)
    uy[: A * LX] = jnp.where(even_y, sny[...] + rny[...], sfy[...] + rfy[...])
    pad(uy, A * LX)


def node_sum(value):
    return jnp.sum(value.reshape(-1, LY, LZ), 0)


def row(tile):
    return jnp.sum(tile, 0, keepdims=True)


def second_kernel(p_ref, rhs_ref, rfx, rfy, rny, rnx, snx, sfx, sny, sfy, k_ref, m_ref, wh_ref, wl_ref,
                  v1_ref, p1_ref, tnx, tfx, tny, tfy, sums_ref, ux, uy, upx, lowx, upy, lowy):
    assemble(p_ref, snx, sfx, sny, sfy, rnx, rfx, rny, rfy, v1_ref, ux, uy)
    v0 = rhs_ref[...]
    v1 = v1_ref[:ROWS]
    sums_ref[0:8] = node_sum(v0)
    sums_ref[8:16] = node_sum(v1)
    sums_ref[16:24] = node_sum(v0 * v0)
    sums_ref[24:32] = node_sum(v0 * v1)
    sums_ref[32:40] = node_sum(v1 * v1)
    apply_operator(v1_ref, ux, uy, k_ref, m_ref, wh_ref, wl_ref, p1_ref, upx, lowx, upy, lowy)
    route(is_even("gx"), upx, lowx, tnx, tfx)
    route(is_even("gy"), upy, lowy, tny, tfy)


def third_kernel(p_ref, v1_ref, rfx, rfy, rny, rnx, snx, sfx, sny, sfy, sums_ref, k_ref, m_ref, wh_ref, wl_ref,
                 v2_out, p2_out, upx, upy, loads_ref, v2_ref, p2_ref, ux, uy, v2_sem, p2_sem):
    assemble(p_ref, snx, sfx, sny, sfy, rnx, rfx, rny, rfy, v2_ref, ux, uy)
    v2_copy = pltpu.make_async_copy(v2_ref.at[:ROWS], v2_out, v2_sem)
    v2_copy.start()
    v1 = v1_ref[:ROWS]
    v2 = v2_ref[:ROWS]
    loads_ref[0:16] = sums_ref[0:16]
    loads_ref[16:24] = node_sum(v2)
    m3 = node_sum(v1 * v2)
    m4 = node_sum(v2 * v2)
    apply_operator(v2_ref, ux, uy, k_ref, m_ref, wh_ref, wl_ref, p2_ref, upx, None, upy, None)
    p2_copy = pltpu.make_async_copy(p2_ref, p2_out, p2_sem)
    p2_copy.start()
    p2 = p2_ref[...]
    above = upx[...]
    loads_ref[24:32] = node_sum(p2)
    loads_ref[32:40] = node_sum(above)
    energy = node_sum(v2_ref[:ROWS] * p2) + node_sum(ux[: A * LY] * above)
    tail = row(uy[: A * LX] * upy[...])
    for k in range(3):
        loads_ref[40 + k : 41 + k] = row(sums_ref[16 + 8 * k : 24 + 8 * k])
    loads_ref[43:44] = row(m3)
    loads_ref[44:45] = row(m4)
    loads_ref[45:46] = row(energy) + tail
    loads_ref[46:47] = row(upy[...])
    loads_ref[47:48] = jnp.zeros((1, LZ), f32)
    v2_copy.wait()
    p2_copy.wait()


def weigh_kernel(own, near, far, both, upx, upy, *outs, table, ny):
    *outs, mom_ref, cx_ref, cy_ref = outs
    cx_ref[...] = upx[...]
    cy_ref[...] = upy[...]
    nx = len(table)
    me = lax.axis_index("gx")
    q = lax.rem(me, 4)
    low, high = lax.rem(q, 2) == 0, q < 2
    one, two = jnp.where(low, 1, -1), jnp.where(high, 2, -2)
    sources = ((own, 0, (0,)), (near, one, (1, -1)), (far, two, (2, -2)), (both, one + two, (3, 1, -1, -3)))

    def pick(at, shift, span):
        value = jnp.float32(table[(at - span[0]) % nx])
        for s in span[1:]:
            value = jnp.where(shift == s, table[(at - s) % nx], value)
        return value

    tile = own[40:48] + near[40:48] + far[40:48] + both[40:48]
    for lanes in (64, 32, 16):
        tile = tile + pltpu.roll(tile, lanes, 1)
    lane = lax.broadcasted_iota(jnp.int32, (8, LZ), 1)
    moment = lax.broadcasted_iota(jnp.int32, (8, LZ), 0)
    packed = row(jnp.where((lax.div(lane, 16) == moment) & (moment < 6), tile, 0.0))
    groups = nx // 4
    for z, out in enumerate(outs):
        total = [0.0] * 4
        edge = 0.0
        for ref, shift, span in sources:
            w = pick(4 * z, shift, span)
            for k in range(4):
                total[k] = total[k] + ref[k * 8 : k * 8 + 8] * w
            total[3] = total[3] + ref[32:40] * pick(4 * z - 1, shift, span)
            edge = edge + ref[46:47] * w
        for k in range(4):
            out[k * 8 : k * 8 + 8] = total[k]
        pair = jnp.concatenate([packed, edge] * 4, 0)
        first = lax.rem(lax.div(me, 4) + z, groups) * (2 * ny)
        for at in range(0, 2 * ny, 8):
            mom_ref[pl.ds(pl.multiple_of(first + at, 8), 8), :] = pair


def two_sum(a, b):
    s = a + b
    t = s - a
    return s, (a - (s - t)) + (b - t)


def pair_add(a, b):
    s, e = two_sum(a[0], b[0])
    e = e + (a[1] + b[1])
    h = s + e
    return h, e - (h - s)


def split(a):
    t = a * 4097.0
    h = t - (t - a)
    return h, a - h


def pair_times(a, c):
    p = a[0] * c
    ah, al = split(a[0])
    ch, cl = split(c)
    return p, ((ah * ch - p) + ah * cl + al * ch) + al * cl + a[1] * c


def moments(got):
    pairs = [(got[at : at + 8], jnp.zeros((8, LZ), f32)) for at in range(0, got.shape[0], 8)]
    while len(pairs) > 1:
        pairs = [pair_add(a, b) for a, b in zip(pairs[::2], pairs[1::2])]
    t = pairs[0]
    for rows in (4, 2):
        t = pair_add(t, tuple(pltpu.roll(p, rows, 0) for p in t))
    for lanes in (8, 4, 2, 1):
        t = pair_add(t, tuple(pltpu.roll(p, LZ - lanes, 1) for p in t))
    c = t[0][0:1, 16:17] / t[0][0:1, 0:1]
    wide = jnp.broadcast_to(c, (8, LZ))
    m = [t[0][0:1, 0:1]]
    for _ in range(5):
        up = tuple(pltpu.roll(p, LZ - 16, 1) for p in t)
        t = pair_add(up, pair_times(t, -wide))
        m.append(t[0][0:1, 0:1])
    return c, m


def conjugate_gradient(c, m):
    def dot(a, b):
        s = None
        for i, ai in enumerate(a):
            for j, bj in enumerate(b):
                t = ai * bj * m[i + j]
                s = t if s is None else s + t
        return s

    def add(a, b, factor):
        longer = []
        for i in range(max(len(a), len(b))):
            if i >= len(b):
                longer.append(a[i])
            elif i >= len(a):
                longer.append(factor * b[i])
            else:
                longer.append(a[i] + factor * b[i])
        return longer

    def times(a, shift):
        return [a[0] * shift] + [a[i] * shift + a[i - 1] for i in range(1, len(a))] + [a[-1]]

    def plain(a):
        out = [a[-1]]
        for coefficient in a[-2::-1]:
            out = times(out, -c)
            out[0] = out[0] + coefficient
        return out

    one = jnp.ones((1, 1), f32)
    iterate, residual, direction = [], [one], [one]
    norm = m[0]
    for step in range(ITERS):
        img = times(direction, c)
        alpha = norm / dot(direction, img)
        iterate = add(iterate, direction, alpha)
        residual = add(residual, img, -alpha)
        if step < ITERS - 1:
            norm_next = dot(residual, residual)
            direction = add(residual, direction, norm_next / norm)
            norm = norm_next
    return plain(iterate), plain(residual)


def last_kernel(prolong_ref, got_ref, c0, c1, c2, c3, inv_ref, rhs_ref, v1_ref, v2_hbm, p2_hbm, rx_ref, ry_ref,
                sol_hbm, res_hbm, coarse_ref, v2_ref, p2_ref, sol_ref, res_ref, in_sems, out_sems, *, ny):
    fetches = []
    for f in range(F):
        rows = pl.ds(f * FACE, FACE)
        for i, (src, dst) in enumerate(((v2_hbm, v2_ref), (p2_hbm, p2_ref))):
            fetches.append(pltpu.make_async_copy(src.at[rows], dst.at[rows], in_sems.at[2 * f + i]))
            fetches[-1].start()
    x, d = conjugate_gradient(*moments(got_ref[...]))
    inv = inv_ref[0:1, 0:1]
    x = [t * inv for t in x]
    below = lax.rem(lax.axis_index("gy") + ny - 1, ny)
    edge = jnp.zeros((1, LZ), f32)
    for z in range(got_ref.shape[0] // (2 * ny)):
        edge = edge + got_ref[pl.ds(2 * (z * ny + below) + 1, 1), :]
    circ = [c0[k * 8 : k * 8 + 8] + c1[k * 8 : k * 8 + 8] + c2[k * 8 : k * 8 + 8] + c3[k * 8 : k * 8 + 8] for k in range(4)]
    at_first = lax.broadcasted_iota(jnp.int32, (LY, LZ), 0) == 0
    circ[3] = circ[3] + jnp.where(at_first, jnp.broadcast_to(edge, (LY, LZ)), 0.0)
    coarse = d[0] * circ[0] + d[1] * circ[1] + d[2] * circ[2] + d[3] * circ[3]
    coarse_ref[...] = coarse
    x = [jnp.broadcast_to(t, (LY, LZ)) for t in x]
    d = [jnp.broadcast_to(t, (LY, LZ)) for t in d]
    stores = []
    for f in range(F):
        fetches[2 * f].wait()
        fetches[2 * f + 1].wait()
        for a in range(A):
            at = (f * A + a) * CELLS
            spread = coarse * prolong_ref[f, a]
            for cell in range(LX):
                rows = slice(at + cell * LY, at + (cell + 1) * LY)
                v0, v1, v2 = rhs_ref[rows, :], v1_ref[rows, :], v2_ref[rows, :]
                img = p2_ref[rows, :]
                if f == 0 and cell == 0:
                    img = img + rx_ref[a * LY : (a + 1) * LY, :]
                sol_ref[rows, :] = x[0] * v0 + x[1] * v1 + x[2] * v2 + spread
                res_ref[rows, :] = d[0] * v0 + d[1] * v1 + d[2] * v2 + d[3] * img
        if f == 1:
            first = pl.ds(FACE, A * LX, stride=LY)
            res_ref[first, :] = res_ref[first, :] + d[3][0:1] * ry_ref[...]
        rows = pl.ds(f * FACE, FACE)
        for i, (src, dst) in enumerate(((sol_ref, sol_hbm), (res_ref, res_hbm))):
            stores.append(pltpu.make_async_copy(src.at[rows], dst.at[rows], out_sems.at[2 * f + i]))
            stores[-1].start()
    for store in stores:
        store.wait()


def jacobi_weights(n):
    coarse = np.zeros(n)
    load = np.zeros(n)
    load[0] = 1.0
    for _ in range(SWEEPS):
        coarse = (load + np.roll(coarse, 1) + np.roll(coarse, -1)) / 2.2
    return coarse / 75.0


def struct(*shape):
    return jax.ShapeDtypeStruct(shape, f32)


PARAMS = pltpu.CompilerParams(vmem_limit_bytes=16 * 1024 * 1024)


def shards(rhs, kappa, mass, stiffness, mass_matrix, prolong):
    nx, ny = lax.axis_size("gx"), lax.axis_size("gy")
    vx, vy = A * LY, A * LX
    rhs2 = rhs.reshape(ROWS, LZ)
    k2 = kappa.reshape(CELLS, LZ)
    m2 = mass.reshape(CELLS, LZ)
    sends = [struct(vx, LZ), struct(vx, LZ), struct(vy, LZ), struct(vy, LZ)]
    upper = [pltpu.VMEM((AP * LY, LZ), f32), pltpu.VMEM((AP * LX, LZ), f32)]
    field = [pltpu.VMEM((PADDED, LZ), f32)] + upper
    edges = [pltpu.VMEM((vx, LZ), f32)] * 2 + [pltpu.VMEM((vy, LZ), f32)] * 2

    def call(kernel, name, ins, outs, scratch=(), **static):
        specs = [i[1] if isinstance(i, tuple) else VM for i in ins]
        ins = [i[0] if isinstance(i, tuple) else i for i in ins]

        def bound(*refs):
            kernel(*refs, **static)

        return pl.pallas_call(
            bound,
            out_shape=outs,
            in_specs=specs,
            out_specs=[ANY if isinstance(o, pl.MemoryRef) else VM for o in outs],
            scratch_shapes=list(scratch),
            compiler_params=PARAMS,
            name=name,
        )(*ins)

    def swap(s):
        far_x = far_swap(s[1], "gx")
        far_y = far_swap(s[3], "gy")
        near_y = near_swap(s[2], "gy")
        near_x = near_swap(s[0], "gx")
        return [far_x, far_y, near_y, near_x]

    hbm = pltpu.with_memory_space_constraint(rhs, pltpu.HBM)
    fx, fy = call(
        edge_kernel, "edges", [(hbm, ANY)], [struct(A, LY, LZ), struct(A, LX, LZ)],
        [pltpu.SemaphoreType.DMA, pltpu.SemaphoreType.DMA],
    )
    hx = shifted(fx.reshape(vx, LZ), "gx", -1)
    hy = shifted(fy.reshape(vy, LZ), "gy", -1)
    half = jax.ShapeDtypeStruct((12 * AP, 6 * AP), bf16)
    wh, wl, inv = call(weight_kernel, "weights", [stiffness, mass_matrix], [half, half, struct(8, LZ)])

    p0, *s = call(
        first_kernel, "first", [rhs2, hx, hy, k2, m2, wh, wl], [struct(ROWS, LZ)] + sends, field + edges,
    )
    r = swap(s)
    v1, p1, *s, sums = call(
        second_kernel, "second", [p0, rhs2, *r, *s, k2, m2, wh, wl],
        [struct(PADDED, LZ), struct(ROWS, LZ)] + sends + [struct(40, LZ)], upper + edges,
    )
    r = swap(s)
    dma = pltpu.SemaphoreType.DMA
    v2, p2, upx, upy, loads = call(
        third_kernel, "third", [p1, v1, *r, *s, sums, k2, m2, wh, wl],
        [pltpu.HBM((ROWS, LZ), f32)] * 2 + [struct(vx, LZ), struct(vy, LZ), struct(48, LZ)],
        [field[0], pltpu.VMEM((ROWS, LZ), f32)] + upper + [dma, dma],
    )
    table = [float(t) for t in jacobi_weights(nx)]
    group = [lax.ppermute(loads, "gx", [(i, i ^ b) for i in range(nx)]) for b in (1, 2, 3)]
    *pieces, mom, upx, upy = call(
        weigh_kernel, "weigh", [loads, *group, upx, upy],
        [struct(32, LZ)] * (nx // 4) + [struct(nx // 4 * ny * 2, LZ), struct(vx, LZ), struct(vy, LZ)], table=table, ny=ny,
    )
    coarse = [pieces[0]] + [shifted(p, "gx", 4 * z) for z, p in enumerate(pieces) if z]
    alike = [[(4 * z + q) * ny + y for z in range(nx // 4) for y in range(ny)] for q in range(4)]
    got = lax.all_to_all(mom.reshape(-1, 2, LZ), ("gx", "gy"), 0, 0, tiled=True, axis_index_groups=alike).reshape(mom.shape)
    rx = shifted(upx, "gx", 1)
    ry = shifted(upy, "gy", 1)
    v2, p2 = (pltpu.with_memory_space_constraint(v, pltpu.HBM) for v in (v2, p2))
    sol, res, coarse = call(
        last_kernel, "last", [(prolong, SM), got, *coarse, inv, rhs2, v1, (v2, ANY), (p2, ANY), rx, ry],
        [pltpu.HBM((ROWS, LZ), f32)] * 2 + [struct(LY, LZ)],
        [pltpu.VMEM((ROWS, LZ), f32)] * 4 + [pltpu.SemaphoreType.DMA((6,))] * 2, ny=ny,
    )
    return sol.reshape(rhs.shape), res.reshape(rhs.shape), coarse[None]


def solution(mesh):
    placed = (
        P(None, None, "gx", "gy", None),
        P("gx", "gy", None),
        P("gx", "gy", None),
        P(),
        P(),
        P(),
    )
    return jax.shard_map(
        shards,
        mesh=mesh,
        in_specs=placed,
        out_specs=(
            P(None, None, "gx", "gy", None),
            P(None, None, "gx", "gy", None),
            P("gx", "gy", None),
        ),
        check_vma=False,
    )
```

```python
import jax
import jax.numpy as jnp
import numpy as np
from jax import lax
from jax.experimental import pallas as pl
from jax.experimental.pallas import tpu as pltpu
from jax.sharding import PartitionSpec as P

ITERS = 3
SWEEPS = 8
F, A = 3, 25
B = 24
LAST = 6 * B
OUT, IN = LAST + 8, LAST + 16
LX, LY, LZ = 4, 8, 128
CELLS = LX * LY
FACE = A * CELLS
ROWS = F * FACE
f32, bf16 = jnp.float32, jnp.bfloat16
VM = pl.BlockSpec(memory_space=pltpu.VMEM)
SM = pl.BlockSpec(memory_space=pltpu.SMEM)
ANY = pl.BlockSpec(memory_space=pl.ANY)


def shifted(value, axis, by):
    n = lax.axis_size(axis)
    return lax.ppermute(value, axis, [(i, (i + by) % n) for i in range(n)])


def near_swap(value, axis):
    n = lax.axis_size(axis)
    return lax.ppermute(value, axis, [(i, i ^ 1) for i in range(n)])


def far_swap(value, axis):
    n = lax.axis_size(axis)
    pairs = [(i, (i + 1) % n) if i % 2 else (i, (i - 1) % n) for i in range(n)]
    return lax.ppermute(value, axis, pairs)


def halves(v):
    hi = v.astype(bf16)
    lo = (v - hi.astype(f32)).astype(bf16)
    return hi, lo


def apply_operator(v_ref, ux_ref, uy_ref, k_ref, m_ref, w_ref, out_ref, up_x, low_x, up_y, low_y, last_in, last_out):
    w_all = w_ref[...]
    at_first = lax.broadcasted_iota(jnp.int32, (LY, LZ), 0) == 0
    last_in[LAST // B * LY :] = jnp.zeros((2 * LY, LZ), f32)

    def face(f, x, y):
        if f == 0 and x == LX:
            return ux_ref[pl.ds(y, B, stride=LY), :]
        if f == 1 and y == LY:
            return uy_ref[pl.ds(x, B, stride=LX), :]
        return v_ref[pl.ds(f * FACE + x * LY + y, B, stride=CELLS), :]

    def last_rows(f, x):
        if x == LX:
            return ux_ref[B * LY :, :]
        at = f * FACE + B * CELLS + x * LY
        return v_ref[at : at + LY, :]

    def put(f, x, y, value):
        out_ref[pl.ds(f * FACE + x * LY + y, B, stride=CELLS), :] = value

    def put_last(f, x, value):
        at = f * FACE + B * CELLS + x * LY
        out_ref[at : at + LY, :] = value

    filler = jnp.zeros((IN - OUT, LZ), f32)
    carry = last_carry = None
    for x in range(LX):
        z_last = last_rows(2, x)
        y_last = last_rows(1, x)
        above = uy_ref[B * LX + x : B * LX + x + 1, :]
        top = lax.broadcasted_iota(jnp.int32, (LY, LZ), 0) == LY - 1
        y_up = jnp.where(top, jnp.broadcast_to(above, (LY, LZ)), pltpu.roll(y_last, LY - 1, 0))
        for j, tile in enumerate((last_rows(0, x), y_last, z_last, last_rows(0, x + 1), y_up, pltpu.roll(z_last, LZ - 1, 1))):
            last_in[j * LY : (j + 1) * LY] = tile
        columns = []
        for y in range(LY):
            z = face(2, x, y)
            six = [face(0, x, y), face(0, x + 1, y), face(1, x, y), face(1, x, y + 1), z, pltpu.roll(z, LZ - 1, 1)]
            columns.append(jnp.concatenate(six + [last_in[pl.ds(y, 8, stride=LY), :], filler], 0))
        hi, lo = halves(jnp.concatenate(columns, 1))
        prod = jnp.dot(w_all, jnp.concatenate([hi, lo, hi], 0), preferred_element_type=f32)
        parts = []
        for y in range(LY):
            k = k_ref[x * LY + y : x * LY + y + 1, :]
            m = m_ref[x * LY + y : x * LY + y + 1, :]
            cols = slice(y * LZ, (y + 1) * LZ)
            w = prod[:OUT, cols] * k + prod[OUT:, cols] * m
            parts.append([w[b * B : (b + 1) * B] for b in range(6)])
            last_out[pl.ds(y, 8, stride=LY), :] = w[LAST:]
        for y in range(LY):
            wlx, wux, wly, wuy, wlz, wuz = parts[y]
            put(0, x, y, wlx if x == 0 else wlx + carry[y])
            put(1, x, y, wly if y == 0 else wly + parts[y - 1][3])
            put(2, x, y, wlz + pltpu.roll(wuz, 1, 1))
            if x == 0 and low_x is not None:
                low_x[pl.ds(y, B, stride=LY), :] = wlx
            if x == LX - 1:
                up_x[pl.ds(y, B, stride=LY), :] = wux
        tiles = [last_out[j * LY : (j + 1) * LY] for j in range(6)]
        put_last(0, x, tiles[0] if x == 0 else tiles[0] + last_carry)
        put_last(1, x, tiles[1] + jnp.where(at_first, 0.0, pltpu.roll(tiles[4], 1, 0)))
        put_last(2, x, tiles[2] + pltpu.roll(tiles[5], 1, 1))
        if x == 0 and low_x is not None:
            low_x[B * LY :] = tiles[0]
        if x == LX - 1:
            up_x[B * LY :] = tiles[3]
        if low_y is not None:
            low_y[pl.ds(x, B, stride=LX), :] = parts[0][2]
            low_y[B * LX + x : B * LX + x + 1] = tiles[1][:1]
        up_y[pl.ds(x, B, stride=LX), :] = parts[LY - 1][3]
        up_y[B * LX + x : B * LX + x + 1] = tiles[4][LY - 1 :]
        carry = [parts[y][1] for y in range(LY)]
        last_carry = tiles[3]


def is_even(axis):
    return lax.rem(lax.axis_index(axis), 2) == 0


def route(even, up, low, near, far):
    near[...] = jnp.where(even, up[...], low[...])
    far[...] = jnp.where(even, low[...], up[...])


def edge_kernel(rhs_ref, fx_ref, fy_ref, sem_x, sem_y):
    face_x = pltpu.make_async_copy(rhs_ref.at[0, :, 0], fx_ref, sem_x)
    face_y = pltpu.make_async_copy(rhs_ref.at[1, :, :, 0], fy_ref, sem_y)
    face_x.start()
    face_y.start()
    face_x.wait()
    face_y.wait()


def weight_kernel(s_ref, m_ref, w_ref, inv_ref):
    n = 6 * A

    def placing(rows, span):
        r = lax.broadcasted_iota(jnp.int32, (rows, n), 0)
        c = lax.broadcasted_iota(jnp.int32, (rows, n), 1)
        p = lax.rem(r, span)
        j = p - LAST
        node = jnp.where(p < LAST, lax.div(p, B) * A + lax.rem(p, B), (2 * lax.rem(j, 3) + lax.div(j, 3)) * A + B)
        return (node == c) & (p < n), lax.div(r, span)

    def ones(mask):
        return jnp.where(mask, 1.0, 0.0).astype(bf16)

    rows = ones(placing(OUT, OUT)[0])
    mask, third = placing(3 * IN, IN)
    columns = (ones(mask & (third < 2)), ones(mask & (third == 2)))
    diagonal = lax.broadcasted_iota(jnp.int32, (n, n), 0) == lax.broadcasted_iota(jnp.int32, (n, n), 1)

    def largest(v):
        return jnp.max(jnp.max(jnp.where(diagonal, v, 0.0), 0, keepdims=True), 1, keepdims=True)

    inv = 1.0 / (10.0 * largest(s_ref[...]) + 2.0 * largest(m_ref[...]))
    inv_ref[...] = jnp.broadcast_to(inv, (8, LZ))
    for i, ref in enumerate((s_ref, m_ref)):
        full = 0.0
        for part, place in zip(halves(ref[...] * inv), columns):
            moved = jnp.dot(rows, part, preferred_element_type=f32).astype(bf16)
            full = full + lax.dot_general(moved, place, (((1,), (1,)), ((), ())), preferred_element_type=f32)
        w_ref[i * OUT : (i + 1) * OUT] = full.astype(bf16)


def first_kernel(rhs_ref, hx_ref, hy_ref, k_ref, m_ref, w_ref,
                 p_ref, snx, sfx, sny, sfy, v, ux, uy, last_in, last_out, upx, lowx, upy, lowy):
    v[...] = rhs_ref[...]
    ux[...] = hx_ref[...]
    uy[...] = hy_ref[...]
    apply_operator(v, ux, uy, k_ref, m_ref, w_ref, p_ref, upx, lowx, upy, lowy, last_in, last_out)
    route(is_even("gx"), upx, lowx, snx, sfx)
    route(is_even("gy"), upy, lowy, sny, sfy)


def assemble(p_ref, snx, sfx, sny, sfy, rnx, rfx, rny, rfy, v, ux, uy):
    even_x = is_even("gx")
    even_y = is_even("gy")
    v[...] = p_ref[...]
    below_x = jnp.where(even_x, rfx[...], rnx[...])
    for a in range(A):
        rows = slice(a * CELLS, a * CELLS + LY)
        v[rows, :] = v[rows, :] + below_x[a * LY : (a + 1) * LY]
    below_y = jnp.where(even_y, rfy[...], rny[...])
    first = pl.ds(FACE, A * LX, stride=LY)
    v[first, :] = v[first, :] + below_y
    ux[...] = jnp.where(even_x, snx[...] + rnx[...], sfx[...] + rfx[...])
    uy[...] = jnp.where(even_y, sny[...] + rny[...], sfy[...] + rfy[...])


def node_sum(value):
    return jnp.sum(value.reshape(-1, LY, LZ), 0)


def row(tile):
    return jnp.sum(tile, 0, keepdims=True)


def second_kernel(p_ref, rhs_ref, rfx, rfy, rny, rnx, snx, sfx, sny, sfy, k_ref, m_ref, w_ref,
                  v1_ref, p1_ref, tnx, tfx, tny, tfy, sums_ref, ux, uy, last_in, last_out, upx, lowx, upy, lowy):
    assemble(p_ref, snx, sfx, sny, sfy, rnx, rfx, rny, rfy, v1_ref, ux, uy)
    v0 = rhs_ref[...]
    v1 = v1_ref[...]
    sums_ref[0:8] = node_sum(v0)
    sums_ref[8:16] = node_sum(v1)
    sums_ref[16:24] = node_sum(v0 * v0)
    sums_ref[24:32] = node_sum(v0 * v1)
    sums_ref[32:40] = node_sum(v1 * v1)
    apply_operator(v1_ref, ux, uy, k_ref, m_ref, w_ref, p1_ref, upx, lowx, upy, lowy, last_in, last_out)
    route(is_even("gx"), upx, lowx, tnx, tfx)
    route(is_even("gy"), upy, lowy, tny, tfy)


def third_kernel(p_ref, v1_ref, rfx, rfy, rny, rnx, snx, sfx, sny, sfy, sums_ref, k_ref, m_ref, w_ref,
                 v2_out, p2_out, upx, upy, loads_ref, v2_ref, p2_ref, ux, uy, last_in, last_out, v2_sem, p2_sem):
    assemble(p_ref, snx, sfx, sny, sfy, rnx, rfx, rny, rfy, v2_ref, ux, uy)
    v2_copy = pltpu.make_async_copy(v2_ref, v2_out, v2_sem)
    v2_copy.start()
    v1 = v1_ref[...]
    v2 = v2_ref[...]
    loads_ref[0:16] = sums_ref[0:16]
    loads_ref[16:24] = node_sum(v2)
    m3 = node_sum(v1 * v2)
    m4 = node_sum(v2 * v2)
    apply_operator(v2_ref, ux, uy, k_ref, m_ref, w_ref, p2_ref, upx, None, upy, None, last_in, last_out)
    p2_copy = pltpu.make_async_copy(p2_ref, p2_out, p2_sem)
    p2_copy.start()
    p2 = p2_ref[...]
    above = upx[...]
    loads_ref[24:32] = node_sum(p2)
    loads_ref[32:40] = node_sum(above)
    energy = node_sum(v2_ref[...] * p2) + node_sum(ux[...] * above)
    tail = row(uy[...] * upy[...])
    for k in range(3):
        loads_ref[40 + k : 41 + k] = row(sums_ref[16 + 8 * k : 24 + 8 * k])
    loads_ref[43:44] = row(m3)
    loads_ref[44:45] = row(m4)
    loads_ref[45:46] = row(energy) + tail
    loads_ref[46:47] = row(upy[...])
    loads_ref[47:48] = jnp.zeros((1, LZ), f32)
    v2_copy.wait()
    p2_copy.wait()


def weigh_kernel(own, near, far, both, upx, upy, *outs, table, ny):
    *outs, mom_ref, cx_ref, cy_ref = outs
    cx_ref[...] = upx[...]
    cy_ref[...] = upy[...]
    nx = len(table)
    me = lax.axis_index("gx")
    q = lax.rem(me, 4)
    low, high = lax.rem(q, 2) == 0, q < 2
    one, two = jnp.where(low, 1, -1), jnp.where(high, 2, -2)
    sources = ((own, 0, (0,)), (near, one, (1, -1)), (far, two, (2, -2)), (both, one + two, (3, 1, -1, -3)))

    def pick(at, shift, span):
        value = jnp.float32(table[(at - span[0]) % nx])
        for s in span[1:]:
            value = jnp.where(shift == s, table[(at - s) % nx], value)
        return value

    tile = own[40:48] + near[40:48] + far[40:48] + both[40:48]
    for lanes in (64, 32, 16):
        tile = tile + pltpu.roll(tile, lanes, 1)
    lane = lax.broadcasted_iota(jnp.int32, (8, LZ), 1)
    moment = lax.broadcasted_iota(jnp.int32, (8, LZ), 0)
    packed = row(jnp.where((lax.div(lane, 16) == moment) & (moment < 6), tile, 0.0))
    groups = nx // 4
    for z, out in enumerate(outs):
        total = [0.0] * 4
        edge = 0.0
        for ref, shift, span in sources:
            w = pick(4 * z, shift, span)
            for k in range(4):
                total[k] = total[k] + ref[k * 8 : k * 8 + 8] * w
            total[3] = total[3] + ref[32:40] * pick(4 * z - 1, shift, span)
            edge = edge + ref[46:47] * w
        for k in range(4):
            out[k * 8 : k * 8 + 8] = total[k]
        pair = jnp.concatenate([packed, edge] * 4, 0)
        first = lax.rem(lax.div(me, 4) + z, groups) * (2 * ny)
        for at in range(0, 2 * ny, 8):
            mom_ref[pl.ds(pl.multiple_of(first + at, 8), 8), :] = pair


def two_sum(a, b):
    s = a + b
    t = s - a
    return s, (a - (s - t)) + (b - t)


def pair_add(a, b):
    s, e = two_sum(a[0], b[0])
    e = e + (a[1] + b[1])
    h = s + e
    return h, e - (h - s)


def split(a):
    t = a * 4097.0
    h = t - (t - a)
    return h, a - h


def pair_times(a, c):
    p = a[0] * c
    ah, al = split(a[0])
    ch, cl = split(c)
    return p, ((ah * ch - p) + ah * cl + al * ch) + al * cl + a[1] * c


def moments(got):
    pairs = [(got[at : at + 8], jnp.zeros((8, LZ), f32)) for at in range(0, got.shape[0], 8)]
    while len(pairs) > 1:
        pairs = [pair_add(a, b) for a, b in zip(pairs[::2], pairs[1::2])]
    t = pairs[0]
    for rows in (4, 2):
        t = pair_add(t, tuple(pltpu.roll(p, rows, 0) for p in t))
    for lanes in (8, 4, 2, 1):
        t = pair_add(t, tuple(pltpu.roll(p, LZ - lanes, 1) for p in t))
    c = t[0][0:1, 16:17] / t[0][0:1, 0:1]
    wide = jnp.broadcast_to(c, (8, LZ))
    m = [t[0][0:1, 0:1]]
    for _ in range(5):
        up = tuple(pltpu.roll(p, LZ - 16, 1) for p in t)
        t = pair_add(up, pair_times(t, -wide))
        m.append(t[0][0:1, 0:1])
    return c, m


def conjugate_gradient(c, m):
    def dot(a, b):
        s = None
        for i, ai in enumerate(a):
            for j, bj in enumerate(b):
                t = ai * bj * m[i + j]
                s = t if s is None else s + t
        return s

    def add(a, b, factor):
        longer = []
        for i in range(max(len(a), len(b))):
            if i >= len(b):
                longer.append(a[i])
            elif i >= len(a):
                longer.append(factor * b[i])
            else:
                longer.append(a[i] + factor * b[i])
        return longer

    def times(a, shift):
        return [a[0] * shift] + [a[i] * shift + a[i - 1] for i in range(1, len(a))] + [a[-1]]

    def plain(a):
        out = [a[-1]]
        for coefficient in a[-2::-1]:
            out = times(out, -c)
            out[0] = out[0] + coefficient
        return out

    one = jnp.ones((1, 1), f32)
    iterate, residual, direction = [], [one], [one]
    norm = m[0]
    for step in range(ITERS):
        img = times(direction, c)
        alpha = norm / dot(direction, img)
        iterate = add(iterate, direction, alpha)
        residual = add(residual, img, -alpha)
        if step < ITERS - 1:
            norm_next = dot(residual, residual)
            direction = add(residual, direction, norm_next / norm)
            norm = norm_next
    return plain(iterate), plain(residual)


def last_kernel(prolong_ref, got_ref, c0, c1, c2, c3, inv_ref, rhs_ref, v1_ref, v2_hbm, p2_hbm, rx_ref, ry_ref,
                sol_hbm, res_hbm, coarse_ref, v2_ref, p2_ref, sol_ref, res_ref, in_sems, out_sems, *, ny):
    fetches = []
    for f in range(F):
        rows = pl.ds(f * FACE, FACE)
        for i, (src, dst) in enumerate(((v2_hbm, v2_ref), (p2_hbm, p2_ref))):
            fetches.append(pltpu.make_async_copy(src.at[rows], dst.at[rows], in_sems.at[2 * f + i]))
            fetches[-1].start()
    x, d = conjugate_gradient(*moments(got_ref[...]))
    inv = inv_ref[0:1, 0:1]
    x = [t * inv for t in x]
    below = lax.rem(lax.axis_index("gy") + ny - 1, ny)
    edge = jnp.zeros((1, LZ), f32)
    for z in range(got_ref.shape[0] // (2 * ny)):
        edge = edge + got_ref[pl.ds(2 * (z * ny + below) + 1, 1), :]
    circ = [c0[k * 8 : k * 8 + 8] + c1[k * 8 : k * 8 + 8] + c2[k * 8 : k * 8 + 8] + c3[k * 8 : k * 8 + 8] for k in range(4)]
    at_first = lax.broadcasted_iota(jnp.int32, (LY, LZ), 0) == 0
    circ[3] = circ[3] + jnp.where(at_first, jnp.broadcast_to(edge, (LY, LZ)), 0.0)
    coarse = d[0] * circ[0] + d[1] * circ[1] + d[2] * circ[2] + d[3] * circ[3]
    coarse_ref[...] = coarse
    x = [jnp.broadcast_to(t, (LY, LZ)) for t in x]
    d = [jnp.broadcast_to(t, (LY, LZ)) for t in d]
    stores = []
    for f in range(F):
        fetches[2 * f].wait()
        fetches[2 * f + 1].wait()
        for a in range(A):
            at = (f * A + a) * CELLS
            spread = coarse * prolong_ref[f, a]
            for cell in range(LX):
                rows = slice(at + cell * LY, at + (cell + 1) * LY)
                v0, v1, v2 = rhs_ref[rows, :], v1_ref[rows, :], v2_ref[rows, :]
                img = p2_ref[rows, :]
                if f == 0 and cell == 0:
                    img = img + rx_ref[a * LY : (a + 1) * LY, :]
                sol_ref[rows, :] = x[0] * v0 + x[1] * v1 + x[2] * v2 + spread
                res_ref[rows, :] = d[0] * v0 + d[1] * v1 + d[2] * v2 + d[3] * img
        if f == 1:
            first = pl.ds(FACE, A * LX, stride=LY)
            res_ref[first, :] = res_ref[first, :] + d[3][0:1] * ry_ref[...]
        rows = pl.ds(f * FACE, FACE)
        for i, (src, dst) in enumerate(((sol_ref, sol_hbm), (res_ref, res_hbm))):
            stores.append(pltpu.make_async_copy(src.at[rows], dst.at[rows], out_sems.at[2 * f + i]))
            stores[-1].start()
    for store in stores:
        store.wait()


def jacobi_weights(n):
    coarse = np.zeros(n)
    load = np.zeros(n)
    load[0] = 1.0
    for _ in range(SWEEPS):
        coarse = (load + np.roll(coarse, 1) + np.roll(coarse, -1)) / 2.2
    return coarse / 75.0


def struct(*shape):
    return jax.ShapeDtypeStruct(shape, f32)


PARAMS = pltpu.CompilerParams(vmem_limit_bytes=16 * 1024 * 1024)


def shards(rhs, kappa, mass, stiffness, mass_matrix, prolong):
    nx, ny = lax.axis_size("gx"), lax.axis_size("gy")
    vx, vy = A * LY, A * LX
    rhs2 = rhs.reshape(ROWS, LZ)
    k2 = kappa.reshape(CELLS, LZ)
    m2 = mass.reshape(CELLS, LZ)
    sends = [struct(vx, LZ), struct(vx, LZ), struct(vy, LZ), struct(vy, LZ)]
    upper = [pltpu.VMEM((vx, LZ), f32), pltpu.VMEM((vy, LZ), f32)] + [pltpu.VMEM((8 * LY, LZ), f32)] * 2
    field = [pltpu.VMEM((ROWS, LZ), f32)] + upper
    edges = [pltpu.VMEM((vx, LZ), f32)] * 2 + [pltpu.VMEM((vy, LZ), f32)] * 2

    def call(kernel, name, ins, outs, scratch=(), **static):
        specs = [i[1] if isinstance(i, tuple) else VM for i in ins]
        ins = [i[0] if isinstance(i, tuple) else i for i in ins]

        def bound(*refs):
            kernel(*refs, **static)

        return pl.pallas_call(
            bound,
            out_shape=outs,
            in_specs=specs,
            out_specs=[ANY if isinstance(o, pl.MemoryRef) else VM for o in outs],
            scratch_shapes=list(scratch),
            compiler_params=PARAMS,
            name=name,
        )(*ins)

    def swap(s):
        far_x = far_swap(s[1], "gx")
        far_y = far_swap(s[3], "gy")
        near_y = near_swap(s[2], "gy")
        near_x = near_swap(s[0], "gx")
        return [far_x, far_y, near_y, near_x]

    hbm = pltpu.with_memory_space_constraint(rhs, pltpu.HBM)
    fx, fy = call(
        edge_kernel, "edges", [(hbm, ANY)], [struct(A, LY, LZ), struct(A, LX, LZ)],
        [pltpu.SemaphoreType.DMA, pltpu.SemaphoreType.DMA],
    )
    hx = shifted(fx.reshape(vx, LZ), "gx", -1)
    hy = shifted(fy.reshape(vy, LZ), "gy", -1)
    w, inv = call(
        weight_kernel, "weights", [stiffness, mass_matrix],
        [jax.ShapeDtypeStruct((2 * OUT, 3 * IN), bf16), struct(8, LZ)],
    )

    p0, *s = call(
        first_kernel, "first", [rhs2, hx, hy, k2, m2, w], [struct(ROWS, LZ)] + sends, field + edges,
    )
    r = swap(s)
    v1, p1, *s, sums = call(
        second_kernel, "second", [p0, rhs2, *r, *s, k2, m2, w],
        [struct(ROWS, LZ), struct(ROWS, LZ)] + sends + [struct(40, LZ)], upper + edges,
    )
    r = swap(s)
    dma = pltpu.SemaphoreType.DMA
    v2, p2, upx, upy, loads = call(
        third_kernel, "third", [p1, v1, *r, *s, sums, k2, m2, w],
        [pltpu.HBM((ROWS, LZ), f32)] * 2 + [struct(vx, LZ), struct(vy, LZ), struct(48, LZ)],
        [field[0], pltpu.VMEM((ROWS, LZ), f32)] + upper + [dma, dma],
    )
    table = [float(t) for t in jacobi_weights(nx)]
    group = [lax.ppermute(loads, "gx", [(i, i ^ b) for i in range(nx)]) for b in (1, 2, 3)]
    *pieces, mom, upx, upy = call(
        weigh_kernel, "weigh", [loads, *group, upx, upy],
        [struct(32, LZ)] * (nx // 4) + [struct(nx // 4 * ny * 2, LZ), struct(vx, LZ), struct(vy, LZ)], table=table, ny=ny,
    )
    coarse = [pieces[0]] + [shifted(p, "gx", 4 * z) for z, p in enumerate(pieces) if z]
    alike = [[(4 * z + q) * ny + y for z in range(nx // 4) for y in range(ny)] for q in range(4)]
    got = lax.all_to_all(mom.reshape(-1, 2, LZ), ("gx", "gy"), 0, 0, tiled=True, axis_index_groups=alike).reshape(mom.shape)
    rx = shifted(upx, "gx", 1)
    ry = shifted(upy, "gy", 1)
    v2, p2 = (pltpu.with_memory_space_constraint(v, pltpu.HBM) for v in (v2, p2))
    sol, res, coarse = call(
        last_kernel, "last", [(prolong, SM), got, *coarse, inv, rhs2, v1, (v2, ANY), (p2, ANY), rx, ry],
        [pltpu.HBM((ROWS, LZ), f32)] * 2 + [struct(LY, LZ)],
        [pltpu.VMEM((ROWS, LZ), f32)] * 4 + [pltpu.SemaphoreType.DMA((6,))] * 2, ny=ny,
    )
    return sol.reshape(rhs.shape), res.reshape(rhs.shape), coarse[None]


def solution(mesh):
    placed = (
        P(None, None, "gx", "gy", None),
        P("gx", "gy", None),
        P("gx", "gy", None),
        P(),
        P(),
        P(),
    )
    return jax.shard_map(
        shards,
        mesh=mesh,
        in_specs=placed,
        out_specs=(
            P(None, None, "gx", "gy", None),
            P(None, None, "gx", "gy", None),
            P("gx", "gy", None),
        ),
        check_vma=False,
    )
```

```python
import jax
import jax.numpy as jnp
import numpy as np
from jax import lax
from jax.experimental import pallas as pl
from jax.experimental.pallas import tpu as pltpu
from jax.sharding import PartitionSpec as P

ITERS = 3
SWEEPS = 8
F, A = 3, 25
B = 24
LAST = 6 * B
OUT, IN = LAST + 8, LAST + 16
LX, LY, LZ = 4, 8, 128
CELLS = LX * LY
FACE = A * CELLS
ROWS = F * FACE
PIECE = 72
f32, bf16 = jnp.float32, jnp.bfloat16
VM = pl.BlockSpec(memory_space=pltpu.VMEM)
SM = pl.BlockSpec(memory_space=pltpu.SMEM)
ANY = pl.BlockSpec(memory_space=pl.ANY)


def shifted(value, axis, by):
    n = lax.axis_size(axis)
    return lax.ppermute(value, axis, [(i, (i + by) % n) for i in range(n)])


def near_swap(value, axis):
    n = lax.axis_size(axis)
    return lax.ppermute(value, axis, [(i, i ^ 1) for i in range(n)])


def far_swap(value, axis):
    n = lax.axis_size(axis)
    pairs = [(i, (i + 1) % n) if i % 2 else (i, (i - 1) % n) for i in range(n)]
    return lax.ppermute(value, axis, pairs)


def halves(v):
    hi = v.astype(bf16)
    lo = (v - hi.astype(f32)).astype(bf16)
    return hi, lo


def apply_operator(v_ref, ux_ref, uy_ref, k_ref, m_ref, w_ref, out_ref, up_x, low_x, up_y, low_y, last_in, last_out, layer_done=None):
    w_all = w_ref[...]
    at_first = lax.broadcasted_iota(jnp.int32, (LY, LZ), 0) == 0
    last_in[LAST // B * LY :] = jnp.zeros((2 * LY, LZ), f32)

    def face(f, x, y):
        if f == 0 and x == LX:
            return ux_ref[pl.ds(y, B, stride=LY), :]
        if f == 1 and y == LY:
            return uy_ref[pl.ds(x, B, stride=LX), :]
        return v_ref[pl.ds(f * FACE + x * LY + y, B, stride=CELLS), :]

    def last_rows(f, x):
        if x == LX:
            return ux_ref[B * LY :, :]
        at = f * FACE + B * CELLS + x * LY
        return v_ref[at : at + LY, :]

    def put(f, x, y, value):
        out_ref[pl.ds(f * FACE + x * LY + y, B, stride=CELLS), :] = value

    def put_last(f, x, value):
        at = f * FACE + B * CELLS + x * LY
        out_ref[at : at + LY, :] = value

    filler = jnp.zeros((IN - OUT, LZ), f32)
    carry = last_carry = None
    for x in range(LX):
        z_last = last_rows(2, x)
        y_last = last_rows(1, x)
        above = uy_ref[B * LX + x : B * LX + x + 1, :]
        top = lax.broadcasted_iota(jnp.int32, (LY, LZ), 0) == LY - 1
        y_up = jnp.where(top, jnp.broadcast_to(above, (LY, LZ)), pltpu.roll(y_last, LY - 1, 0))
        for j, tile in enumerate((last_rows(0, x), y_last, z_last, last_rows(0, x + 1), y_up, pltpu.roll(z_last, LZ - 1, 1))):
            last_in[j * LY : (j + 1) * LY] = tile
        columns = []
        for y in range(LY):
            z = face(2, x, y)
            six = [face(0, x, y), face(0, x + 1, y), face(1, x, y), face(1, x, y + 1), z, pltpu.roll(z, LZ - 1, 1)]
            columns.append(jnp.concatenate(six + [last_in[pl.ds(y, 8, stride=LY), :], filler], 0))
        hi, lo = halves(jnp.concatenate(columns, 1))
        prod = jnp.dot(w_all, jnp.concatenate([hi, lo, hi], 0), preferred_element_type=f32)
        parts = []
        for y in range(LY):
            k = k_ref[x * LY + y : x * LY + y + 1, :]
            m = m_ref[x * LY + y : x * LY + y + 1, :]
            cols = slice(y * LZ, (y + 1) * LZ)
            w = prod[:OUT, cols] * k + prod[OUT:, cols] * m
            parts.append([w[b * B : (b + 1) * B] for b in range(6)])
            last_out[pl.ds(y, 8, stride=LY), :] = w[LAST:]
        for y in range(LY):
            wlx, wux, wly, wuy, wlz, wuz = parts[y]
            put(0, x, y, wlx if x == 0 else wlx + carry[y])
            put(1, x, y, wly if y == 0 else wly + parts[y - 1][3])
            put(2, x, y, wlz + pltpu.roll(wuz, 1, 1))
            if x == 0 and low_x is not None:
                low_x[pl.ds(y, B, stride=LY), :] = wlx
            if x == LX - 1:
                up_x[pl.ds(y, B, stride=LY), :] = wux
        tiles = [last_out[j * LY : (j + 1) * LY] for j in range(6)]
        put_last(0, x, tiles[0] if x == 0 else tiles[0] + last_carry)
        put_last(1, x, tiles[1] + jnp.where(at_first, 0.0, pltpu.roll(tiles[4], 1, 0)))
        put_last(2, x, tiles[2] + pltpu.roll(tiles[5], 1, 1))
        if x == 0 and low_x is not None:
            low_x[B * LY :] = tiles[0]
        if x == LX - 1:
            up_x[B * LY :] = tiles[3]
        if low_y is not None:
            low_y[pl.ds(x, B, stride=LX), :] = parts[0][2]
            low_y[B * LX + x : B * LX + x + 1] = tiles[1][:1]
        up_y[pl.ds(x, B, stride=LX), :] = parts[LY - 1][3]
        up_y[B * LX + x : B * LX + x + 1] = tiles[4][LY - 1 :]
        carry = [parts[y][1] for y in range(LY)]
        last_carry = tiles[3]
        if layer_done is not None:
            layer_done(x)


def is_even(axis):
    return lax.rem(lax.axis_index(axis), 2) == 0


def route(even, up, low, near, far):
    near[...] = jnp.where(even, up[...], low[...])
    far[...] = jnp.where(even, low[...], up[...])


def edge_kernel(rhs_ref, fx_ref, fy_ref, sem_x, sem_y):
    face_x = pltpu.make_async_copy(rhs_ref.at[0, :, 0], fx_ref, sem_x)
    face_y = pltpu.make_async_copy(rhs_ref.at[1, :, :, 0], fy_ref, sem_y)
    face_x.start()
    face_y.start()
    face_x.wait()
    face_y.wait()


def weight_kernel(s_ref, m_ref, w_ref, inv_ref):
    n = 6 * A

    def placing(rows, span):
        r = lax.broadcasted_iota(jnp.int32, (rows, n), 0)
        c = lax.broadcasted_iota(jnp.int32, (rows, n), 1)
        p = lax.rem(r, span)
        j = p - LAST
        node = jnp.where(p < LAST, lax.div(p, B) * A + lax.rem(p, B), (2 * lax.rem(j, 3) + lax.div(j, 3)) * A + B)
        return (node == c) & (p < n), lax.div(r, span)

    def ones(mask):
        return jnp.where(mask, 1.0, 0.0).astype(bf16)

    rows = ones(placing(OUT, OUT)[0])
    mask, third = placing(3 * IN, IN)
    columns = (ones(mask & (third < 2)), ones(mask & (third == 2)))
    diagonal = lax.broadcasted_iota(jnp.int32, (n, n), 0) == lax.broadcasted_iota(jnp.int32, (n, n), 1)

    def largest(v):
        return jnp.max(jnp.max(jnp.where(diagonal, v, 0.0), 0, keepdims=True), 1, keepdims=True)

    inv = 1.0 / (10.0 * largest(s_ref[...]) + 2.0 * largest(m_ref[...]))
    inv_ref[...] = jnp.broadcast_to(inv, (8, LZ))
    for i, ref in enumerate((s_ref, m_ref)):
        full = 0.0
        for part, place in zip(halves(ref[...] * inv), columns):
            moved = jnp.dot(rows, part, preferred_element_type=f32).astype(bf16)
            full = full + lax.dot_general(moved, place, (((1,), (1,)), ((), ())), preferred_element_type=f32)
        w_ref[i * OUT : (i + 1) * OUT] = full.astype(bf16)


def first_kernel(rhs_ref, hx_ref, hy_ref, k_ref, m_ref, w_ref,
                 p_ref, snx, sfx, sny, sfy, last_in, last_out, upx, lowx, upy, lowy):
    apply_operator(rhs_ref, hx_ref, hy_ref, k_ref, m_ref, w_ref, p_ref, upx, lowx, upy, lowy, last_in, last_out)
    route(is_even("gx"), upx, lowx, snx, sfx)
    route(is_even("gy"), upy, lowy, sny, sfy)


def assemble(p_ref, snx, sfx, sny, sfy, rnx, rfx, rny, rfy, v, ux, uy):
    even_x = is_even("gx")
    even_y = is_even("gy")
    v[...] = p_ref[...]
    below_x = jnp.where(even_x, rfx[...], rnx[...])
    for a in range(A):
        rows = slice(a * CELLS, a * CELLS + LY)
        v[rows, :] = v[rows, :] + below_x[a * LY : (a + 1) * LY]
    below_y = jnp.where(even_y, rfy[...], rny[...])
    first = pl.ds(FACE, A * LX, stride=LY)
    v[first, :] = v[first, :] + below_y
    ux[...] = jnp.where(even_x, snx[...] + rnx[...], sfx[...] + rfx[...])
    uy[...] = jnp.where(even_y, sny[...] + rny[...], sfy[...] + rfy[...])


def node_sum(value):
    return jnp.sum(value.reshape(-1, LY, LZ), 0)


def row(tile):
    return jnp.sum(tile, 0, keepdims=True)


def second_kernel(p_ref, rfx, rfy, rny, rnx, snx, sfx, sny, sfy, k_ref, m_ref, w_ref,
                  v1_ref, p1_ref, tnx, tfx, tny, tfy, ux, uy, last_in, last_out, upx, lowx, upy, lowy):
    assemble(p_ref, snx, sfx, sny, sfy, rnx, rfx, rny, rfy, v1_ref, ux, uy)
    apply_operator(v1_ref, ux, uy, k_ref, m_ref, w_ref, p1_ref, upx, lowx, upy, lowy, last_in, last_out)
    route(is_even("gx"), upx, lowx, tnx, tfx)
    route(is_even("gy"), upy, lowy, tny, tfy)


def products_kernel(v0_ref, v1_ref, sums_ref):
    v0 = v0_ref[...]
    v1 = v1_ref[...]
    sums_ref[0:8] = node_sum(v0)
    sums_ref[8:16] = node_sum(v1)
    sums_ref[16:24] = node_sum(v0 * v0)
    sums_ref[24:32] = node_sum(v0 * v1)
    sums_ref[32:40] = node_sum(v1 * v1)


def third_kernel(p_ref, v1_ref, rfx, rfy, rny, rnx, snx, sfx, sny, sfy, sums_ref, k_ref, m_ref, w_ref,
                 v2_out, p2_out, upx, upy, loads_ref, v2_ref, p2_ref, ux, uy, last_in, last_out, v2_sem, p2_sem):
    assemble(p_ref, snx, sfx, sny, sfy, rnx, rfx, rny, rfy, v2_ref, ux, uy)
    v2_copy = pltpu.make_async_copy(v2_ref, v2_out, v2_sem)
    v2_copy.start()
    v1 = v1_ref[...]
    v2 = v2_ref[...]
    loads_ref[0:16] = sums_ref[0:16]
    loads_ref[16:24] = node_sum(v2)
    m3 = node_sum(v1 * v2)
    m4 = node_sum(v2 * v2)
    p2_copies = [
        pltpu.make_async_copy(p2_ref.reshape(F * A, LX, LY, LZ).at[:, x], p2_out.at[:, x], p2_sem.at[x]) for x in range(LX)
    ]

    def layer_done(x):
        p2_copies[x].start()

    apply_operator(v2_ref, ux, uy, k_ref, m_ref, w_ref, p2_ref, upx, None, upy, None, last_in, last_out, layer_done)
    p2 = p2_ref[...]
    above = upx[...]
    loads_ref[24:32] = node_sum(p2)
    loads_ref[32:40] = node_sum(above)
    energy = node_sum(v2_ref[...] * p2) + node_sum(ux[...] * above)
    tail = row(uy[...] * upy[...])
    for k in range(3):
        loads_ref[40 + k : 41 + k] = row(sums_ref[16 + 8 * k : 24 + 8 * k])
    loads_ref[43:44] = row(m3)
    loads_ref[44:45] = row(m4)
    loads_ref[45:46] = row(energy) + tail
    loads_ref[46:47] = row(upy[...])
    loads_ref[47:48] = jnp.zeros((1, LZ), f32)
    v2_copy.wait()
    for copy in p2_copies:
        copy.wait()


def weigh_kernel(own, near, far, both, *outs, table, ny):
    *outs, mom_ref = outs
    nx = len(table)
    me = lax.axis_index("gx")
    q = lax.rem(me, 4)
    low, high = lax.rem(q, 2) == 0, q < 2
    one, two = jnp.where(low, 1, -1), jnp.where(high, 2, -2)
    sources = ((own, 0, (0,)), (near, one, (1, -1)), (far, two, (2, -2)), (both, one + two, (3, 1, -1, -3)))

    def pick(at, shift, span):
        value = jnp.float32(table[(at - span[0]) % nx])
        for s in span[1:]:
            value = jnp.where(shift == s, table[(at - s) % nx], value)
        return value

    tile = own[40:48] + near[40:48] + far[40:48] + both[40:48]
    for lanes in (64, 32, 16):
        tile = tile + pltpu.roll(tile, lanes, 1)
    lane = lax.broadcasted_iota(jnp.int32, (8, LZ), 1)
    moment = lax.broadcasted_iota(jnp.int32, (8, LZ), 0)
    packed = row(jnp.where((lax.div(lane, 16) == moment) & (moment < 6), tile, 0.0))
    groups = nx // 4
    for z, out in enumerate(outs):
        total = [0.0] * 4
        edge = 0.0
        for ref, shift, span in sources:
            w = pick(4 * z, shift, span)
            for k in range(4):
                total[k] = total[k] + ref[k * 8 : k * 8 + 8] * w
            total[3] = total[3] + ref[32:40] * pick(4 * z - 1, shift, span)
            edge = edge + ref[46:47] * w
        for k in range(4):
            out[k * 8 : k * 8 + 8] = total[k]
        out[32:] = jnp.zeros((out.shape[0] - 32, LZ), f32)
        pair = jnp.concatenate([packed, edge] * 4, 0)
        first = lax.rem(lax.div(me, 4) + z, groups) * (2 * ny)
        for at in range(0, 2 * ny, 8):
            mom_ref[pl.ds(pl.multiple_of(first + at, 8), 8), :] = pair


def two_sum(a, b):
    s = a + b
    t = s - a
    return s, (a - (s - t)) + (b - t)


def pair_add(a, b):
    s, e = two_sum(a[0], b[0])
    e = e + (a[1] + b[1])
    h = s + e
    return h, e - (h - s)


def split(a):
    t = a * 4097.0
    h = t - (t - a)
    return h, a - h


def pair_times(a, c):
    p = a[0] * c
    ah, al = split(a[0])
    ch, cl = split(c)
    return p, ((ah * ch - p) + ah * cl + al * ch) + al * cl + a[1] * c


def moments(got):
    zero = jnp.zeros((8, LZ), f32)
    pairs = [(got[at : at + 8], zero) for at in range(0, got.shape[0], 8)]
    while len(pairs) > 1:
        pairs = [pair_add(a, b) for a, b in zip(pairs[::2], pairs[1::2])]
    h, l = pairs[0]
    rows = [(h[r : r + 1], l[r : r + 1]) for r in (0, 2, 4, 6)]
    t = pair_add(pair_add(rows[0], rows[1]), pair_add(rows[2], rows[3]))
    level = [t] + [tuple(pltpu.roll(p, LZ - 16 * k, 1) for p in t) for k in range(1, 6)]
    inside = lax.broadcasted_iota(jnp.int32, (1, LZ), 1) < 16

    def total(value):
        return jnp.sum(jnp.where(inside, value, 0.0), axis=1, keepdims=True)

    c = total(level[1][0]) / total(level[0][0])
    minus = jnp.broadcast_to(-c, (1, LZ))
    heads = [level[0]]
    while len(level) > 1:
        level = [pair_add(up, pair_times(at, minus)) for at, up in zip(level, level[1:])]
        heads.append(level[0])
    return c, [total(p[0] + p[1]) for p in heads]


def conjugate_gradient(c, m):
    def dot(a, b):
        s = None
        for i, ai in enumerate(a):
            for j, bj in enumerate(b):
                t = ai * bj * m[i + j]
                s = t if s is None else s + t
        return s

    def add(a, b, factor):
        longer = []
        for i in range(max(len(a), len(b))):
            if i >= len(b):
                longer.append(a[i])
            elif i >= len(a):
                longer.append(factor * b[i])
            else:
                longer.append(a[i] + factor * b[i])
        return longer

    def times(a, shift):
        return [a[0] * shift] + [a[i] * shift + a[i - 1] for i in range(1, len(a))] + [a[-1]]

    def plain(a):
        out = [a[-1]]
        for coefficient in a[-2::-1]:
            out = times(out, -c)
            out[0] = out[0] + coefficient
        return out

    one = jnp.ones((1, 1), f32)
    iterate, residual, direction = [], [one], [one]
    norm = m[0]
    for step in range(ITERS):
        img = times(direction, c)
        alpha = norm / dot(direction, img)
        iterate = add(iterate, direction, alpha)
        residual = add(residual, img, -alpha)
        if step < ITERS - 1:
            norm_next = dot(residual, residual)
            direction = add(residual, direction, norm_next / norm)
            norm = norm_next
    return plain(iterate), plain(residual)


def last_kernel(prolong_ref, got_ref, c0, c1, c2, c3, inv_ref, rhs_ref, v1_ref, v2_hbm, p2_hbm, rx_ref, ry_ref,
                sol_hbm, res_hbm, coarse_ref, v2_ref, p2_ref, sol_ref, res_ref, in_sems, out_sems, *, ny):
    fetches = []
    for f in range(F):
        rows = pl.ds(f * FACE, FACE)
        for i, (src, dst) in enumerate(((v2_hbm, v2_ref), (p2_hbm, p2_ref))):
            fetches.append(pltpu.make_async_copy(src.at[rows], dst.at[rows], in_sems.at[2 * f + i]))
            fetches[-1].start()
    x, d = conjugate_gradient(*moments(got_ref[...]))
    inv = inv_ref[0:1, 0:1]
    x = [t * inv for t in x]
    below = lax.rem(lax.axis_index("gy") + ny - 1, ny)
    edge = jnp.zeros((1, LZ), f32)
    for z in range(got_ref.shape[0] // (2 * ny)):
        edge = edge + got_ref[pl.ds(2 * (z * ny + below) + 1, 1), :]
    circ = [c0[k * 8 : k * 8 + 8] + c1[k * 8 : k * 8 + 8] + c2[k * 8 : k * 8 + 8] + c3[k * 8 : k * 8 + 8] for k in range(4)]
    at_first = lax.broadcasted_iota(jnp.int32, (LY, LZ), 0) == 0
    circ[3] = circ[3] + jnp.where(at_first, jnp.broadcast_to(edge, (LY, LZ)), 0.0)
    coarse = d[0] * circ[0] + d[1] * circ[1] + d[2] * circ[2] + d[3] * circ[3]
    coarse_ref[...] = coarse
    x = [jnp.broadcast_to(t, (LY, LZ)) for t in x]
    d = [jnp.broadcast_to(t, (LY, LZ)) for t in d]
    stores = []
    for f in range(F):
        fetches[2 * f].wait()
        fetches[2 * f + 1].wait()
        for a in range(A):
            at = (f * A + a) * CELLS
            spread = coarse * prolong_ref[f, a]
            for cell in range(LX):
                rows = slice(at + cell * LY, at + (cell + 1) * LY)
                v0, v1, v2 = rhs_ref[rows, :], v1_ref[rows, :], v2_ref[rows, :]
                img = p2_ref[rows, :]
                if f == 0 and cell == 0:
                    img = img + rx_ref[a * LY : (a + 1) * LY, :]
                sol_ref[rows, :] = x[0] * v0 + x[1] * v1 + x[2] * v2 + spread
                res_ref[rows, :] = d[0] * v0 + d[1] * v1 + d[2] * v2 + d[3] * img
        if f == 1:
            first = pl.ds(FACE, A * LX, stride=LY)
            res_ref[first, :] = res_ref[first, :] + d[3][0:1] * ry_ref[...]
        rows = pl.ds(f * FACE, FACE)
        for i, (src, dst) in enumerate(((sol_ref, sol_hbm), (res_ref, res_hbm))):
            stores.append(pltpu.make_async_copy(src.at[rows], dst.at[rows], out_sems.at[2 * f + i]))
            stores[-1].start()
    for store in stores:
        store.wait()


def jacobi_weights(n):
    coarse = np.zeros(n)
    load = np.zeros(n)
    load[0] = 1.0
    for _ in range(SWEEPS):
        coarse = (load + np.roll(coarse, 1) + np.roll(coarse, -1)) / 2.2
    return coarse / 75.0


def struct(*shape):
    return jax.ShapeDtypeStruct(shape, f32)


PARAMS = pltpu.CompilerParams(vmem_limit_bytes=16 * 1024 * 1024)


def shards(rhs, kappa, mass, stiffness, mass_matrix, prolong):
    nx, ny = lax.axis_size("gx"), lax.axis_size("gy")
    vx, vy = A * LY, A * LX
    rhs2 = rhs.reshape(ROWS, LZ)
    k2 = kappa.reshape(CELLS, LZ)
    m2 = mass.reshape(CELLS, LZ)
    sends = [struct(vx, LZ), struct(vx, LZ), struct(vy, LZ), struct(vy, LZ)]
    upper = [pltpu.VMEM((vx, LZ), f32), pltpu.VMEM((vy, LZ), f32)] + [pltpu.VMEM((8 * LY, LZ), f32)] * 2
    edges = [pltpu.VMEM((vx, LZ), f32)] * 2 + [pltpu.VMEM((vy, LZ), f32)] * 2

    def call(kernel, name, ins, outs, scratch=(), **static):
        specs = [i[1] if isinstance(i, tuple) else VM for i in ins]
        ins = [i[0] if isinstance(i, tuple) else i for i in ins]

        def bound(*refs):
            kernel(*refs, **static)

        return pl.pallas_call(
            bound,
            out_shape=outs,
            in_specs=specs,
            out_specs=[ANY if isinstance(o, pl.MemoryRef) else VM for o in outs],
            scratch_shapes=list(scratch),
            compiler_params=PARAMS,
            name=name,
        )(*ins)

    def swap(s):
        far_x = far_swap(s[1], "gx")
        far_y = far_swap(s[3], "gy")
        near_y = near_swap(s[2], "gy")
        near_x = near_swap(s[0], "gx")
        return [far_x, far_y, near_y, near_x]

    hbm = pltpu.with_memory_space_constraint(rhs, pltpu.HBM)
    fx, fy = call(
        edge_kernel, "edges", [(hbm, ANY)], [struct(A, LY, LZ), struct(A, LX, LZ)],
        [pltpu.SemaphoreType.DMA, pltpu.SemaphoreType.DMA],
    )
    hx = shifted(fx.reshape(vx, LZ), "gx", -1)
    hy = shifted(fy.reshape(vy, LZ), "gy", -1)
    w, inv = call(
        weight_kernel, "weights", [stiffness, mass_matrix],
        [jax.ShapeDtypeStruct((2 * OUT, 3 * IN), bf16), struct(8, LZ)],
    )

    p0, *s = call(
        first_kernel, "first", [rhs2, hx, hy, k2, m2, w], [struct(ROWS, LZ)] + sends, upper[2:] + edges,
    )
    r = swap(s)
    v1, p1, *s = call(
        second_kernel, "second", [p0, *r, *s, k2, m2, w],
        [struct(ROWS, LZ), struct(ROWS, LZ)] + sends, upper + edges,
    )
    r = swap(s)
    sums, = call(products_kernel, "products", [rhs2, v1], [struct(40, LZ)])
    dma = pltpu.SemaphoreType.DMA
    v2, p2, upx, upy, loads = call(
        third_kernel, "third", [p1, v1, *r, *s, sums, k2, m2, w],
        [pltpu.HBM((ROWS, LZ), f32), pltpu.HBM((F * A, LX, LY, LZ), f32), struct(vx, LZ), struct(vy, LZ), struct(48, LZ)],
        [pltpu.VMEM((ROWS, LZ), f32)] * 2 + upper + [dma, pltpu.SemaphoreType.DMA((LX,))],
    )
    table = [float(t) for t in jacobi_weights(nx)]
    group = [lax.ppermute(loads, "gx", [(i, i ^ b) for i in range(nx)]) for b in (1, 2, 3)]
    *pieces, mom = call(
        weigh_kernel, "weigh", [loads, *group],
        [struct(PIECE, LZ)] * (nx // 4) + [struct(nx // 4 * ny * 2, LZ)], table=table, ny=ny,
    )
    coarse = [pieces[0]] + [shifted(p, "gx", 4 * z) for z, p in enumerate(pieces) if z]
    alike = [[(4 * z + q) * ny + y for z in range(nx // 4) for y in range(ny)] for q in range(4)]
    got = lax.all_to_all(mom.reshape(-1, 2, LZ), ("gx", "gy"), 0, 0, tiled=True, axis_index_groups=alike).reshape(mom.shape)
    rx = shifted(upx, "gx", 1)
    ry = shifted(upy, "gy", 1)
    v2, p2 = (pltpu.with_memory_space_constraint(v, pltpu.HBM) for v in (v2, p2.reshape(ROWS, LZ)))
    sol, res, coarse = call(
        last_kernel, "last", [(prolong, SM), got, *coarse, inv, rhs2, v1, (v2, ANY), (p2, ANY), rx, ry],
        [pltpu.HBM((ROWS, LZ), f32)] * 2 + [struct(LY, LZ)],
        [pltpu.VMEM((ROWS, LZ), f32)] * 4 + [pltpu.SemaphoreType.DMA((6,))] * 2, ny=ny,
    )
    return sol.reshape(rhs.shape), res.reshape(rhs.shape), coarse[None]


def solution(mesh):
    placed = (
        P(None, None, "gx", "gy", None),
        P("gx", "gy", None),
        P("gx", "gy", None),
        P(),
        P(),
        P(),
    )
    return jax.shard_map(
        shards,
        mesh=mesh,
        in_specs=placed,
        out_specs=(
            P(None, None, "gx", "gy", None),
            P(None, None, "gx", "gy", None),
            P("gx", "gy", None),
        ),
        check_vma=False,
    )
```

```python
import jax
import jax.numpy as jnp
import numpy as np
from jax import lax
from jax.experimental import pallas as pl
from jax.experimental.pallas import tpu as pltpu
from jax.sharding import PartitionSpec as P

ITERS = 3
SWEEPS = 8
F, A = 3, 25
B = 24
LAST = 6 * B
OUT, IN = LAST + 8, LAST + 16
LX, LY, LZ = 4, 8, 128
CELLS = LX * LY
FACE = A * CELLS
ROWS = F * FACE
f32, bf16 = jnp.float32, jnp.bfloat16
VM = pl.BlockSpec(memory_space=pltpu.VMEM)
SM = pl.BlockSpec(memory_space=pltpu.SMEM)
ANY = pl.BlockSpec(memory_space=pl.ANY)


def shifted(value, axis, by):
    n = lax.axis_size(axis)
    return lax.ppermute(value, axis, [(i, (i + by) % n) for i in range(n)])


def near_swap(value, axis):
    n = lax.axis_size(axis)
    return lax.ppermute(value, axis, [(i, i ^ 1) for i in range(n)])


def far_swap(value, axis):
    n = lax.axis_size(axis)
    pairs = [(i, (i + 1) % n) if i % 2 else (i, (i - 1) % n) for i in range(n)]
    return lax.ppermute(value, axis, pairs)


def halves(v):
    hi = v.astype(bf16)
    lo = (v - hi.astype(f32)).astype(bf16)
    return hi, lo


def apply_operator(v_ref, ux_ref, uy_ref, k_ref, m_ref, w_ref, out_ref, up_x, low_x, up_y, low_y, last_in, last_out, layer_done=None):
    w_all = w_ref[...]
    at_first = lax.broadcasted_iota(jnp.int32, (LY, LZ), 0) == 0
    last_in[LAST // B * LY :] = jnp.zeros((2 * LY, LZ), f32)

    def face(f, x, y):
        if f == 0 and x == LX:
            return ux_ref[pl.ds(y, B, stride=LY), :]
        if f == 1 and y == LY:
            return uy_ref[pl.ds(x, B, stride=LX), :]
        return v_ref[pl.ds(f * FACE + x * LY + y, B, stride=CELLS), :]

    def last_rows(f, x):
        if x == LX:
            return ux_ref[B * LY :, :]
        at = f * FACE + B * CELLS + x * LY
        return v_ref[at : at + LY, :]

    def put(f, x, y, value):
        out_ref[pl.ds(f * FACE + x * LY + y, B, stride=CELLS), :] = value

    def put_last(f, x, value):
        at = f * FACE + B * CELLS + x * LY
        out_ref[at : at + LY, :] = value

    filler = jnp.zeros((IN - OUT, LZ), f32)
    carry = last_carry = None
    for x in range(LX):
        z_last = last_rows(2, x)
        y_last = last_rows(1, x)
        above = uy_ref[B * LX + x : B * LX + x + 1, :]
        top = lax.broadcasted_iota(jnp.int32, (LY, LZ), 0) == LY - 1
        y_up = jnp.where(top, jnp.broadcast_to(above, (LY, LZ)), pltpu.roll(y_last, LY - 1, 0))
        for j, tile in enumerate((last_rows(0, x), y_last, z_last, last_rows(0, x + 1), y_up, pltpu.roll(z_last, LZ - 1, 1))):
            last_in[j * LY : (j + 1) * LY] = tile
        columns = []
        for y in range(LY):
            z = face(2, x, y)
            six = [face(0, x, y), face(0, x + 1, y), face(1, x, y), face(1, x, y + 1), z, pltpu.roll(z, LZ - 1, 1)]
            columns.append(jnp.concatenate(six + [last_in[pl.ds(y, 8, stride=LY), :], filler], 0))
        hi, lo = halves(jnp.concatenate(columns, 1))
        prod = jnp.dot(w_all, jnp.concatenate([hi, lo, hi], 0), preferred_element_type=f32)
        parts = []
        for y in range(LY):
            k = k_ref[x * LY + y : x * LY + y + 1, :]
            m = m_ref[x * LY + y : x * LY + y + 1, :]
            cols = slice(y * LZ, (y + 1) * LZ)
            w = prod[:OUT, cols] * k + prod[OUT:, cols] * m
            parts.append([w[b * B : (b + 1) * B] for b in range(6)])
            last_out[pl.ds(y, 8, stride=LY), :] = w[LAST:]
        for y in range(LY):
            wlx, wux, wly, wuy, wlz, wuz = parts[y]
            put(0, x, y, wlx if x == 0 else wlx + carry[y])
            put(1, x, y, wly if y == 0 else wly + parts[y - 1][3])
            put(2, x, y, wlz + pltpu.roll(wuz, 1, 1))
            if x == 0 and low_x is not None:
                low_x[pl.ds(y, B, stride=LY), :] = wlx
            if x == LX - 1:
                up_x[pl.ds(y, B, stride=LY), :] = wux
        tiles = [last_out[j * LY : (j + 1) * LY] for j in range(6)]
        put_last(0, x, tiles[0] if x == 0 else tiles[0] + last_carry)
        put_last(1, x, tiles[1] + jnp.where(at_first, 0.0, pltpu.roll(tiles[4], 1, 0)))
        put_last(2, x, tiles[2] + pltpu.roll(tiles[5], 1, 1))
        if x == 0 and low_x is not None:
            low_x[B * LY :] = tiles[0]
        if x == LX - 1:
            up_x[B * LY :] = tiles[3]
        if low_y is not None:
            low_y[pl.ds(x, B, stride=LX), :] = parts[0][2]
            low_y[B * LX + x : B * LX + x + 1] = tiles[1][:1]
        up_y[pl.ds(x, B, stride=LX), :] = parts[LY - 1][3]
        up_y[B * LX + x : B * LX + x + 1] = tiles[4][LY - 1 :]
        carry = [parts[y][1] for y in range(LY)]
        last_carry = tiles[3]
        if layer_done is not None:
            layer_done(x)


def is_even(axis):
    return lax.rem(lax.axis_index(axis), 2) == 0


def route(even, up, low, near, far):
    near[...] = jnp.where(even, up[...], low[...])
    far[...] = jnp.where(even, low[...], up[...])


def edge_kernel(rhs_ref, fx_ref, fy_ref, sem_x, sem_y):
    face_x = pltpu.make_async_copy(rhs_ref.at[0, :, 0], fx_ref, sem_x)
    face_y = pltpu.make_async_copy(rhs_ref.at[1, :, :, 0], fy_ref, sem_y)
    face_x.start()
    face_y.start()
    face_x.wait()
    face_y.wait()


def weight_kernel(s_ref, m_ref, w_ref, inv_ref):
    n = 6 * A

    def placing(rows, span):
        r = lax.broadcasted_iota(jnp.int32, (rows, n), 0)
        c = lax.broadcasted_iota(jnp.int32, (rows, n), 1)
        p = lax.rem(r, span)
        j = p - LAST
        node = jnp.where(p < LAST, lax.div(p, B) * A + lax.rem(p, B), (2 * lax.rem(j, 3) + lax.div(j, 3)) * A + B)
        return (node == c) & (p < n), lax.div(r, span)

    def ones(mask):
        return jnp.where(mask, 1.0, 0.0).astype(bf16)

    rows = ones(placing(OUT, OUT)[0])
    mask, third = placing(3 * IN, IN)
    columns = (ones(mask & (third < 2)), ones(mask & (third == 2)))
    diagonal = lax.broadcasted_iota(jnp.int32, (n, n), 0) == lax.broadcasted_iota(jnp.int32, (n, n), 1)

    def largest(v):
        return jnp.max(jnp.max(jnp.where(diagonal, v, 0.0), 0, keepdims=True), 1, keepdims=True)

    inv = 1.0 / (10.0 * largest(s_ref[...]) + 2.0 * largest(m_ref[...]))
    inv_ref[...] = jnp.broadcast_to(inv, (8, LZ))
    for i, ref in enumerate((s_ref, m_ref)):
        full = 0.0
        for part, place in zip(halves(ref[...] * inv), columns):
            moved = jnp.dot(rows, part, preferred_element_type=f32).astype(bf16)
            full = full + lax.dot_general(moved, place, (((1,), (1,)), ((), ())), preferred_element_type=f32)
        w_ref[i * OUT : (i + 1) * OUT] = full.astype(bf16)


def first_kernel(rhs_ref, hx_ref, hy_ref, k_ref, m_ref, w_ref,
                 p_ref, snx, sfx, sny, sfy, last_in, last_out, upx, lowx, upy, lowy):
    apply_operator(rhs_ref, hx_ref, hy_ref, k_ref, m_ref, w_ref, p_ref, upx, lowx, upy, lowy, last_in, last_out)
    route(is_even("gx"), upx, lowx, snx, sfx)
    route(is_even("gy"), upy, lowy, sny, sfy)


def assemble(p_ref, snx, sfx, sny, sfy, rnx, rfx, rny, rfy, v, ux, uy):
    even_x = is_even("gx")
    even_y = is_even("gy")
    v[...] = p_ref[...]
    below_x = jnp.where(even_x, rfx[...], rnx[...])
    for a in range(A):
        rows = slice(a * CELLS, a * CELLS + LY)
        v[rows, :] = v[rows, :] + below_x[a * LY : (a + 1) * LY]
    below_y = jnp.where(even_y, rfy[...], rny[...])
    first = pl.ds(FACE, A * LX, stride=LY)
    v[first, :] = v[first, :] + below_y
    ux[...] = jnp.where(even_x, snx[...] + rnx[...], sfx[...] + rfx[...])
    uy[...] = jnp.where(even_y, sny[...] + rny[...], sfy[...] + rfy[...])


def node_sum(value):
    return jnp.sum(value.reshape(-1, LY, LZ), 0)


def row(tile):
    return jnp.sum(tile, 0, keepdims=True)


def second_kernel(p_ref, rfx, rfy, rny, rnx, snx, sfx, sny, sfy, k_ref, m_ref, w_ref,
                  v1_ref, p1_ref, tnx, tfx, tny, tfy, ux, uy, last_in, last_out, upx, lowx, upy, lowy):
    assemble(p_ref, snx, sfx, sny, sfy, rnx, rfx, rny, rfy, v1_ref, ux, uy)
    apply_operator(v1_ref, ux, uy, k_ref, m_ref, w_ref, p1_ref, upx, lowx, upy, lowy, last_in, last_out)
    route(is_even("gx"), upx, lowx, tnx, tfx)
    route(is_even("gy"), upy, lowy, tny, tfy)


def products_kernel(v0_ref, v1_ref, sums_ref):
    v0 = v0_ref[...]
    v1 = v1_ref[...]
    sums_ref[0:8] = node_sum(v0)
    sums_ref[8:16] = node_sum(v1)
    sums_ref[16:24] = node_sum(v0 * v0)
    sums_ref[24:32] = node_sum(v0 * v1)
    sums_ref[32:40] = node_sum(v1 * v1)


def third_kernel(p_ref, v1_ref, rfx, rfy, rny, rnx, snx, sfx, sny, sfy, sums_ref, k_ref, m_ref, w_ref,
                 v2_out, p2_out, upx, upy, loads_ref, mom_ref, v2_ref, p2_ref, ux, uy, last_in, last_out, v2_sem, p2_sem):
    assemble(p_ref, snx, sfx, sny, sfy, rnx, rfx, rny, rfy, v2_ref, ux, uy)
    v2_copy = pltpu.make_async_copy(v2_ref, v2_out, v2_sem)
    v2_copy.start()
    v1 = v1_ref[...]
    v2 = v2_ref[...]
    loads_ref[0:16] = sums_ref[0:16]
    loads_ref[16:24] = node_sum(v2)
    m3 = node_sum(v1 * v2)
    m4 = node_sum(v2 * v2)
    p2_copies = [
        pltpu.make_async_copy(p2_ref.reshape(F * A, LX, LY, LZ).at[:, x], p2_out.at[:, x], p2_sem.at[x]) for x in range(LX)
    ]

    def layer_done(x):
        p2_copies[x].start()

    apply_operator(v2_ref, ux, uy, k_ref, m_ref, w_ref, p2_ref, upx, None, upy, None, last_in, last_out, layer_done)
    p2 = p2_ref[...]
    above = upx[...]
    loads_ref[24:32] = node_sum(p2)
    loads_ref[32:40] = node_sum(above)
    energy = node_sum(v2_ref[...] * p2) + node_sum(ux[...] * above)
    tail = row(uy[...] * upy[...])
    tile = jnp.concatenate(
        [row(sums_ref[16 + 8 * k : 24 + 8 * k]) for k in range(3)]
        + [row(m3), row(m4), row(energy) + tail, jnp.zeros((2, LZ), f32)], 0,
    )
    for lanes in (64, 32, 16):
        tile = tile + pltpu.roll(tile, lanes, 1)
    lane = lax.broadcasted_iota(jnp.int32, (8, LZ), 1)
    moment = lax.broadcasted_iota(jnp.int32, (8, LZ), 0)
    packed = row(jnp.where(lax.div(lane, 16) == moment, tile, 0.0))
    pair = jnp.concatenate([packed, row(upy[...])] * 4, 0)
    for at in range(0, mom_ref.shape[0], 8):
        mom_ref[at : at + 8] = pair
    loads_ref[40:] = jnp.zeros((loads_ref.shape[0] - 40, LZ), f32)
    v2_copy.wait()
    for copy in p2_copies:
        copy.wait()


def weigh_kernel(own, near, far, both, *outs, table):
    nx = len(table)
    q = lax.rem(lax.axis_index("gx"), 4)
    low, high = lax.rem(q, 2) == 0, q < 2
    one, two = jnp.where(low, 1, -1), jnp.where(high, 2, -2)
    sources = ((own, 0, (0,)), (near, one, (1, -1)), (far, two, (2, -2)), (both, one + two, (3, 1, -1, -3)))

    def pick(at, shift, span):
        value = jnp.float32(table[(at - span[0]) % nx])
        for s in span[1:]:
            value = jnp.where(shift == s, table[(at - s) % nx], value)
        return value

    for z, out in enumerate(outs):
        total = [0.0] * 4
        for ref, shift, span in sources:
            w = pick(4 * z, shift, span)
            for k in range(4):
                total[k] = total[k] + ref[k * 8 : k * 8 + 8] * w
            total[3] = total[3] + ref[32:40] * pick(4 * z - 1, shift, span)
        for k in range(4):
            out[k * 8 : k * 8 + 8] = total[k]


def two_sum(a, b):
    s = a + b
    t = s - a
    return s, (a - (s - t)) + (b - t)


def pair_add(a, b):
    s, e = two_sum(a[0], b[0])
    e = e + (a[1] + b[1])
    h = s + e
    return h, e - (h - s)


def split(a):
    t = a * 4097.0
    h = t - (t - a)
    return h, a - h


def pair_times(a, c):
    p = a[0] * c
    ah, al = split(a[0])
    ch, cl = split(c)
    return p, ((ah * ch - p) + ah * cl + al * ch) + al * cl + a[1] * c


def moments(got):
    zero = jnp.zeros((8, LZ), f32)
    pairs = [(got[at : at + 8], zero) for at in range(0, got.shape[0], 8)]
    while len(pairs) > 1:
        pairs = [pair_add(a, b) for a, b in zip(pairs[::2], pairs[1::2])]
    h, l = pairs[0]
    rows = [(h[r : r + 1], l[r : r + 1]) for r in (0, 2, 4, 6)]
    t = pair_add(pair_add(rows[0], rows[1]), pair_add(rows[2], rows[3]))
    level = [t] + [tuple(pltpu.roll(p, LZ - 16 * k, 1) for p in t) for k in range(1, 6)]
    inside = lax.broadcasted_iota(jnp.int32, (1, LZ), 1) < 16

    def total(value):
        return jnp.sum(jnp.where(inside, value, 0.0), axis=1, keepdims=True)

    c = total(level[1][0]) / total(level[0][0])
    minus = jnp.broadcast_to(-c, (1, LZ))
    heads = [level[0]]
    while len(level) > 1:
        level = [pair_add(up, pair_times(at, minus)) for at, up in zip(level, level[1:])]
        heads.append(level[0])
    return c, [total(p[0] + p[1]) for p in heads]


def conjugate_gradient(c, m):
    def dot(a, b):
        s = None
        for i, ai in enumerate(a):
            for j, bj in enumerate(b):
                t = ai * bj * m[i + j]
                s = t if s is None else s + t
        return s

    def add(a, b, factor):
        longer = []
        for i in range(max(len(a), len(b))):
            if i >= len(b):
                longer.append(a[i])
            elif i >= len(a):
                longer.append(factor * b[i])
            else:
                longer.append(a[i] + factor * b[i])
        return longer

    def times(a, shift):
        return [a[0] * shift] + [a[i] * shift + a[i - 1] for i in range(1, len(a))] + [a[-1]]

    def plain(a):
        out = [a[-1]]
        for coefficient in a[-2::-1]:
            out = times(out, -c)
            out[0] = out[0] + coefficient
        return out

    one = jnp.ones((1, 1), f32)
    iterate, residual, direction = [], [one], [one]
    norm = m[0]
    for step in range(ITERS):
        img = times(direction, c)
        alpha = norm / dot(direction, img)
        iterate = add(iterate, direction, alpha)
        residual = add(residual, img, -alpha)
        if step < ITERS - 1:
            norm_next = dot(residual, residual)
            direction = add(residual, direction, norm_next / norm)
            norm = norm_next
    return plain(iterate), plain(residual)


def last_kernel(prolong_ref, got_ref, c0, c1, c2, c3, inv_ref, rhs_ref, v1_ref, v2_hbm, p2_hbm, rx_ref, ry_ref,
                sol_hbm, res_hbm, coarse_ref, v2_ref, p2_ref, sol_ref, res_ref, in_sems, out_sems, *, table, ny):
    fetches = []
    for f in range(F):
        rows = pl.ds(f * FACE, FACE)
        for i, (src, dst) in enumerate(((v2_hbm, v2_ref), (p2_hbm, p2_ref))):
            fetches.append(pltpu.make_async_copy(src.at[rows], dst.at[rows], in_sems.at[2 * f + i]))
            fetches[-1].start()
    x, d = conjugate_gradient(*moments(got_ref[...]))
    inv = inv_ref[0:1, 0:1]
    x = [t * inv for t in x]
    below = lax.rem(lax.axis_index("gy") + ny - 1, ny)
    me = lax.axis_index("gx")
    nx = len(table)
    edge = jnp.zeros((1, LZ), f32)
    for offset, weight in enumerate(table):
        slab = lax.rem(me + nx - offset, nx)
        edge = edge + got_ref[pl.ds(2 * (slab * ny + below) + 1, 1), :] * weight
    circ = [c0[k * 8 : k * 8 + 8] + c1[k * 8 : k * 8 + 8] + c2[k * 8 : k * 8 + 8] + c3[k * 8 : k * 8 + 8] for k in range(4)]
    at_first = lax.broadcasted_iota(jnp.int32, (LY, LZ), 0) == 0
    circ[3] = circ[3] + jnp.where(at_first, jnp.broadcast_to(edge, (LY, LZ)), 0.0)
    coarse = d[0] * circ[0] + d[1] * circ[1] + d[2] * circ[2] + d[3] * circ[3]
    coarse_ref[...] = coarse
    x = [jnp.broadcast_to(t, (LY, LZ)) for t in x]
    d = [jnp.broadcast_to(t, (LY, LZ)) for t in d]
    stores = []
    for f in range(F):
        fetches[2 * f].wait()
        fetches[2 * f + 1].wait()
        for a in range(A):
            at = (f * A + a) * CELLS
            spread = coarse * prolong_ref[f, a]
            for cell in range(LX):
                rows = slice(at + cell * LY, at + (cell + 1) * LY)
                v0, v1, v2 = rhs_ref[rows, :], v1_ref[rows, :], v2_ref[rows, :]
                img = p2_ref[rows, :]
                if f == 0 and cell == 0:
                    img = img + rx_ref[a * LY : (a + 1) * LY, :]
                sol_ref[rows, :] = x[0] * v0 + x[1] * v1 + x[2] * v2 + spread
                res_ref[rows, :] = d[0] * v0 + d[1] * v1 + d[2] * v2 + d[3] * img
        if f == 1:
            first = pl.ds(FACE, A * LX, stride=LY)
            res_ref[first, :] = res_ref[first, :] + d[3][0:1] * ry_ref[...]
        rows = pl.ds(f * FACE, FACE)
        for i, (src, dst) in enumerate(((sol_ref, sol_hbm), (res_ref, res_hbm))):
            stores.append(pltpu.make_async_copy(src.at[rows], dst.at[rows], out_sems.at[2 * f + i]))
            stores[-1].start()
    for store in stores:
        store.wait()


def jacobi_weights(n):
    coarse = np.zeros(n)
    load = np.zeros(n)
    load[0] = 1.0
    for _ in range(SWEEPS):
        coarse = (load + np.roll(coarse, 1) + np.roll(coarse, -1)) / 2.2
    return coarse / 75.0


def struct(*shape):
    return jax.ShapeDtypeStruct(shape, f32)


PARAMS = pltpu.CompilerParams(vmem_limit_bytes=16 * 1024 * 1024)


def shards(rhs, kappa, mass, stiffness, mass_matrix, prolong):
    nx, ny = lax.axis_size("gx"), lax.axis_size("gy")
    vx, vy = A * LY, A * LX
    rhs2 = rhs.reshape(ROWS, LZ)
    k2 = kappa.reshape(CELLS, LZ)
    m2 = mass.reshape(CELLS, LZ)
    sends = [struct(vx, LZ), struct(vx, LZ), struct(vy, LZ), struct(vy, LZ)]
    upper = [pltpu.VMEM((vx, LZ), f32), pltpu.VMEM((vy, LZ), f32)] + [pltpu.VMEM((8 * LY, LZ), f32)] * 2
    edges = [pltpu.VMEM((vx, LZ), f32)] * 2 + [pltpu.VMEM((vy, LZ), f32)] * 2

    def call(kernel, name, ins, outs, scratch=(), **static):
        specs = [i[1] if isinstance(i, tuple) else VM for i in ins]
        ins = [i[0] if isinstance(i, tuple) else i for i in ins]

        def bound(*refs):
            kernel(*refs, **static)

        return pl.pallas_call(
            bound,
            out_shape=outs,
            in_specs=specs,
            out_specs=[ANY if isinstance(o, pl.MemoryRef) else VM for o in outs],
            scratch_shapes=list(scratch),
            compiler_params=PARAMS,
            name=name,
        )(*ins)

    def swap(s):
        far_x = far_swap(s[1], "gx")
        far_y = far_swap(s[3], "gy")
        near_y = near_swap(s[2], "gy")
        near_x = near_swap(s[0], "gx")
        return [far_x, far_y, near_y, near_x]

    hbm = pltpu.with_memory_space_constraint(rhs, pltpu.HBM)
    fx, fy = call(
        edge_kernel, "edges", [(hbm, ANY)], [struct(A, LY, LZ), struct(A, LX, LZ)],
        [pltpu.SemaphoreType.DMA, pltpu.SemaphoreType.DMA],
    )
    hx = shifted(fx.reshape(vx, LZ), "gx", -1)
    hy = shifted(fy.reshape(vy, LZ), "gy", -1)
    w, inv = call(
        weight_kernel, "weights", [stiffness, mass_matrix],
        [jax.ShapeDtypeStruct((2 * OUT, 3 * IN), bf16), struct(8, LZ)],
    )

    p0, *s = call(
        first_kernel, "first", [rhs2, hx, hy, k2, m2, w], [struct(ROWS, LZ)] + sends, upper[2:] + edges,
    )
    r = swap(s)
    v1, p1, *s = call(
        second_kernel, "second", [p0, *r, *s, k2, m2, w],
        [struct(ROWS, LZ), struct(ROWS, LZ)] + sends, upper + edges,
    )
    r = swap(s)
    sums, = call(products_kernel, "products", [rhs2, v1], [struct(40, LZ)])
    dma = pltpu.SemaphoreType.DMA
    peers = nx * ny * 2
    v2, p2, upx, upy, loads, mom = call(
        third_kernel, "third", [p1, v1, *r, *s, sums, k2, m2, w],
        [pltpu.HBM((ROWS, LZ), f32), pltpu.HBM((F * A, LX, LY, LZ), f32), struct(vx, LZ), struct(vy, LZ)]
        + [struct(peers + 8, LZ), struct(peers, LZ)],
        [pltpu.VMEM((ROWS, LZ), f32)] * 2 + upper + [dma, pltpu.SemaphoreType.DMA((LX,))],
    )
    table = [float(t) for t in jacobi_weights(nx)]
    group = [lax.ppermute(loads, "gx", [(i, i ^ b) for i in range(nx)]) for b in (1, 2, 3)]
    pieces = call(weigh_kernel, "weigh", [loads, *group], [struct(32, LZ)] * (nx // 4), table=table)
    coarse = [pieces[0]] + [shifted(p, "gx", 4 * z) for z, p in enumerate(pieces) if z]
    got = lax.all_to_all(mom.reshape(-1, 2, LZ), ("gx", "gy"), 0, 0, tiled=True).reshape(mom.shape)
    rx = shifted(upx, "gx", 1)
    ry = shifted(upy, "gy", 1)
    v2, p2 = (pltpu.with_memory_space_constraint(v, pltpu.HBM) for v in (v2, p2.reshape(ROWS, LZ)))
    sol, res, coarse = call(
        last_kernel, "last", [(prolong, SM), got, *coarse, inv, rhs2, v1, (v2, ANY), (p2, ANY), rx, ry],
        [pltpu.HBM((ROWS, LZ), f32)] * 2 + [struct(LY, LZ)],
        [pltpu.VMEM((ROWS, LZ), f32)] * 4 + [pltpu.SemaphoreType.DMA((6,))] * 2, table=table, ny=ny,
    )
    return sol.reshape(rhs.shape), res.reshape(rhs.shape), coarse[None]


def solution(mesh):
    placed = (
        P(None, None, "gx", "gy", None),
        P("gx", "gy", None),
        P("gx", "gy", None),
        P(),
        P(),
        P(),
    )
    return jax.shard_map(
        shards,
        mesh=mesh,
        in_specs=placed,
        out_specs=(
            P(None, None, "gx", "gy", None),
            P(None, None, "gx", "gy", None),
            P("gx", "gy", None),
        ),
        check_vma=False,
    )
```

```python
import jax
import jax.numpy as jnp
import numpy as np
from jax import lax
from jax.experimental import pallas as pl
from jax.experimental.pallas import tpu as pltpu
from jax.sharding import PartitionSpec as P

ITERS = 3
SWEEPS = 8
F, A = 3, 25
B = 24
LAST = 6 * B
OUT, IN = LAST + 8, LAST + 16
LX, LY, LZ = 4, 8, 128
CELLS = LX * LY
FACE = A * CELLS
ROWS = F * FACE
TAIL = F * CELLS * B
f32, bf16 = jnp.float32, jnp.bfloat16
VM = pl.BlockSpec(memory_space=pltpu.VMEM)
SM = pl.BlockSpec(memory_space=pltpu.SMEM)
ANY = pl.BlockSpec(memory_space=pl.ANY)


def shifted(value, axis, by):
    n = lax.axis_size(axis)
    return lax.ppermute(value, axis, [(i, (i + by) % n) for i in range(n)])


def near_swap(value, axis):
    n = lax.axis_size(axis)
    return lax.ppermute(value, axis, [(i, i ^ 1) for i in range(n)])


def far_swap(value, axis):
    n = lax.axis_size(axis)
    pairs = [(i, (i + 1) % n) if i % 2 else (i, (i - 1) % n) for i in range(n)]
    return lax.ppermute(value, axis, pairs)


def halves(v):
    hi = v.astype(bf16)
    lo = (v - hi.astype(f32)).astype(bf16)
    return hi, lo


def apply_operator(v_ref, ux_ref, uy_ref, k_ref, m_ref, w_ref, out_ref, up_x, low_x, up_y, low_y, last_in, last_out, by_nodes=False):
    w_all = w_ref[...]
    at_first = lax.broadcasted_iota(jnp.int32, (LY, LZ), 0) == 0
    last_in[LAST // B * LY :] = jnp.zeros((2 * LY, LZ), f32)

    def block(ref, at, pitch, i):
        if by_nodes:
            return ref[pl.ds(at * A + i, B, stride=pitch), :]
        return ref[(at + i) * B : (at + i + 1) * B, :]

    def face(f, x, y):
        if f == 0 and x == LX:
            return block(ux_ref, 0, LY, y)
        if f == 1 and y == LY:
            return block(uy_ref, 0, LX, x)
        return block(v_ref, f * CELLS, CELLS, x * LY + y)

    def last_rows(f, x):
        if x == LX:
            return ux_ref[B * LY :, :]
        at = (f * FACE + B * CELLS if by_nodes else TAIL + f * CELLS) + x * LY
        return v_ref[at : at + LY, :]

    def put(f, x, y, value):
        at = (f * CELLS + x * LY + y) * B
        out_ref[at : at + B, :] = value

    def put_last(f, x, value):
        at = TAIL + f * CELLS + x * LY
        out_ref[at : at + LY, :] = value

    filler = jnp.zeros((IN - OUT, LZ), f32)
    carry = last_carry = None
    for x in range(LX):
        z_last = last_rows(2, x)
        y_last = last_rows(1, x)
        above = uy_ref[B * LX + x : B * LX + x + 1, :]
        top = lax.broadcasted_iota(jnp.int32, (LY, LZ), 0) == LY - 1
        y_up = jnp.where(top, jnp.broadcast_to(above, (LY, LZ)), pltpu.roll(y_last, LY - 1, 0))
        for j, tile in enumerate((last_rows(0, x), y_last, z_last, last_rows(0, x + 1), y_up, pltpu.roll(z_last, LZ - 1, 1))):
            last_in[j * LY : (j + 1) * LY] = tile
        columns = []
        for y in range(LY):
            z = face(2, x, y)
            six = [face(0, x, y), face(0, x + 1, y), face(1, x, y), face(1, x, y + 1), z, pltpu.roll(z, LZ - 1, 1)]
            columns.append(jnp.concatenate(six + [last_in[pl.ds(y, 8, stride=LY), :], filler], 0))
        hi, lo = halves(jnp.concatenate(columns, 1))
        prod = jnp.dot(w_all, jnp.concatenate([hi, lo, hi], 0), preferred_element_type=f32)
        parts = []
        for y in range(LY):
            k = k_ref[x * LY + y : x * LY + y + 1, :]
            m = m_ref[x * LY + y : x * LY + y + 1, :]
            cols = slice(y * LZ, (y + 1) * LZ)
            w = prod[:OUT, cols] * k + prod[OUT:, cols] * m
            parts.append([w[b * B : (b + 1) * B] for b in range(6)])
            last_out[pl.ds(y, 8, stride=LY), :] = w[LAST:]
        for y in range(LY):
            wlx, wux, wly, wuy, wlz, wuz = parts[y]
            put(0, x, y, wlx if x == 0 else wlx + carry[y])
            put(1, x, y, wly if y == 0 else wly + parts[y - 1][3])
            put(2, x, y, wlz + pltpu.roll(wuz, 1, 1))
            if x == 0 and low_x is not None:
                low_x[y * B : (y + 1) * B] = wlx
            if x == LX - 1:
                up_x[y * B : (y + 1) * B] = wux
        tiles = [last_out[j * LY : (j + 1) * LY] for j in range(6)]
        put_last(0, x, tiles[0] if x == 0 else tiles[0] + last_carry)
        put_last(1, x, tiles[1] + jnp.where(at_first, 0.0, pltpu.roll(tiles[4], 1, 0)))
        put_last(2, x, tiles[2] + pltpu.roll(tiles[5], 1, 1))
        if x == 0 and low_x is not None:
            low_x[B * LY :] = tiles[0]
        if x == LX - 1:
            up_x[B * LY :] = tiles[3]
        if low_y is not None:
            low_y[x * B : (x + 1) * B] = parts[0][2]
            low_y[B * LX + x : B * LX + x + 1] = tiles[1][:1]
        up_y[x * B : (x + 1) * B] = parts[LY - 1][3]
        up_y[B * LX + x : B * LX + x + 1] = tiles[4][LY - 1 :]
        carry = [parts[y][1] for y in range(LY)]
        last_carry = tiles[3]


def is_even(axis):
    return lax.rem(lax.axis_index(axis), 2) == 0


def route(even, up, low, near, far):
    near[...] = jnp.where(even, up[...], low[...])
    far[...] = jnp.where(even, low[...], up[...])


def edge_kernel(rhs_ref, fx_ref, fy_ref, sem_x, sem_y):
    face_x = pltpu.make_async_copy(rhs_ref.at[0, :, 0], fx_ref, sem_x)
    face_y = pltpu.make_async_copy(rhs_ref.at[1, :, :, 0], fy_ref, sem_y)
    face_x.start()
    face_y.start()
    face_x.wait()
    face_y.wait()


def weight_kernel(s_ref, m_ref, w_ref, inv_ref):
    n = 6 * A

    def placing(rows, span):
        r = lax.broadcasted_iota(jnp.int32, (rows, n), 0)
        c = lax.broadcasted_iota(jnp.int32, (rows, n), 1)
        p = lax.rem(r, span)
        j = p - LAST
        node = jnp.where(p < LAST, lax.div(p, B) * A + lax.rem(p, B), (2 * lax.rem(j, 3) + lax.div(j, 3)) * A + B)
        return (node == c) & (p < n), lax.div(r, span)

    def ones(mask):
        return jnp.where(mask, 1.0, 0.0).astype(bf16)

    rows = ones(placing(OUT, OUT)[0])
    mask, third = placing(3 * IN, IN)
    columns = (ones(mask & (third < 2)), ones(mask & (third == 2)))
    diagonal = lax.broadcasted_iota(jnp.int32, (n, n), 0) == lax.broadcasted_iota(jnp.int32, (n, n), 1)

    def largest(v):
        return jnp.max(jnp.max(jnp.where(diagonal, v, 0.0), 0, keepdims=True), 1, keepdims=True)

    inv = 1.0 / (10.0 * largest(s_ref[...]) + 2.0 * largest(m_ref[...]))
    inv_ref[...] = jnp.broadcast_to(inv, (8, LZ))
    for i, ref in enumerate((s_ref, m_ref)):
        full = 0.0
        for part, place in zip(halves(ref[...] * inv), columns):
            moved = jnp.dot(rows, part, preferred_element_type=f32).astype(bf16)
            full = full + lax.dot_general(moved, place, (((1,), (1,)), ((), ())), preferred_element_type=f32)
        w_ref[i * OUT : (i + 1) * OUT] = full.astype(bf16)


def first_kernel(rhs_ref, hx_ref, hy_ref, k_ref, m_ref, w_ref,
                 p_ref, snx, sfx, sny, sfy, last_in, last_out, upx, lowx, upy, lowy):
    apply_operator(rhs_ref, hx_ref, hy_ref, k_ref, m_ref, w_ref, p_ref, upx, lowx, upy, lowy, last_in, last_out, True)
    route(is_even("gx"), upx, lowx, snx, sfx)
    route(is_even("gy"), upy, lowy, sny, sfy)


def assemble(p_ref, snx, sfx, sny, sfy, rnx, rfx, rny, rfy, v, ux, uy):
    even_x = is_even("gx")
    even_y = is_even("gy")
    v[...] = p_ref[...]
    below_x = jnp.where(even_x, rfx[...], rnx[...])
    v[: B * LY] = v[: B * LY] + below_x[: B * LY]
    v[TAIL : TAIL + LY] = v[TAIL : TAIL + LY] + below_x[B * LY :]
    below_y = jnp.where(even_y, rfy[...], rny[...])
    for x in range(LX):
        at = (CELLS + x * LY) * B
        v[at : at + B] = v[at : at + B] + below_y[x * B : (x + 1) * B]
        at = TAIL + CELLS + x * LY
        v[at : at + 1] = v[at : at + 1] + below_y[B * LX + x : B * LX + x + 1]
    ux[...] = jnp.where(even_x, snx[...] + rnx[...], sfx[...] + rfx[...])
    uy[...] = jnp.where(even_y, sny[...] + rny[...], sfy[...] + rfy[...])


def node_sum(value):
    return jnp.sum(value.reshape(-1, LY, LZ), 0)


def row(tile):
    return jnp.sum(tile, 0, keepdims=True)


def second_kernel(p_ref, rfx, rfy, rny, rnx, snx, sfx, sny, sfy, k_ref, m_ref, w_ref,
                  v1_ref, p1_ref, tnx, tfx, tny, tfy, ux, uy, last_in, last_out, upx, lowx, upy, lowy):
    assemble(p_ref, snx, sfx, sny, sfy, rnx, rfx, rny, rfy, v1_ref, ux, uy)
    apply_operator(v1_ref, ux, uy, k_ref, m_ref, w_ref, p1_ref, upx, lowx, upy, lowy, last_in, last_out)
    route(is_even("gx"), upx, lowx, tnx, tfx)
    route(is_even("gy"), upy, lowy, tny, tfy)


def element_sum(ref, faces):
    rows = []
    for y in range(LY):
        total = 0.0
        for at in range(0, faces, LY):
            first = (at + y) * B
            total = total + (ref[first : first + 8] + ref[first + 8 : first + 16] + ref[first + 16 : first + B])
        rows.append(row(total))
    return jnp.concatenate(rows, 0) + node_sum(ref[faces * B :])


def tile_of(ref, faces, f, a, x):
    at = f * CELLS + x * LY
    if a == B:
        return ref[faces * B + at : faces * B + at + LY, :]
    return ref[pl.ds(at * B + a, LY, stride=B), :]


def products_kernel(v0_ref, v1_ref, sums_ref):
    s0 = s1 = s00 = s01 = s11 = 0.0
    for f in range(F):
        for a in range(A):
            for x in range(LX):
                at = (f * A + a) * CELLS + x * LY
                v0 = v0_ref[at : at + LY, :]
                v1 = tile_of(v1_ref, F * CELLS, f, a, x)
                s0, s1, s00, s01, s11 = s0 + v0, s1 + v1, s00 + v0 * v0, s01 + v0 * v1, s11 + v1 * v1
    for k, s in enumerate((s0, s1, s00, s01, s11)):
        sums_ref[8 * k : 8 * k + 8] = s


def third_kernel(p_ref, v1_ref, rfx, rfy, rny, rnx, snx, sfx, sny, sfy, sums_ref, k_ref, m_ref, w_ref,
                 v2_ref, p2_ref, upx, upy, loads_ref, mom_ref, ux, uy, last_in, last_out):
    assemble(p_ref, snx, sfx, sny, sfy, rnx, rfx, rny, rfy, v2_ref, ux, uy)
    v1 = v1_ref[...]
    v2 = v2_ref[...]
    loads_ref[0:16] = sums_ref[0:16]
    loads_ref[16:24] = element_sum(v2_ref, F * CELLS)
    m3 = node_sum(v1 * v2)
    m4 = node_sum(v2 * v2)
    apply_operator(v2_ref, ux, uy, k_ref, m_ref, w_ref, p2_ref, upx, None, upy, None, last_in, last_out)
    loads_ref[24:32] = element_sum(p2_ref, F * CELLS)
    loads_ref[32:40] = element_sum(upx, LY)
    energy = node_sum(v2_ref[...] * p2_ref[...]) + node_sum(ux[...] * upx[...])
    tail = row(uy[...] * upy[...])
    tile = jnp.concatenate(
        [row(sums_ref[16 + 8 * k : 24 + 8 * k]) for k in range(3)]
        + [row(m3), row(m4), row(energy) + tail, jnp.zeros((2, LZ), f32)], 0,
    )
    for lanes in (64, 32, 16):
        tile = tile + pltpu.roll(tile, lanes, 1)
    lane = lax.broadcasted_iota(jnp.int32, (8, LZ), 1)
    moment = lax.broadcasted_iota(jnp.int32, (8, LZ), 0)
    packed = row(jnp.where(lax.div(lane, 16) == moment, tile, 0.0))
    pair = jnp.concatenate([packed, row(upy[...])] * 4, 0)
    for at in range(0, mom_ref.shape[0], 8):
        mom_ref[at : at + 8] = pair
    loads_ref[40:] = jnp.zeros((loads_ref.shape[0] - 40, LZ), f32)


def weigh_kernel(own, near, far, both, *outs, table):
    nx = len(table)
    q = lax.rem(lax.axis_index("gx"), 4)
    low, high = lax.rem(q, 2) == 0, q < 2
    one, two = jnp.where(low, 1, -1), jnp.where(high, 2, -2)
    sources = ((own, 0, (0,)), (near, one, (1, -1)), (far, two, (2, -2)), (both, one + two, (3, 1, -1, -3)))

    def pick(at, shift, span):
        value = jnp.float32(table[(at - span[0]) % nx])
        for s in span[1:]:
            value = jnp.where(shift == s, table[(at - s) % nx], value)
        return value

    for z, out in enumerate(outs):
        total = [0.0] * 4
        for ref, shift, span in sources:
            w = pick(4 * z, shift, span)
            for k in range(4):
                total[k] = total[k] + ref[k * 8 : k * 8 + 8] * w
            total[3] = total[3] + ref[32:40] * pick(4 * z - 1, shift, span)
        for k in range(4):
            out[k * 8 : k * 8 + 8] = total[k]


def two_sum(a, b):
    s = a + b
    t = s - a
    return s, (a - (s - t)) + (b - t)


def pair_add(a, b):
    s, e = two_sum(a[0], b[0])
    e = e + (a[1] + b[1])
    h = s + e
    return h, e - (h - s)


def split(a):
    t = a * 4097.0
    h = t - (t - a)
    return h, a - h


def pair_times(a, c):
    p = a[0] * c
    ah, al = split(a[0])
    ch, cl = split(c)
    return p, ((ah * ch - p) + ah * cl + al * ch) + al * cl + a[1] * c


def moments(got):
    zero = jnp.zeros((8, LZ), f32)
    pairs = [(got[at : at + 8], zero) for at in range(0, got.shape[0], 8)]
    while len(pairs) > 1:
        pairs = [pair_add(a, b) for a, b in zip(pairs[::2], pairs[1::2])]
    h, l = pairs[0]
    rows = [(h[r : r + 1], l[r : r + 1]) for r in (0, 2, 4, 6)]
    t = pair_add(pair_add(rows[0], rows[1]), pair_add(rows[2], rows[3]))
    level = [t] + [tuple(pltpu.roll(p, LZ - 16 * k, 1) for p in t) for k in range(1, 6)]
    inside = lax.broadcasted_iota(jnp.int32, (1, LZ), 1) < 16

    def total(value):
        return jnp.sum(jnp.where(inside, value, 0.0), axis=1, keepdims=True)

    c = total(level[1][0]) / total(level[0][0])
    minus = jnp.broadcast_to(-c, (1, LZ))
    heads = [level[0]]
    while len(level) > 1:
        level = [pair_add(up, pair_times(at, minus)) for at, up in zip(level, level[1:])]
        heads.append(level[0])
    return c, [total(p[0] + p[1]) for p in heads]


def conjugate_gradient(c, m):
    def dot(a, b):
        s = None
        for i, ai in enumerate(a):
            for j, bj in enumerate(b):
                t = ai * bj * m[i + j]
                s = t if s is None else s + t
        return s

    def add(a, b, factor):
        longer = []
        for i in range(max(len(a), len(b))):
            if i >= len(b):
                longer.append(a[i])
            elif i >= len(a):
                longer.append(factor * b[i])
            else:
                longer.append(a[i] + factor * b[i])
        return longer

    def times(a, shift):
        return [a[0] * shift] + [a[i] * shift + a[i - 1] for i in range(1, len(a))] + [a[-1]]

    def plain(a):
        out = [a[-1]]
        for coefficient in a[-2::-1]:
            out = times(out, -c)
            out[0] = out[0] + coefficient
        return out

    one = jnp.ones((1, 1), f32)
    iterate, residual, direction = [], [one], [one]
    norm = m[0]
    for step in range(ITERS):
        img = times(direction, c)
        alpha = norm / dot(direction, img)
        iterate = add(iterate, direction, alpha)
        residual = add(residual, img, -alpha)
        if step < ITERS - 1:
            norm_next = dot(residual, residual)
            direction = add(residual, direction, norm_next / norm)
            norm = norm_next
    return plain(iterate), plain(residual)


def last_kernel(prolong_ref, got_ref, c0, c1, c2, c3, inv_ref, rhs_hbm, v1_ref, v2_ref, p2_ref, rx_ref, ry_ref,
                sol_hbm, res_hbm, coarse_ref, rhs_ref, sol_ref, res_ref, in_sem, out_sems, *, table, ny):
    fetch = pltpu.make_async_copy(rhs_hbm, rhs_ref, in_sem)
    fetch.start()
    x, d = conjugate_gradient(*moments(got_ref[...]))
    inv = inv_ref[0:1, 0:1]
    x = [t * inv for t in x]
    below = lax.rem(lax.axis_index("gy") + ny - 1, ny)
    me = lax.axis_index("gx")
    nx = len(table)
    edge = jnp.zeros((1, LZ), f32)
    for offset, weight in enumerate(table):
        slab = lax.rem(me + nx - offset, nx)
        edge = edge + got_ref[pl.ds(2 * (slab * ny + below) + 1, 1), :] * weight
    circ = [c0[k * 8 : k * 8 + 8] + c1[k * 8 : k * 8 + 8] + c2[k * 8 : k * 8 + 8] + c3[k * 8 : k * 8 + 8] for k in range(4)]
    at_first = lax.broadcasted_iota(jnp.int32, (LY, LZ), 0) == 0
    circ[3] = circ[3] + jnp.where(at_first, jnp.broadcast_to(edge, (LY, LZ)), 0.0)
    coarse = d[0] * circ[0] + d[1] * circ[1] + d[2] * circ[2] + d[3] * circ[3]
    coarse_ref[...] = coarse
    x = [jnp.broadcast_to(t, (LY, LZ)) for t in x]
    d = [jnp.broadcast_to(t, (LY, LZ)) for t in d]
    stores = []
    fetch.wait()
    for f in range(F):
        for a in range(A):
            at = (f * A + a) * CELLS
            spread = coarse * prolong_ref[f, a]
            for cell in range(LX):
                rows = slice(at + cell * LY, at + (cell + 1) * LY)
                v0 = rhs_ref[rows, :]
                v1, v2, img = (tile_of(ref, F * CELLS, f, a, cell) for ref in (v1_ref, v2_ref, p2_ref))
                if f == 0 and cell == 0:
                    img = img + tile_of(rx_ref, LY, 0, a, 0)
                sol_ref[rows, :] = x[0] * v0 + x[1] * v1 + x[2] * v2 + spread
                res_ref[rows, :] = d[0] * v0 + d[1] * v1 + d[2] * v2 + d[3] * img
        if f == 1:
            below = d[3][0:1] * ry_ref[...]
            for cell in range(LX):
                first = pl.ds(FACE + cell * LY, B, stride=CELLS)
                res_ref[first, :] = res_ref[first, :] + below[cell * B : (cell + 1) * B]
            first = pl.ds(FACE + B * CELLS, LX, stride=LY)
            res_ref[first, :] = res_ref[first, :] + below[B * LX :]
        rows = pl.ds(f * FACE, FACE)
        for i, (src, dst) in enumerate(((sol_ref, sol_hbm), (res_ref, res_hbm))):
            stores.append(pltpu.make_async_copy(src.at[rows], dst.at[rows], out_sems.at[2 * f + i]))
            stores[-1].start()
    for store in stores:
        store.wait()


def jacobi_weights(n):
    coarse = np.zeros(n)
    load = np.zeros(n)
    load[0] = 1.0
    for _ in range(SWEEPS):
        coarse = (load + np.roll(coarse, 1) + np.roll(coarse, -1)) / 2.2
    return coarse / 75.0


def struct(*shape):
    return jax.ShapeDtypeStruct(shape, f32)


PARAMS = pltpu.CompilerParams(vmem_limit_bytes=16 * 1024 * 1024)


def shards(rhs, kappa, mass, stiffness, mass_matrix, prolong):
    nx, ny = lax.axis_size("gx"), lax.axis_size("gy")
    vx, vy = A * LY, A * LX
    rhs2 = rhs.reshape(ROWS, LZ)
    k2 = kappa.reshape(CELLS, LZ)
    m2 = mass.reshape(CELLS, LZ)
    sends = [struct(vx, LZ), struct(vx, LZ), struct(vy, LZ), struct(vy, LZ)]
    upper = [pltpu.VMEM((vx, LZ), f32), pltpu.VMEM((vy, LZ), f32)] + [pltpu.VMEM((8 * LY, LZ), f32)] * 2
    edges = [pltpu.VMEM((vx, LZ), f32)] * 2 + [pltpu.VMEM((vy, LZ), f32)] * 2

    def call(kernel, name, ins, outs, scratch=(), **static):
        specs = [i[1] if isinstance(i, tuple) else VM for i in ins]
        ins = [i[0] if isinstance(i, tuple) else i for i in ins]

        def bound(*refs):
            kernel(*refs, **static)

        return pl.pallas_call(
            bound,
            out_shape=outs,
            in_specs=specs,
            out_specs=[ANY if isinstance(o, pl.MemoryRef) else VM for o in outs],
            scratch_shapes=list(scratch),
            compiler_params=PARAMS,
            name=name,
        )(*ins)

    def swap(s):
        far_x = far_swap(s[1], "gx")
        far_y = far_swap(s[3], "gy")
        near_y = near_swap(s[2], "gy")
        near_x = near_swap(s[0], "gx")
        return [far_x, far_y, near_y, near_x]

    hbm = pltpu.with_memory_space_constraint(rhs, pltpu.HBM)
    fx, fy = call(
        edge_kernel, "edges", [(hbm, ANY)], [struct(A, LY, LZ), struct(A, LX, LZ)],
        [pltpu.SemaphoreType.DMA, pltpu.SemaphoreType.DMA],
    )
    hx = shifted(fx.reshape(vx, LZ), "gx", -1)
    hy = shifted(fy.reshape(vy, LZ), "gy", -1)
    w, inv = call(
        weight_kernel, "weights", [stiffness, mass_matrix],
        [jax.ShapeDtypeStruct((2 * OUT, 3 * IN), bf16), struct(8, LZ)],
    )

    p0, *s = call(
        first_kernel, "first", [rhs2, hx, hy, k2, m2, w], [struct(ROWS, LZ)] + sends, upper[2:] + edges,
    )
    r = swap(s)
    v1, p1, *s = call(
        second_kernel, "second", [p0, *r, *s, k2, m2, w],
        [struct(ROWS, LZ), struct(ROWS, LZ)] + sends, upper + edges,
    )
    r = swap(s)
    sums, = call(products_kernel, "products", [rhs2, v1], [struct(40, LZ)])
    peers = nx * ny * 2
    v2, p2, upx, upy, loads, mom = call(
        third_kernel, "third", [p1, v1, *r, *s, sums, k2, m2, w],
        [struct(ROWS, LZ)] * 2 + [struct(vx, LZ), struct(vy, LZ), struct(peers + 8, LZ), struct(peers, LZ)], upper,
    )
    table = [float(t) for t in jacobi_weights(nx)]
    group = [lax.ppermute(loads, "gx", [(i, i ^ b) for i in range(nx)]) for b in (1, 2, 3)]
    pieces = call(weigh_kernel, "weigh", [loads, *group], [struct(32, LZ)] * (nx // 4), table=table)
    coarse = [pieces[0]] + [shifted(p, "gx", 4 * z) for z, p in enumerate(pieces) if z]
    got = lax.all_to_all(mom.reshape(-1, 2, LZ), ("gx", "gy"), 0, 0, tiled=True).reshape(mom.shape)
    rx = shifted(upx, "gx", 1)
    ry = shifted(upy, "gy", 1)
    sol, res, coarse = call(
        last_kernel, "last", [(prolong, SM), got, *coarse, inv, (pltpu.with_memory_space_constraint(rhs2, pltpu.HBM), ANY), v1, v2, p2, rx, ry],
        [pltpu.HBM((ROWS, LZ), f32)] * 2 + [struct(LY, LZ)],
        [pltpu.VMEM((ROWS, LZ), f32)] * 3 + [pltpu.SemaphoreType.DMA, pltpu.SemaphoreType.DMA((6,))], table=table, ny=ny,
    )
    return sol.reshape(rhs.shape), res.reshape(rhs.shape), coarse[None]


def solution(mesh):
    placed = (
        P(None, None, "gx", "gy", None),
        P("gx", "gy", None),
        P("gx", "gy", None),
        P(),
        P(),
        P(),
    )
    return jax.shard_map(
        shards,
        mesh=mesh,
        in_specs=placed,
        out_specs=(
            P(None, None, "gx", "gy", None),
            P(None, None, "gx", "gy", None),
            P("gx", "gy", None),
        ),
        check_vma=False,
    )
```

```python
import jax
import jax.numpy as jnp
import numpy as np
from jax import lax
from jax.experimental import pallas as pl
from jax.experimental.pallas import tpu as pltpu
from jax.sharding import PartitionSpec as P

ITERS = 3
SWEEPS = 8
F, A = 3, 25
B = 24
LAST = 6 * B
OUT, IN = LAST + 8, LAST + 16
LX, LY, LZ = 4, 8, 128
CELLS = LX * LY
FACE = A * CELLS
ROWS = F * FACE
TAIL = F * CELLS * B
f32, bf16 = jnp.float32, jnp.bfloat16
VM = pl.BlockSpec(memory_space=pltpu.VMEM)
SM = pl.BlockSpec(memory_space=pltpu.SMEM)
ANY = pl.BlockSpec(memory_space=pl.ANY)


def shifted(value, axis, by):
    n = lax.axis_size(axis)
    return lax.ppermute(value, axis, [(i, (i + by) % n) for i in range(n)])


def near_swap(value, axis):
    n = lax.axis_size(axis)
    return lax.ppermute(value, axis, [(i, i ^ 1) for i in range(n)])


def far_swap(value, axis):
    n = lax.axis_size(axis)
    pairs = [(i, (i + 1) % n) if i % 2 else (i, (i - 1) % n) for i in range(n)]
    return lax.ppermute(value, axis, pairs)


def halves(v):
    hi = v.astype(bf16)
    lo = (v - hi.astype(f32)).astype(bf16)
    return hi, lo


def apply_operator(v_ref, ux_ref, uy_ref, k_ref, m_ref, w_ref, out_ref, up_x, low_x, up_y, low_y, last_in, last_out, by_nodes=False):
    w_all = w_ref[...]
    at_first = lax.broadcasted_iota(jnp.int32, (LY, LZ), 0) == 0
    last_in[LAST // B * LY :] = jnp.zeros((2 * LY, LZ), f32)

    def block(ref, at, pitch, i):
        if by_nodes:
            return ref[pl.ds(at * A + i, B, stride=pitch), :]
        return ref[(at + i) * B : (at + i + 1) * B, :]

    def face(f, x, y):
        if f == 0 and x == LX:
            return block(ux_ref, 0, LY, y)
        if f == 1 and y == LY:
            return block(uy_ref, 0, LX, x)
        return block(v_ref, f * CELLS, CELLS, x * LY + y)

    def last_rows(f, x):
        if x == LX:
            return ux_ref[B * LY :, :]
        at = (f * FACE + B * CELLS if by_nodes else TAIL + f * CELLS) + x * LY
        return v_ref[at : at + LY, :]

    def put(f, x, y, value):
        at = (f * CELLS + x * LY + y) * B
        out_ref[at : at + B, :] = value

    def put_last(f, x, value):
        at = TAIL + f * CELLS + x * LY
        out_ref[at : at + LY, :] = value

    filler = jnp.zeros((IN - OUT, LZ), f32)
    carry = last_carry = None
    for x in range(LX):
        z_last = last_rows(2, x)
        y_last = last_rows(1, x)
        above = uy_ref[B * LX + x : B * LX + x + 1, :]
        top = lax.broadcasted_iota(jnp.int32, (LY, LZ), 0) == LY - 1
        y_up = jnp.where(top, jnp.broadcast_to(above, (LY, LZ)), pltpu.roll(y_last, LY - 1, 0))
        for j, tile in enumerate((last_rows(0, x), y_last, z_last, last_rows(0, x + 1), y_up, pltpu.roll(z_last, LZ - 1, 1))):
            last_in[j * LY : (j + 1) * LY] = tile
        columns = []
        for y in range(LY):
            z = face(2, x, y)
            six = [face(0, x, y), face(0, x + 1, y), face(1, x, y), face(1, x, y + 1), z, pltpu.roll(z, LZ - 1, 1)]
            columns.append(jnp.concatenate(six + [last_in[pl.ds(y, 8, stride=LY), :], filler], 0))
        hi, lo = halves(jnp.concatenate(columns, 1))
        prod = jnp.dot(w_all, jnp.concatenate([hi, lo, hi], 0), preferred_element_type=f32)
        parts = []
        for y in range(LY):
            k = k_ref[x * LY + y : x * LY + y + 1, :]
            m = m_ref[x * LY + y : x * LY + y + 1, :]
            cols = slice(y * LZ, (y + 1) * LZ)
            w = prod[:OUT, cols] * k + prod[OUT:, cols] * m
            parts.append([w[b * B : (b + 1) * B] for b in range(6)])
            last_out[pl.ds(y, 8, stride=LY), :] = w[LAST:]
        for y in range(LY):
            wlx, wux, wly, wuy, wlz, wuz = parts[y]
            put(0, x, y, wlx if x == 0 else wlx + carry[y])
            put(1, x, y, wly if y == 0 else wly + parts[y - 1][3])
            put(2, x, y, wlz + pltpu.roll(wuz, 1, 1))
            if x == 0 and low_x is not None:
                low_x[y * B : (y + 1) * B] = wlx
            if x == LX - 1:
                up_x[y * B : (y + 1) * B] = wux
        tiles = [last_out[j * LY : (j + 1) * LY] for j in range(6)]
        put_last(0, x, tiles[0] if x == 0 else tiles[0] + last_carry)
        put_last(1, x, tiles[1] + jnp.where(at_first, 0.0, pltpu.roll(tiles[4], 1, 0)))
        put_last(2, x, tiles[2] + pltpu.roll(tiles[5], 1, 1))
        if x == 0 and low_x is not None:
            low_x[B * LY :] = tiles[0]
        if x == LX - 1:
            up_x[B * LY :] = tiles[3]
        if low_y is not None:
            low_y[x * B : (x + 1) * B] = parts[0][2]
            low_y[B * LX + x : B * LX + x + 1] = tiles[1][:1]
        up_y[x * B : (x + 1) * B] = parts[LY - 1][3]
        up_y[B * LX + x : B * LX + x + 1] = tiles[4][LY - 1 :]
        carry = [parts[y][1] for y in range(LY)]
        last_carry = tiles[3]


def is_even(axis):
    return lax.rem(lax.axis_index(axis), 2) == 0


def route(even, up, low, near, far):
    near[...] = jnp.where(even, up[...], low[...])
    far[...] = jnp.where(even, low[...], up[...])


def edge_kernel(rhs_ref, fx_ref, fy_ref, sem_x, sem_y):
    face_x = pltpu.make_async_copy(rhs_ref.at[0, :, 0], fx_ref, sem_x)
    face_y = pltpu.make_async_copy(rhs_ref.at[1, :, :, 0], fy_ref, sem_y)
    face_x.start()
    face_y.start()
    face_x.wait()
    face_y.wait()


def weight_kernel(s_ref, m_ref, w_ref, inv_ref):
    n = 6 * A

    def placing(rows, span):
        r = lax.broadcasted_iota(jnp.int32, (rows, n), 0)
        c = lax.broadcasted_iota(jnp.int32, (rows, n), 1)
        p = lax.rem(r, span)
        j = p - LAST
        node = jnp.where(p < LAST, lax.div(p, B) * A + lax.rem(p, B), (2 * lax.rem(j, 3) + lax.div(j, 3)) * A + B)
        return (node == c) & (p < n), lax.div(r, span)

    def ones(mask):
        return jnp.where(mask, 1.0, 0.0).astype(bf16)

    rows = ones(placing(OUT, OUT)[0])
    mask, third = placing(3 * IN, IN)
    columns = (ones(mask & (third < 2)), ones(mask & (third == 2)))
    diagonal = lax.broadcasted_iota(jnp.int32, (n, n), 0) == lax.broadcasted_iota(jnp.int32, (n, n), 1)

    def largest(v):
        return jnp.max(jnp.max(jnp.where(diagonal, v, 0.0), 0, keepdims=True), 1, keepdims=True)

    inv = 1.0 / (10.0 * largest(s_ref[...]) + 2.0 * largest(m_ref[...]))
    inv_ref[...] = jnp.broadcast_to(inv, (8, LZ))
    for i, ref in enumerate((s_ref, m_ref)):
        full = 0.0
        for part, place in zip(halves(ref[...] * inv), columns):
            moved = jnp.dot(rows, part, preferred_element_type=f32).astype(bf16)
            full = full + lax.dot_general(moved, place, (((1,), (1,)), ((), ())), preferred_element_type=f32)
        w_ref[i * OUT : (i + 1) * OUT] = full.astype(bf16)


def first_kernel(rhs_ref, hx_ref, hy_ref, k_ref, m_ref, w_ref,
                 p_ref, snx, sfx, sny, sfy, last_in, last_out, upx, lowx, upy, lowy):
    apply_operator(rhs_ref, hx_ref, hy_ref, k_ref, m_ref, w_ref, p_ref, upx, lowx, upy, lowy, last_in, last_out, True)
    route(is_even("gx"), upx, lowx, snx, sfx)
    route(is_even("gy"), upy, lowy, sny, sfy)


def assemble(p_ref, snx, sfx, sny, sfy, rnx, rfx, rny, rfy, v, ux, uy):
    even_x = is_even("gx")
    even_y = is_even("gy")
    v[...] = p_ref[...]
    below_x = jnp.where(even_x, rfx[...], rnx[...])
    v[: B * LY] = v[: B * LY] + below_x[: B * LY]
    v[TAIL : TAIL + LY] = v[TAIL : TAIL + LY] + below_x[B * LY :]
    below_y = jnp.where(even_y, rfy[...], rny[...])
    for x in range(LX):
        at = (CELLS + x * LY) * B
        v[at : at + B] = v[at : at + B] + below_y[x * B : (x + 1) * B]
        at = TAIL + CELLS + x * LY
        v[at : at + 1] = v[at : at + 1] + below_y[B * LX + x : B * LX + x + 1]
    ux[...] = jnp.where(even_x, snx[...] + rnx[...], sfx[...] + rfx[...])
    uy[...] = jnp.where(even_y, sny[...] + rny[...], sfy[...] + rfy[...])


def node_sum(value):
    return jnp.sum(value.reshape(-1, LY, LZ), 0)


def row(tile):
    return jnp.sum(tile, 0, keepdims=True)


def second_kernel(p_ref, rfx, rfy, rny, rnx, snx, sfx, sny, sfy, k_ref, m_ref, w_ref,
                  v1_ref, p1_ref, tnx, tfx, tny, tfy, ux, uy, last_in, last_out, upx, lowx, upy, lowy):
    assemble(p_ref, snx, sfx, sny, sfy, rnx, rfx, rny, rfy, v1_ref, ux, uy)
    apply_operator(v1_ref, ux, uy, k_ref, m_ref, w_ref, p1_ref, upx, lowx, upy, lowy, last_in, last_out)
    route(is_even("gx"), upx, lowx, tnx, tfx)
    route(is_even("gy"), upy, lowy, tny, tfy)


def element_sum(ref, faces):
    rows = []
    for y in range(LY):
        total = 0.0
        for at in range(0, faces, LY):
            first = (at + y) * B
            total = total + (ref[first : first + 8] + ref[first + 8 : first + 16] + ref[first + 16 : first + B])
        rows.append(row(total))
    return jnp.concatenate(rows, 0) + node_sum(ref[faces * B :])


def tile_of(ref, faces, f, a, x):
    at = f * CELLS + x * LY
    if a == B:
        return ref[faces * B + at : faces * B + at + LY, :]
    return ref[pl.ds(at * B + a, LY, stride=B), :]


def products_kernel(v0_ref, v1_ref, sums_ref, v1_hbm, sem):
    keep = pltpu.make_async_copy(v1_ref, v1_hbm, sem)
    keep.start()
    s0 = s1 = s00 = s01 = s11 = 0.0
    for f in range(F):
        for a in range(A):
            for x in range(LX):
                at = (f * A + a) * CELLS + x * LY
                v0 = v0_ref[at : at + LY, :]
                v1 = tile_of(v1_ref, F * CELLS, f, a, x)
                s0, s1, s00, s01, s11 = s0 + v0, s1 + v1, s00 + v0 * v0, s01 + v0 * v1, s11 + v1 * v1
    for k, s in enumerate((s0, s1, s00, s01, s11)):
        sums_ref[8 * k : 8 * k + 8] = s
    keep.wait()


def third_kernel(p_ref, v1_ref, rfx, rfy, rny, rnx, snx, sfx, sny, sfy, sums_ref, k_ref, m_ref, w_ref,
                 v2_ref, p2_ref, upx, upy, loads_ref, mom_ref, ux, uy, last_in, last_out):
    assemble(p_ref, snx, sfx, sny, sfy, rnx, rfx, rny, rfy, v2_ref, ux, uy)
    v1 = v1_ref[...]
    v2 = v2_ref[...]
    loads_ref[0:16] = sums_ref[0:16]
    loads_ref[16:24] = element_sum(v2_ref, F * CELLS)
    m3 = node_sum(v1 * v2)
    m4 = node_sum(v2 * v2)
    apply_operator(v2_ref, ux, uy, k_ref, m_ref, w_ref, p2_ref, upx, None, upy, None, last_in, last_out)
    loads_ref[24:32] = element_sum(p2_ref, F * CELLS)
    loads_ref[32:40] = element_sum(upx, LY)
    energy = node_sum(v2_ref[...] * p2_ref[...]) + node_sum(ux[...] * upx[...])
    tail = row(uy[...] * upy[...])
    tile = jnp.concatenate(
        [row(sums_ref[16 + 8 * k : 24 + 8 * k]) for k in range(3)]
        + [row(m3), row(m4), row(energy) + tail, jnp.zeros((2, LZ), f32)], 0,
    )
    for lanes in (64, 32, 16):
        tile = tile + pltpu.roll(tile, lanes, 1)
    lane = lax.broadcasted_iota(jnp.int32, (8, LZ), 1)
    moment = lax.broadcasted_iota(jnp.int32, (8, LZ), 0)
    packed = row(jnp.where(lax.div(lane, 16) == moment, tile, 0.0))
    pair = jnp.concatenate([packed, row(upy[...])] * 4, 0)
    for at in range(0, mom_ref.shape[0], 8):
        mom_ref[at : at + 8] = pair
    loads_ref[40:] = jnp.zeros((loads_ref.shape[0] - 40, LZ), f32)


def weigh_kernel(own, near, far, both, *outs, table):
    nx = len(table)
    q = lax.rem(lax.axis_index("gx"), 4)
    low, high = lax.rem(q, 2) == 0, q < 2
    one, two = jnp.where(low, 1, -1), jnp.where(high, 2, -2)
    sources = ((own, 0, (0,)), (near, one, (1, -1)), (far, two, (2, -2)), (both, one + two, (3, 1, -1, -3)))

    def pick(at, shift, span):
        value = jnp.float32(table[(at - span[0]) % nx])
        for s in span[1:]:
            value = jnp.where(shift == s, table[(at - s) % nx], value)
        return value

    for z, out in enumerate(outs):
        total = [0.0] * 4
        for ref, shift, span in sources:
            w = pick(4 * z, shift, span)
            for k in range(4):
                total[k] = total[k] + ref[k * 8 : k * 8 + 8] * w
            total[3] = total[3] + ref[32:40] * pick(4 * z - 1, shift, span)
        for k in range(4):
            out[k * 8 : k * 8 + 8] = total[k]


def two_sum(a, b):
    s = a + b
    t = s - a
    return s, (a - (s - t)) + (b - t)


def pair_add(a, b):
    s, e = two_sum(a[0], b[0])
    e = e + (a[1] + b[1])
    h = s + e
    return h, e - (h - s)


def split(a):
    t = a * 4097.0
    h = t - (t - a)
    return h, a - h


def pair_times(a, c):
    p = a[0] * c
    ah, al = split(a[0])
    ch, cl = split(c)
    return p, ((ah * ch - p) + ah * cl + al * ch) + al * cl + a[1] * c


def moments(got):
    zero = jnp.zeros((8, LZ), f32)
    pairs = [(got[at : at + 8], zero) for at in range(0, got.shape[0], 8)]
    while len(pairs) > 1:
        pairs = [pair_add(a, b) for a, b in zip(pairs[::2], pairs[1::2])]
    h, l = pairs[0]
    rows = [(h[r : r + 1], l[r : r + 1]) for r in (0, 2, 4, 6)]
    t = pair_add(pair_add(rows[0], rows[1]), pair_add(rows[2], rows[3]))
    level = [t] + [tuple(pltpu.roll(p, LZ - 16 * k, 1) for p in t) for k in range(1, 6)]
    inside = lax.broadcasted_iota(jnp.int32, (1, LZ), 1) < 16

    def total(value):
        return jnp.sum(jnp.where(inside, value, 0.0), axis=1, keepdims=True)

    c = total(level[1][0]) / total(level[0][0])
    minus = jnp.broadcast_to(-c, (1, LZ))
    heads = [level[0]]
    while len(level) > 1:
        level = [pair_add(up, pair_times(at, minus)) for at, up in zip(level, level[1:])]
        heads.append(level[0])
    return c, [total(p[0] + p[1]) for p in heads]


def conjugate_gradient(c, m):
    def dot(a, b):
        s = None
        for i, ai in enumerate(a):
            for j, bj in enumerate(b):
                t = ai * bj * m[i + j]
                s = t if s is None else s + t
        return s

    def add(a, b, factor):
        longer = []
        for i in range(max(len(a), len(b))):
            if i >= len(b):
                longer.append(a[i])
            elif i >= len(a):
                longer.append(factor * b[i])
            else:
                longer.append(a[i] + factor * b[i])
        return longer

    def times(a, shift):
        return [a[0] * shift] + [a[i] * shift + a[i - 1] for i in range(1, len(a))] + [a[-1]]

    def plain(a):
        out = [a[-1]]
        for coefficient in a[-2::-1]:
            out = times(out, -c)
            out[0] = out[0] + coefficient
        return out

    one = jnp.ones((1, 1), f32)
    iterate, residual, direction = [], [one], [one]
    norm = m[0]
    for step in range(ITERS):
        img = times(direction, c)
        alpha = norm / dot(direction, img)
        iterate = add(iterate, direction, alpha)
        residual = add(residual, img, -alpha)
        if step < ITERS - 1:
            norm_next = dot(residual, residual)
            direction = add(residual, direction, norm_next / norm)
            norm = norm_next
    return plain(iterate), plain(residual)


def coefficients_kernel(got_ref, inv_ref, rhs_hbm, v1_hbm, rhs_ref, v1_ref, coef_ref, edge_ref, sems, *, table, ny):
    fetches = [pltpu.make_async_copy(rhs_hbm, rhs_ref, sems.at[0]), pltpu.make_async_copy(v1_hbm, v1_ref, sems.at[1])]
    for fetch in fetches:
        fetch.start()
    x, d = conjugate_gradient(*moments(got_ref[...]))
    inv = inv_ref[0:1, 0:1]
    for k, t in enumerate([t * inv for t in x] + d):
        coef_ref[k : k + 1] = jnp.broadcast_to(t, (1, LZ))
    coef_ref[7:8] = jnp.zeros((1, LZ), f32)
    below = lax.rem(lax.axis_index("gy") + ny - 1, ny)
    me = lax.axis_index("gx")
    nx = len(table)
    edge = jnp.zeros((1, LZ), f32)
    for offset, weight in enumerate(table):
        slab = lax.rem(me + nx - offset, nx)
        edge = edge + got_ref[pl.ds(2 * (slab * ny + below) + 1, 1), :] * weight
    edge_ref[...] = jnp.concatenate([edge, jnp.zeros((LY - 1, LZ), f32)], 0)
    for fetch in fetches:
        fetch.wait()


def last_kernel(prolong_ref, coef_ref, edge_ref, c0, c1, c2, c3, rhs_ref, v1_ref, v2_ref, p2_ref, rx_ref, ry_ref,
                sol_hbm, res_hbm, coarse_ref, sol_ref, res_ref, out_sems):
    coef = [jnp.broadcast_to(coef_ref[k : k + 1], (LY, LZ)) for k in range(7)]
    x, d = coef[:3], coef[3:]
    circ = [c0[k * 8 : k * 8 + 8] + c1[k * 8 : k * 8 + 8] + c2[k * 8 : k * 8 + 8] + c3[k * 8 : k * 8 + 8] for k in range(4)]
    coarse = d[0] * circ[0] + d[1] * circ[1] + d[2] * circ[2] + d[3] * (circ[3] + edge_ref[...])
    coarse_ref[...] = coarse
    stores = []
    for f in range(F):
        for a in range(A):
            at = (f * A + a) * CELLS
            spread = coarse * prolong_ref[f, a]
            for cell in range(LX):
                rows = slice(at + cell * LY, at + (cell + 1) * LY)
                v0 = rhs_ref[rows, :]
                v1, v2, img = (tile_of(ref, F * CELLS, f, a, cell) for ref in (v1_ref, v2_ref, p2_ref))
                if f == 0 and cell == 0:
                    img = img + tile_of(rx_ref, LY, 0, a, 0)
                sol_ref[rows, :] = x[0] * v0 + x[1] * v1 + x[2] * v2 + spread
                res_ref[rows, :] = d[0] * v0 + d[1] * v1 + d[2] * v2 + d[3] * img
        if f == 1:
            below = d[3][0:1] * ry_ref[...]
            for cell in range(LX):
                first = pl.ds(FACE + cell * LY, B, stride=CELLS)
                res_ref[first, :] = res_ref[first, :] + below[cell * B : (cell + 1) * B]
            first = pl.ds(FACE + B * CELLS, LX, stride=LY)
            res_ref[first, :] = res_ref[first, :] + below[B * LX :]
        rows = pl.ds(f * FACE, FACE)
        for i, (src, dst) in enumerate(((sol_ref, sol_hbm), (res_ref, res_hbm))):
            stores.append(pltpu.make_async_copy(src.at[rows], dst.at[rows], out_sems.at[2 * f + i]))
            stores[-1].start()
    for store in stores:
        store.wait()


def jacobi_weights(n):
    coarse = np.zeros(n)
    load = np.zeros(n)
    load[0] = 1.0
    for _ in range(SWEEPS):
        coarse = (load + np.roll(coarse, 1) + np.roll(coarse, -1)) / 2.2
    return coarse / 75.0


def struct(*shape):
    return jax.ShapeDtypeStruct(shape, f32)


PARAMS = pltpu.CompilerParams(vmem_limit_bytes=16 * 1024 * 1024)


def shards(rhs, kappa, mass, stiffness, mass_matrix, prolong):
    nx, ny = lax.axis_size("gx"), lax.axis_size("gy")
    vx, vy = A * LY, A * LX
    rhs2 = rhs.reshape(ROWS, LZ)
    k2 = kappa.reshape(CELLS, LZ)
    m2 = mass.reshape(CELLS, LZ)
    sends = [struct(vx, LZ), struct(vx, LZ), struct(vy, LZ), struct(vy, LZ)]
    upper = [pltpu.VMEM((vx, LZ), f32), pltpu.VMEM((vy, LZ), f32)] + [pltpu.VMEM((8 * LY, LZ), f32)] * 2
    edges = [pltpu.VMEM((vx, LZ), f32)] * 2 + [pltpu.VMEM((vy, LZ), f32)] * 2

    def call(kernel, name, ins, outs, scratch=(), **static):
        specs = [i[1] if isinstance(i, tuple) else VM for i in ins]
        ins = [i[0] if isinstance(i, tuple) else i for i in ins]

        def bound(*refs):
            kernel(*refs, **static)

        return pl.pallas_call(
            bound,
            out_shape=outs,
            in_specs=specs,
            out_specs=[ANY if isinstance(o, pl.MemoryRef) else VM for o in outs],
            scratch_shapes=list(scratch),
            compiler_params=PARAMS,
            name=name,
        )(*ins)

    def swap(s):
        far_x = far_swap(s[1], "gx")
        far_y = far_swap(s[3], "gy")
        near_y = near_swap(s[2], "gy")
        near_x = near_swap(s[0], "gx")
        return [far_x, far_y, near_y, near_x]

    hbm = pltpu.with_memory_space_constraint(rhs, pltpu.HBM)
    fx, fy = call(
        edge_kernel, "edges", [(hbm, ANY)], [struct(A, LY, LZ), struct(A, LX, LZ)],
        [pltpu.SemaphoreType.DMA, pltpu.SemaphoreType.DMA],
    )
    hx = shifted(fx.reshape(vx, LZ), "gx", -1)
    hy = shifted(fy.reshape(vy, LZ), "gy", -1)
    w, inv = call(
        weight_kernel, "weights", [stiffness, mass_matrix],
        [jax.ShapeDtypeStruct((2 * OUT, 3 * IN), bf16), struct(8, LZ)],
    )

    p0, *s = call(
        first_kernel, "first", [rhs2, hx, hy, k2, m2, w], [struct(ROWS, LZ)] + sends, upper[2:] + edges,
    )
    r = swap(s)
    v1, p1, *s = call(
        second_kernel, "second", [p0, *r, *s, k2, m2, w],
        [struct(ROWS, LZ), struct(ROWS, LZ)] + sends, upper + edges,
    )
    r = swap(s)
    sums, v1_kept = call(
        products_kernel, "products", [rhs2, v1], [struct(40, LZ), pltpu.HBM((ROWS, LZ), f32)], [pltpu.SemaphoreType.DMA],
    )
    peers = nx * ny * 2
    v2, p2, upx, upy, loads, mom = call(
        third_kernel, "third", [p1, v1, *r, *s, sums, k2, m2, w],
        [struct(ROWS, LZ)] * 2 + [struct(vx, LZ), struct(vy, LZ), struct(peers + 8, LZ), struct(peers, LZ)], upper,
    )
    table = [float(t) for t in jacobi_weights(nx)]
    group = [lax.ppermute(loads, "gx", [(i, i ^ b) for i in range(nx)]) for b in (1, 2, 3)]
    pieces = call(weigh_kernel, "weigh", [loads, *group], [struct(32, LZ)] * (nx // 4), table=table)
    coarse = [pieces[0]] + [shifted(p, "gx", 4 * z) for z, p in enumerate(pieces) if z]
    got = lax.all_to_all(mom.reshape(-1, 2, LZ), ("gx", "gy"), 0, 0, tiled=True).reshape(mom.shape)
    rx = shifted(upx, "gx", 1)
    ry = shifted(upy, "gy", 1)
    v0, v1_kept = (pltpu.with_memory_space_constraint(v, pltpu.HBM) for v in (rhs2, v1_kept))
    v0, v1, coef, edge = call(
        coefficients_kernel, "coefficients", [got, inv, (v0, ANY), (v1_kept, ANY)],
        [struct(ROWS, LZ)] * 2 + [struct(8, LZ), struct(LY, LZ)], [pltpu.SemaphoreType.DMA((2,))], table=table, ny=ny,
    )
    sol, res, coarse = call(
        last_kernel, "last", [(prolong, SM), coef, edge, *coarse, v0, v1, v2, p2, rx, ry],
        [pltpu.HBM((ROWS, LZ), f32)] * 2 + [struct(LY, LZ)],
        [pltpu.VMEM((ROWS, LZ), f32)] * 2 + [pltpu.SemaphoreType.DMA((6,))],
    )
    return sol.reshape(rhs.shape), res.reshape(rhs.shape), coarse[None]


def solution(mesh):
    placed = (
        P(None, None, "gx", "gy", None),
        P("gx", "gy", None),
        P("gx", "gy", None),
        P(),
        P(),
        P(),
    )
    return jax.shard_map(
        shards,
        mesh=mesh,
        in_specs=placed,
        out_specs=(
            P(None, None, "gx", "gy", None),
            P(None, None, "gx", "gy", None),
            P("gx", "gy", None),
        ),
        check_vma=False,
    )
```

```python
import jax
import jax.numpy as jnp
import numpy as np
from jax import lax
from jax.experimental import pallas as pl
from jax.experimental.pallas import tpu as pltpu
from jax.sharding import PartitionSpec as P

ITERS = 3
SWEEPS = 8
F, A = 3, 25
B = 24
LAST = 6 * B
OUT, IN = LAST + 8, LAST + 16
LX, LY, LZ = 4, 8, 128
CELLS = LX * LY
FACE = A * CELLS
ROWS = F * FACE
TAIL = F * CELLS * B
f32, bf16 = jnp.float32, jnp.bfloat16
VM = pl.BlockSpec(memory_space=pltpu.VMEM)
SM = pl.BlockSpec(memory_space=pltpu.SMEM)
ANY = pl.BlockSpec(memory_space=pl.ANY)


PARTS = (100, 100)


class Parts:
    def __init__(self, *refs):
        self.refs = refs

    def __getitem__(self, _):
        return jnp.concatenate([ref[...] for ref in self.refs], 0)

    def __setitem__(self, _, value):
        at = 0
        for ref in self.refs:
            ref[...] = value[at : at + ref.shape[0]]
            at += ref.shape[0]


def shifted(value, axis, by):
    n = lax.axis_size(axis)
    return lax.ppermute(value, axis, [(i, (i + by) % n) for i in range(n)])


def near_swap(value, axis):
    n = lax.axis_size(axis)
    return lax.ppermute(value, axis, [(i, i ^ 1) for i in range(n)])


def far_swap(value, axis):
    n = lax.axis_size(axis)
    pairs = [(i, (i + 1) % n) if i % 2 else (i, (i - 1) % n) for i in range(n)]
    return lax.ppermute(value, axis, pairs)


def halves(v):
    hi = v.astype(bf16)
    lo = (v - hi.astype(f32)).astype(bf16)
    return hi, lo


def apply_operator(v_ref, ux_ref, uy_ref, k_ref, m_ref, w_ref, out_ref, up_x, low_x, up_y, low_y, last_in, last_out, by_nodes=False):
    w_all = w_ref[...]
    at_first = lax.broadcasted_iota(jnp.int32, (LY, LZ), 0) == 0
    last_in[LAST // B * LY :] = jnp.zeros((2 * LY, LZ), f32)

    def block(ref, at, pitch, i):
        if by_nodes:
            return ref[pl.ds(at * A + i, B, stride=pitch), :]
        return ref[(at + i) * B : (at + i + 1) * B, :]

    def face(f, x, y):
        if f == 0 and x == LX:
            return block(ux_ref, 0, LY, y)
        if f == 1 and y == LY:
            return block(uy_ref, 0, LX, x)
        return block(v_ref, f * CELLS, CELLS, x * LY + y)

    def last_rows(f, x):
        if x == LX:
            return ux_ref[B * LY :, :]
        at = (f * FACE + B * CELLS if by_nodes else TAIL + f * CELLS) + x * LY
        return v_ref[at : at + LY, :]

    def put(f, x, y, value):
        at = (f * CELLS + x * LY + y) * B
        out_ref[at : at + B, :] = value

    def put_last(f, x, value):
        at = TAIL + f * CELLS + x * LY
        out_ref[at : at + LY, :] = value

    filler = jnp.zeros((IN - OUT, LZ), f32)
    carry = last_carry = None
    for x in range(LX):
        z_last = last_rows(2, x)
        y_last = last_rows(1, x)
        above = uy_ref[B * LX + x : B * LX + x + 1, :]
        top = lax.broadcasted_iota(jnp.int32, (LY, LZ), 0) == LY - 1
        y_up = jnp.where(top, jnp.broadcast_to(above, (LY, LZ)), pltpu.roll(y_last, LY - 1, 0))
        for j, tile in enumerate((last_rows(0, x), y_last, z_last, last_rows(0, x + 1), y_up, pltpu.roll(z_last, LZ - 1, 1))):
            last_in[j * LY : (j + 1) * LY] = tile
        columns = []
        for y in range(LY):
            z = face(2, x, y)
            six = [face(0, x, y), face(0, x + 1, y), face(1, x, y), face(1, x, y + 1), z, pltpu.roll(z, LZ - 1, 1)]
            columns.append(jnp.concatenate(six + [last_in[pl.ds(y, 8, stride=LY), :], filler], 0))
        hi, lo = halves(jnp.concatenate(columns, 1))
        prod = jnp.dot(w_all, jnp.concatenate([hi, lo, hi], 0), preferred_element_type=f32)
        parts = []
        for y in range(LY):
            k = k_ref[x * LY + y : x * LY + y + 1, :]
            m = m_ref[x * LY + y : x * LY + y + 1, :]
            cols = slice(y * LZ, (y + 1) * LZ)
            w = prod[:OUT, cols] * k + prod[OUT:, cols] * m
            parts.append([w[b * B : (b + 1) * B] for b in range(6)])
            last_out[pl.ds(y, 8, stride=LY), :] = w[LAST:]
        for y in range(LY):
            wlx, wux, wly, wuy, wlz, wuz = parts[y]
            put(0, x, y, wlx if x == 0 else wlx + carry[y])
            put(1, x, y, wly if y == 0 else wly + parts[y - 1][3])
            put(2, x, y, wlz + pltpu.roll(wuz, 1, 1))
            if x == 0 and low_x is not None:
                low_x[y * B : (y + 1) * B] = wlx
            if x == LX - 1:
                up_x[y * B : (y + 1) * B] = wux
        tiles = [last_out[j * LY : (j + 1) * LY] for j in range(6)]
        put_last(0, x, tiles[0] if x == 0 else tiles[0] + last_carry)
        put_last(1, x, tiles[1] + jnp.where(at_first, 0.0, pltpu.roll(tiles[4], 1, 0)))
        put_last(2, x, tiles[2] + pltpu.roll(tiles[5], 1, 1))
        if x == 0 and low_x is not None:
            low_x[B * LY :] = tiles[0]
        if x == LX - 1:
            up_x[B * LY :] = tiles[3]
        if low_y is not None:
            low_y[x * B : (x + 1) * B] = parts[0][2]
            low_y[B * LX + x : B * LX + x + 1] = tiles[1][:1]
        up_y[x * B : (x + 1) * B] = parts[LY - 1][3]
        up_y[B * LX + x : B * LX + x + 1] = tiles[4][LY - 1 :]
        carry = [parts[y][1] for y in range(LY)]
        last_carry = tiles[3]


def is_even(axis):
    return lax.rem(lax.axis_index(axis), 2) == 0


def route(even, up, low, near, far):
    near[...] = jnp.where(even, up[...], low[...])
    far[...] = jnp.where(even, low[...], up[...])


def edge_kernel(rhs_ref, fx_ref, fy_ref, sem_x, sem_y):
    face_x = pltpu.make_async_copy(rhs_ref.at[0, :, 0], fx_ref, sem_x)
    face_y = pltpu.make_async_copy(rhs_ref.at[1, :, :, 0], fy_ref, sem_y)
    face_x.start()
    face_y.start()
    face_x.wait()
    face_y.wait()


def weight_kernel(s_ref, m_ref, w_ref, inv_ref):
    n = 6 * A

    def placing(rows, span):
        r = lax.broadcasted_iota(jnp.int32, (rows, n), 0)
        c = lax.broadcasted_iota(jnp.int32, (rows, n), 1)
        p = lax.rem(r, span)
        j = p - LAST
        node = jnp.where(p < LAST, lax.div(p, B) * A + lax.rem(p, B), (2 * lax.rem(j, 3) + lax.div(j, 3)) * A + B)
        return (node == c) & (p < n), lax.div(r, span)

    def ones(mask):
        return jnp.where(mask, 1.0, 0.0).astype(bf16)

    rows = ones(placing(OUT, OUT)[0])
    mask, third = placing(3 * IN, IN)
    columns = (ones(mask & (third < 2)), ones(mask & (third == 2)))
    diagonal = lax.broadcasted_iota(jnp.int32, (n, n), 0) == lax.broadcasted_iota(jnp.int32, (n, n), 1)

    def largest(v):
        return jnp.max(jnp.max(jnp.where(diagonal, v, 0.0), 0, keepdims=True), 1, keepdims=True)

    inv = 1.0 / (10.0 * largest(s_ref[...]) + 2.0 * largest(m_ref[...]))
    inv_ref[...] = jnp.broadcast_to(inv, (8, LZ))
    for i, ref in enumerate((s_ref, m_ref)):
        full = 0.0
        for part, place in zip(halves(ref[...] * inv), columns):
            moved = jnp.dot(rows, part, preferred_element_type=f32).astype(bf16)
            full = full + lax.dot_general(moved, place, (((1,), (1,)), ((), ())), preferred_element_type=f32)
        w_ref[i * OUT : (i + 1) * OUT] = full.astype(bf16)


def first_kernel(rhs_ref, hx_ref, hy_ref, k_ref, m_ref, w_ref,
                 p_ref, sn0, sn1, sfx, sny, sfy, last_in, last_out, upx, lowx, upy, lowy):
    apply_operator(rhs_ref, hx_ref, hy_ref, k_ref, m_ref, w_ref, p_ref, upx, lowx, upy, lowy, last_in, last_out, True)
    route(is_even("gx"), upx, lowx, Parts(sn0, sn1), sfx)
    route(is_even("gy"), upy, lowy, sny, sfy)


def assemble(p_ref, snx, sfx, sny, sfy, rnx, rfx, rny, rfy, v, ux, uy):
    even_x = is_even("gx")
    even_y = is_even("gy")
    v[...] = p_ref[...]
    below_x = jnp.where(even_x, rfx[...], rnx[...])
    v[: B * LY] = v[: B * LY] + below_x[: B * LY]
    v[TAIL : TAIL + LY] = v[TAIL : TAIL + LY] + below_x[B * LY :]
    below_y = jnp.where(even_y, rfy[...], rny[...])
    for x in range(LX):
        at = (CELLS + x * LY) * B
        v[at : at + B] = v[at : at + B] + below_y[x * B : (x + 1) * B]
        at = TAIL + CELLS + x * LY
        v[at : at + 1] = v[at : at + 1] + below_y[B * LX + x : B * LX + x + 1]
    ux[...] = jnp.where(even_x, snx[...] + rnx[...], sfx[...] + rfx[...])
    uy[...] = jnp.where(even_y, sny[...] + rny[...], sfy[...] + rfy[...])


def node_sum(value):
    return jnp.sum(value.reshape(-1, LY, LZ), 0)


def row(tile):
    return jnp.sum(tile, 0, keepdims=True)


def second_kernel(p_ref, rfx, rfy, rny, rn0, rn1, sn0, sn1, sfx, sny, sfy, k_ref, m_ref, w_ref,
                  v1_ref, p1_ref, tn0, tn1, tfx, tny, tfy, ux, uy, last_in, last_out, upx, lowx, upy, lowy):
    assemble(p_ref, Parts(sn0, sn1), sfx, sny, sfy, Parts(rn0, rn1), rfx, rny, rfy, v1_ref, ux, uy)
    apply_operator(v1_ref, ux, uy, k_ref, m_ref, w_ref, p1_ref, upx, lowx, upy, lowy, last_in, last_out)
    route(is_even("gx"), upx, lowx, Parts(tn0, tn1), tfx)
    route(is_even("gy"), upy, lowy, tny, tfy)


def element_sum(ref, faces):
    rows = []
    for y in range(LY):
        total = 0.0
        for at in range(0, faces, LY):
            first = (at + y) * B
            total = total + (ref[first : first + 8] + ref[first + 8 : first + 16] + ref[first + 16 : first + B])
        rows.append(row(total))
    return jnp.concatenate(rows, 0) + node_sum(ref[faces * B :])


def tile_of(ref, faces, f, a, x):
    at = f * CELLS + x * LY
    if a == B:
        return ref[faces * B + at : faces * B + at + LY, :]
    return ref[pl.ds(at * B + a, LY, stride=B), :]


def products_kernel(v0_ref, v1_ref, sums_ref, v1_hbm, sem):
    keep = pltpu.make_async_copy(v1_ref, v1_hbm, sem)
    keep.start()
    s0 = s1 = s00 = s01 = s11 = 0.0
    for f in range(F):
        for a in range(A):
            for x in range(LX):
                at = (f * A + a) * CELLS + x * LY
                v0 = v0_ref[at : at + LY, :]
                v1 = tile_of(v1_ref, F * CELLS, f, a, x)
                s0, s1, s00, s01, s11 = s0 + v0, s1 + v1, s00 + v0 * v0, s01 + v0 * v1, s11 + v1 * v1
    for k, s in enumerate((s0, s1, s00, s01, s11)):
        sums_ref[8 * k : 8 * k + 8] = s
    keep.wait()


def third_kernel(p_ref, v1_ref, rfx, rfy, rny, rn0, rn1, sn0, sn1, sfx, sny, sfy, sums_ref, k_ref, m_ref, w_ref,
                 v2_ref, p2_ref, upx, upy, loads_ref, mom_ref, ux, uy, last_in, last_out):
    assemble(p_ref, Parts(sn0, sn1), sfx, sny, sfy, Parts(rn0, rn1), rfx, rny, rfy, v2_ref, ux, uy)
    v1 = v1_ref[...]
    v2 = v2_ref[...]
    loads_ref[0:16] = sums_ref[0:16]
    loads_ref[16:24] = element_sum(v2_ref, F * CELLS)
    m3 = node_sum(v1 * v2)
    m4 = node_sum(v2 * v2)
    apply_operator(v2_ref, ux, uy, k_ref, m_ref, w_ref, p2_ref, upx, None, upy, None, last_in, last_out)
    loads_ref[24:32] = element_sum(p2_ref, F * CELLS)
    loads_ref[32:40] = element_sum(upx, LY)
    energy = node_sum(v2_ref[...] * p2_ref[...]) + node_sum(ux[...] * upx[...])
    tail = row(uy[...] * upy[...])
    tile = jnp.concatenate(
        [row(sums_ref[16 + 8 * k : 24 + 8 * k]) for k in range(3)]
        + [row(m3), row(m4), row(energy) + tail, jnp.zeros((2, LZ), f32)], 0,
    )
    for lanes in (64, 32, 16):
        tile = tile + pltpu.roll(tile, lanes, 1)
    lane = lax.broadcasted_iota(jnp.int32, (8, LZ), 1)
    moment = lax.broadcasted_iota(jnp.int32, (8, LZ), 0)
    packed = row(jnp.where(lax.div(lane, 16) == moment, tile, 0.0))
    pair = jnp.concatenate([packed, row(upy[...])] * 4, 0)
    for at in range(0, mom_ref.shape[0], 8):
        mom_ref[at : at + 8] = pair
    loads_ref[40:] = jnp.zeros((loads_ref.shape[0] - 40, LZ), f32)


def weigh_kernel(own, near, far, both, *outs, table):
    nx = len(table)
    q = lax.rem(lax.axis_index("gx"), 4)
    low, high = lax.rem(q, 2) == 0, q < 2
    one, two = jnp.where(low, 1, -1), jnp.where(high, 2, -2)
    sources = ((own, 0, (0,)), (near, one, (1, -1)), (far, two, (2, -2)), (both, one + two, (3, 1, -1, -3)))

    def pick(at, shift, span):
        value = jnp.float32(table[(at - span[0]) % nx])
        for s in span[1:]:
            value = jnp.where(shift == s, table[(at - s) % nx], value)
        return value

    for z, out in enumerate(outs):
        total = [0.0] * 4
        for ref, shift, span in sources:
            w = pick(4 * z, shift, span)
            for k in range(4):
                total[k] = total[k] + ref[k * 8 : k * 8 + 8] * w
            total[3] = total[3] + ref[32:40] * pick(4 * z - 1, shift, span)
        for k in range(4):
            out[k * 8 : k * 8 + 8] = total[k]


def two_sum(a, b):
    s = a + b
    t = s - a
    return s, (a - (s - t)) + (b - t)


def pair_add(a, b):
    s, e = two_sum(a[0], b[0])
    e = e + (a[1] + b[1])
    h = s + e
    return h, e - (h - s)


def split(a):
    t = a * 4097.0
    h = t - (t - a)
    return h, a - h


def pair_times(a, c):
    p = a[0] * c
    ah, al = split(a[0])
    ch, cl = split(c)
    return p, ((ah * ch - p) + ah * cl + al * ch) + al * cl + a[1] * c


def moments(got):
    zero = jnp.zeros((8, LZ), f32)
    pairs = [(got[at : at + 8], zero) for at in range(0, got.shape[0], 8)]
    while len(pairs) > 1:
        pairs = [pair_add(a, b) for a, b in zip(pairs[::2], pairs[1::2])]
    h, l = pairs[0]
    rows = [(h[r : r + 1], l[r : r + 1]) for r in (0, 2, 4, 6)]
    t = pair_add(pair_add(rows[0], rows[1]), pair_add(rows[2], rows[3]))
    level = [t] + [tuple(pltpu.roll(p, LZ - 16 * k, 1) for p in t) for k in range(1, 6)]
    inside = lax.broadcasted_iota(jnp.int32, (1, LZ), 1) < 16

    def total(value):
        return jnp.sum(jnp.where(inside, value, 0.0), axis=1, keepdims=True)

    c = total(level[1][0]) / total(level[0][0])
    minus = jnp.broadcast_to(-c, (1, LZ))
    heads = [level[0]]
    while len(level) > 1:
        level = [pair_add(up, pair_times(at, minus)) for at, up in zip(level, level[1:])]
        heads.append(level[0])
    return c, [total(p[0] + p[1]) for p in heads]


def conjugate_gradient(c, m):
    def dot(a, b):
        s = None
        for i, ai in enumerate(a):
            for j, bj in enumerate(b):
                t = ai * bj * m[i + j]
                s = t if s is None else s + t
        return s

    def add(a, b, factor):
        longer = []
        for i in range(max(len(a), len(b))):
            if i >= len(b):
                longer.append(a[i])
            elif i >= len(a):
                longer.append(factor * b[i])
            else:
                longer.append(a[i] + factor * b[i])
        return longer

    def times(a, shift):
        return [a[0] * shift] + [a[i] * shift + a[i - 1] for i in range(1, len(a))] + [a[-1]]

    def plain(a):
        out = [a[-1]]
        for coefficient in a[-2::-1]:
            out = times(out, -c)
            out[0] = out[0] + coefficient
        return out

    one = jnp.ones((1, 1), f32)
    iterate, residual, direction = [], [one], [one]
    norm = m[0]
    for step in range(ITERS):
        img = times(direction, c)
        alpha = norm / dot(direction, img)
        iterate = add(iterate, direction, alpha)
        residual = add(residual, img, -alpha)
        if step < ITERS - 1:
            norm_next = dot(residual, residual)
            direction = add(residual, direction, norm_next / norm)
            norm = norm_next
    return plain(iterate), plain(residual)


def coefficients_kernel(got_ref, inv_ref, rhs_hbm, v1_hbm, rhs_ref, v1_ref, coef_ref, edge_ref, sems, *, table, ny):
    fetches = [pltpu.make_async_copy(rhs_hbm, rhs_ref, sems.at[0]), pltpu.make_async_copy(v1_hbm, v1_ref, sems.at[1])]
    for fetch in fetches:
        fetch.start()
    x, d = conjugate_gradient(*moments(got_ref[...]))
    inv = inv_ref[0:1, 0:1]
    for k, t in enumerate([t * inv for t in x] + d):
        coef_ref[k : k + 1] = jnp.broadcast_to(t, (1, LZ))
    coef_ref[7:8] = jnp.zeros((1, LZ), f32)
    below = lax.rem(lax.axis_index("gy") + ny - 1, ny)
    me = lax.axis_index("gx")
    nx = len(table)
    edge = jnp.zeros((1, LZ), f32)
    for offset, weight in enumerate(table):
        slab = lax.rem(me + nx - offset, nx)
        edge = edge + got_ref[pl.ds(2 * (slab * ny + below) + 1, 1), :] * weight
    edge_ref[...] = jnp.concatenate([edge, jnp.zeros((LY - 1, LZ), f32)], 0)
    for fetch in fetches:
        fetch.wait()


def last_kernel(prolong_ref, coef_ref, edge_ref, c0, c1, c2, c3, rhs_ref, v1_ref, v2_ref, p2_ref, rx_ref, ry_ref,
                sol_hbm, res_hbm, coarse_ref, sol_ref, res_ref, out_sems):
    coef = [jnp.broadcast_to(coef_ref[k : k + 1], (LY, LZ)) for k in range(7)]
    x, d = coef[:3], coef[3:]
    circ = [c0[k * 8 : k * 8 + 8] + c1[k * 8 : k * 8 + 8] + c2[k * 8 : k * 8 + 8] + c3[k * 8 : k * 8 + 8] for k in range(4)]
    coarse = d[0] * circ[0] + d[1] * circ[1] + d[2] * circ[2] + d[3] * (circ[3] + edge_ref[...])
    coarse_ref[...] = coarse
    stores = []
    for f in range(F):
        for a in range(A):
            at = (f * A + a) * CELLS
            spread = coarse * prolong_ref[f, a]
            for cell in range(LX):
                rows = slice(at + cell * LY, at + (cell + 1) * LY)
                v0 = rhs_ref[rows, :]
                v1, v2, img = (tile_of(ref, F * CELLS, f, a, cell) for ref in (v1_ref, v2_ref, p2_ref))
                if f == 0 and cell == 0:
                    img = img + tile_of(rx_ref, LY, 0, a, 0)
                sol_ref[rows, :] = x[0] * v0 + x[1] * v1 + x[2] * v2 + spread
                res_ref[rows, :] = d[0] * v0 + d[1] * v1 + d[2] * v2 + d[3] * img
        if f == 1:
            below = d[3][0:1] * ry_ref[...]
            for cell in range(LX):
                first = pl.ds(FACE + cell * LY, B, stride=CELLS)
                res_ref[first, :] = res_ref[first, :] + below[cell * B : (cell + 1) * B]
            first = pl.ds(FACE + B * CELLS, LX, stride=LY)
            res_ref[first, :] = res_ref[first, :] + below[B * LX :]
        rows = pl.ds(f * FACE, FACE)
        for i, (src, dst) in enumerate(((sol_ref, sol_hbm), (res_ref, res_hbm))):
            stores.append(pltpu.make_async_copy(src.at[rows], dst.at[rows], out_sems.at[2 * f + i]))
            stores[-1].start()
    for store in stores:
        store.wait()


def jacobi_weights(n):
    coarse = np.zeros(n)
    load = np.zeros(n)
    load[0] = 1.0
    for _ in range(SWEEPS):
        coarse = (load + np.roll(coarse, 1) + np.roll(coarse, -1)) / 2.2
    return coarse / 75.0


def struct(*shape):
    return jax.ShapeDtypeStruct(shape, f32)


PARAMS = pltpu.CompilerParams(vmem_limit_bytes=16 * 1024 * 1024)


def shards(rhs, kappa, mass, stiffness, mass_matrix, prolong):
    nx, ny = lax.axis_size("gx"), lax.axis_size("gy")
    vx, vy = A * LY, A * LX
    rhs2 = rhs.reshape(ROWS, LZ)
    k2 = kappa.reshape(CELLS, LZ)
    m2 = mass.reshape(CELLS, LZ)
    sends = [struct(n, LZ) for n in PARTS] + [struct(vx, LZ), struct(vy, LZ), struct(vy, LZ)]
    upper = [pltpu.VMEM((vx, LZ), f32), pltpu.VMEM((vy, LZ), f32)] + [pltpu.VMEM((8 * LY, LZ), f32)] * 2
    edges = [pltpu.VMEM((vx, LZ), f32)] * 2 + [pltpu.VMEM((vy, LZ), f32)] * 2

    def call(kernel, name, ins, outs, scratch=(), **static):
        specs = [i[1] if isinstance(i, tuple) else VM for i in ins]
        ins = [i[0] if isinstance(i, tuple) else i for i in ins]

        def bound(*refs):
            kernel(*refs, **static)

        return pl.pallas_call(
            bound,
            out_shape=outs,
            in_specs=specs,
            out_specs=[ANY if isinstance(o, pl.MemoryRef) else VM for o in outs],
            scratch_shapes=list(scratch),
            compiler_params=PARAMS,
            name=name,
        )(*ins)

    def swap(s):
        *near, far_x, near_y, far_y = s
        far_x = far_swap(far_x, "gx")
        far_y = far_swap(far_y, "gy")
        near_y = near_swap(near_y, "gy")
        return [far_x, far_y, near_y] + [near_swap(part, "gx") for part in near]

    hbm = pltpu.with_memory_space_constraint(rhs, pltpu.HBM)
    fx, fy = call(
        edge_kernel, "edges", [(hbm, ANY)], [struct(A, LY, LZ), struct(A, LX, LZ)],
        [pltpu.SemaphoreType.DMA, pltpu.SemaphoreType.DMA],
    )
    hx = shifted(fx.reshape(vx, LZ), "gx", -1)
    hy = shifted(fy.reshape(vy, LZ), "gy", -1)
    w, inv = call(
        weight_kernel, "weights", [stiffness, mass_matrix],
        [jax.ShapeDtypeStruct((2 * OUT, 3 * IN), bf16), struct(8, LZ)],
    )

    p0, *s = call(
        first_kernel, "first", [rhs2, hx, hy, k2, m2, w], [struct(ROWS, LZ)] + sends, upper[2:] + edges,
    )
    r = swap(s)
    v1, p1, *s = call(
        second_kernel, "second", [p0, *r, *s, k2, m2, w],
        [struct(ROWS, LZ), struct(ROWS, LZ)] + sends, upper + edges,
    )
    r = swap(s)
    sums, v1_kept = call(
        products_kernel, "products", [rhs2, v1], [struct(40, LZ), pltpu.HBM((ROWS, LZ), f32)], [pltpu.SemaphoreType.DMA],
    )
    peers = nx * ny * 2
    v2, p2, upx, upy, loads, mom = call(
        third_kernel, "third", [p1, v1, *r, *s, sums, k2, m2, w],
        [struct(ROWS, LZ)] * 2 + [struct(vx, LZ), struct(vy, LZ), struct(peers + 8, LZ), struct(peers, LZ)], upper,
    )
    table = [float(t) for t in jacobi_weights(nx)]
    group = [lax.ppermute(loads, "gx", [(i, i ^ b) for i in range(nx)]) for b in (1, 2, 3)]
    pieces = call(weigh_kernel, "weigh", [loads, *group], [struct(32, LZ)] * (nx // 4), table=table)
    coarse = [pieces[0]] + [shifted(p, "gx", 4 * z) for z, p in enumerate(pieces) if z]
    got = lax.all_to_all(mom.reshape(-1, 2, LZ), ("gx", "gy"), 0, 0, tiled=True).reshape(mom.shape)
    rx = shifted(upx, "gx", 1)
    ry = shifted(upy, "gy", 1)
    v0, v1_kept = (pltpu.with_memory_space_constraint(v, pltpu.HBM) for v in (rhs2, v1_kept))
    v0, v1, coef, edge = call(
        coefficients_kernel, "coefficients", [got, inv, (v0, ANY), (v1_kept, ANY)],
        [struct(ROWS, LZ)] * 2 + [struct(8, LZ), struct(LY, LZ)], [pltpu.SemaphoreType.DMA((2,))], table=table, ny=ny,
    )
    sol, res, coarse = call(
        last_kernel, "last", [(prolong, SM), coef, edge, *coarse, v0, v1, v2, p2, rx, ry],
        [pltpu.HBM((ROWS, LZ), f32)] * 2 + [struct(LY, LZ)],
        [pltpu.VMEM((ROWS, LZ), f32)] * 2 + [pltpu.SemaphoreType.DMA((6,))],
    )
    return sol.reshape(rhs.shape), res.reshape(rhs.shape), coarse[None]


def solution(mesh):
    placed = (
        P(None, None, "gx", "gy", None),
        P("gx", "gy", None),
        P("gx", "gy", None),
        P(),
        P(),
        P(),
    )
    return jax.shard_map(
        shards,
        mesh=mesh,
        in_specs=placed,
        out_specs=(
            P(None, None, "gx", "gy", None),
            P(None, None, "gx", "gy", None),
            P("gx", "gy", None),
        ),
        check_vma=False,
    )
```

```python
import jax
import jax.numpy as jnp
import numpy as np
from jax import lax
from jax.experimental import pallas as pl
from jax.experimental.pallas import tpu as pltpu
from jax.sharding import PartitionSpec as P

ITERS = 3
SWEEPS = 8
F, A = 3, 25
B = 24
LAST = 6 * B
OUT, IN = LAST + 8, LAST + 16
LX, LY, LZ = 4, 8, 128
CELLS = LX * LY
FACE = A * CELLS
ROWS = F * FACE
TAIL = F * CELLS * B
f32, bf16 = jnp.float32, jnp.bfloat16
VM = pl.BlockSpec(memory_space=pltpu.VMEM)
SM = pl.BlockSpec(memory_space=pltpu.SMEM)
ANY = pl.BlockSpec(memory_space=pl.ANY)


PARTS = (100, 100)


class Parts:
    def __init__(self, *refs):
        self.refs = refs

    def __getitem__(self, _):
        return jnp.concatenate([ref[...] for ref in self.refs], 0)

    def __setitem__(self, _, value):
        at = 0
        for ref in self.refs:
            ref[...] = value[at : at + ref.shape[0]]
            at += ref.shape[0]


def shifted(value, axis, by):
    n = lax.axis_size(axis)
    return lax.ppermute(value, axis, [(i, (i + by) % n) for i in range(n)])


def near_swap(value, axis):
    n = lax.axis_size(axis)
    return lax.ppermute(value, axis, [(i, i ^ 1) for i in range(n)])


def far_swap(value, axis):
    n = lax.axis_size(axis)
    pairs = [(i, (i + 1) % n) if i % 2 else (i, (i - 1) % n) for i in range(n)]
    return lax.ppermute(value, axis, pairs)


def halves(v):
    hi = v.astype(bf16)
    lo = (v - hi.astype(f32)).astype(bf16)
    return hi, lo


def apply_operator(v_ref, ux_ref, uy_ref, k_ref, m_ref, w_ref, out_ref, up_x, low_x, up_y, low_y, last_in, last_out, by_nodes=False):
    w_all = w_ref[...]
    at_first = lax.broadcasted_iota(jnp.int32, (LY, LZ), 0) == 0
    last_in[LAST // B * LY :] = jnp.zeros((2 * LY, LZ), f32)

    def block(ref, at, pitch, i):
        if by_nodes:
            return ref[pl.ds(at * A + i, B, stride=pitch), :]
        return ref[(at + i) * B : (at + i + 1) * B, :]

    def face(f, x, y):
        if f == 0 and x == LX:
            return block(ux_ref, 0, LY, y)
        if f == 1 and y == LY:
            return block(uy_ref, 0, LX, x)
        return block(v_ref, f * CELLS, CELLS, x * LY + y)

    def last_rows(f, x):
        if x == LX:
            return ux_ref[B * LY :, :]
        at = (f * FACE + B * CELLS if by_nodes else TAIL + f * CELLS) + x * LY
        return v_ref[at : at + LY, :]

    def put(f, x, y, value):
        at = (f * CELLS + x * LY + y) * B
        out_ref[at : at + B, :] = value

    def put_last(f, x, value):
        at = TAIL + f * CELLS + x * LY
        out_ref[at : at + LY, :] = value

    filler = jnp.zeros((IN - OUT, LZ), f32)
    carry = last_carry = None
    for x in range(LX):
        z_last = last_rows(2, x)
        y_last = last_rows(1, x)
        above = uy_ref[B * LX + x : B * LX + x + 1, :]
        top = lax.broadcasted_iota(jnp.int32, (LY, LZ), 0) == LY - 1
        y_up = jnp.where(top, jnp.broadcast_to(above, (LY, LZ)), pltpu.roll(y_last, LY - 1, 0))
        for j, tile in enumerate((last_rows(0, x), y_last, z_last, last_rows(0, x + 1), y_up, pltpu.roll(z_last, LZ - 1, 1))):
            last_in[j * LY : (j + 1) * LY] = tile
        columns = []
        for y in range(LY):
            z = face(2, x, y)
            six = [face(0, x, y), face(0, x + 1, y), face(1, x, y), face(1, x, y + 1), z, pltpu.roll(z, LZ - 1, 1)]
            columns.append(jnp.concatenate(six + [last_in[pl.ds(y, 8, stride=LY), :], filler], 0))
        hi, lo = halves(jnp.concatenate(columns, 1))
        prod = jnp.dot(w_all, jnp.concatenate([hi, lo, hi], 0), preferred_element_type=f32)
        parts = []
        for y in range(LY):
            k = k_ref[x * LY + y : x * LY + y + 1, :]
            m = m_ref[x * LY + y : x * LY + y + 1, :]
            cols = slice(y * LZ, (y + 1) * LZ)
            w = prod[:OUT, cols] * k + prod[OUT:, cols] * m
            parts.append([w[b * B : (b + 1) * B] for b in range(6)])
            last_out[pl.ds(y, 8, stride=LY), :] = w[LAST:]
        for y in range(LY):
            wlx, wux, wly, wuy, wlz, wuz = parts[y]
            put(0, x, y, wlx if x == 0 else wlx + carry[y])
            put(1, x, y, wly if y == 0 else wly + parts[y - 1][3])
            put(2, x, y, wlz + pltpu.roll(wuz, 1, 1))
            if x == 0 and low_x is not None:
                low_x[y * B : (y + 1) * B] = wlx
            if x == LX - 1:
                up_x[y * B : (y + 1) * B] = wux
        tiles = [last_out[j * LY : (j + 1) * LY] for j in range(6)]
        put_last(0, x, tiles[0] if x == 0 else tiles[0] + last_carry)
        put_last(1, x, tiles[1] + jnp.where(at_first, 0.0, pltpu.roll(tiles[4], 1, 0)))
        put_last(2, x, tiles[2] + pltpu.roll(tiles[5], 1, 1))
        if x == 0 and low_x is not None:
            low_x[B * LY :] = tiles[0]
        if x == LX - 1:
            up_x[B * LY :] = tiles[3]
        if low_y is not None:
            low_y[x * B : (x + 1) * B] = parts[0][2]
            low_y[B * LX + x : B * LX + x + 1] = tiles[1][:1]
        up_y[x * B : (x + 1) * B] = parts[LY - 1][3]
        up_y[B * LX + x : B * LX + x + 1] = tiles[4][LY - 1 :]
        carry = [parts[y][1] for y in range(LY)]
        last_carry = tiles[3]


def is_even(axis):
    return lax.rem(lax.axis_index(axis), 2) == 0


def route(even, up, low, near, far):
    near[...] = jnp.where(even, up[...], low[...])
    far[...] = jnp.where(even, low[...], up[...])


def edge_kernel(rhs_ref, fx_ref, fy_ref, sem_x, sem_y):
    face_x = pltpu.make_async_copy(rhs_ref.at[0, :, 0], fx_ref, sem_x)
    face_y = pltpu.make_async_copy(rhs_ref.at[1, :, :, 0], fy_ref, sem_y)
    face_x.start()
    face_y.start()
    face_x.wait()
    face_y.wait()


def weight_kernel(s_ref, m_ref, w_ref, inv_ref):
    n = 6 * A

    def placing(rows, span):
        r = lax.broadcasted_iota(jnp.int32, (rows, n), 0)
        c = lax.broadcasted_iota(jnp.int32, (rows, n), 1)
        p = lax.rem(r, span)
        j = p - LAST
        node = jnp.where(p < LAST, lax.div(p, B) * A + lax.rem(p, B), (2 * lax.rem(j, 3) + lax.div(j, 3)) * A + B)
        return (node == c) & (p < n), lax.div(r, span)

    def ones(mask):
        return jnp.where(mask, 1.0, 0.0).astype(bf16)

    rows = ones(placing(OUT, OUT)[0])
    mask, third = placing(3 * IN, IN)
    columns = (ones(mask & (third < 2)), ones(mask & (third == 2)))
    diagonal = lax.broadcasted_iota(jnp.int32, (n, n), 0) == lax.broadcasted_iota(jnp.int32, (n, n), 1)

    def largest(v):
        return jnp.max(jnp.max(jnp.where(diagonal, v, 0.0), 0, keepdims=True), 1, keepdims=True)

    inv = 1.0 / (10.0 * largest(s_ref[...]) + 2.0 * largest(m_ref[...]))
    inv_ref[...] = jnp.broadcast_to(inv, (8, LZ))
    for i, ref in enumerate((s_ref, m_ref)):
        full = 0.0
        for part, place in zip(halves(ref[...] * inv), columns):
            moved = jnp.dot(rows, part, preferred_element_type=f32).astype(bf16)
            full = full + lax.dot_general(moved, place, (((1,), (1,)), ((), ())), preferred_element_type=f32)
        w_ref[i * OUT : (i + 1) * OUT] = full.astype(bf16)


def first_kernel(rhs_ref, hx_ref, hy_ref, k_ref, m_ref, w_ref,
                 p_ref, sn0, sn1, sfx, sny, sfy, last_in, last_out, upx, lowx, upy, lowy):
    apply_operator(rhs_ref, hx_ref, hy_ref, k_ref, m_ref, w_ref, p_ref, upx, lowx, upy, lowy, last_in, last_out, True)
    route(is_even("gx"), upx, lowx, Parts(sn0, sn1), sfx)
    route(is_even("gy"), upy, lowy, sny, sfy)


def assemble(p_ref, snx, sfx, sny, sfy, rnx, rfx, rny, rfy, v, ux, uy):
    even_x = is_even("gx")
    even_y = is_even("gy")
    v[...] = p_ref[...]
    below_x = jnp.where(even_x, rfx[...], rnx[...])
    v[: B * LY] = v[: B * LY] + below_x[: B * LY]
    v[TAIL : TAIL + LY] = v[TAIL : TAIL + LY] + below_x[B * LY :]
    below_y = jnp.where(even_y, rfy[...], rny[...])
    for x in range(LX):
        at = (CELLS + x * LY) * B
        v[at : at + B] = v[at : at + B] + below_y[x * B : (x + 1) * B]
        at = TAIL + CELLS + x * LY
        v[at : at + 1] = v[at : at + 1] + below_y[B * LX + x : B * LX + x + 1]
    ux[...] = jnp.where(even_x, snx[...] + rnx[...], sfx[...] + rfx[...])
    uy[...] = jnp.where(even_y, sny[...] + rny[...], sfy[...] + rfy[...])


def node_sum(value):
    return jnp.sum(value.reshape(-1, LY, LZ), 0)


def row(tile):
    return jnp.sum(tile, 0, keepdims=True)


def second_kernel(p_ref, rfx, rfy, rny, rn0, rn1, sn0, sn1, sfx, sny, sfy, k_ref, m_ref, w_ref,
                  v1_ref, p1_ref, tn0, tn1, tfx, tny, tfy, ux, uy, last_in, last_out, upx, lowx, upy, lowy):
    assemble(p_ref, Parts(sn0, sn1), sfx, sny, sfy, Parts(rn0, rn1), rfx, rny, rfy, v1_ref, ux, uy)
    apply_operator(v1_ref, ux, uy, k_ref, m_ref, w_ref, p1_ref, upx, lowx, upy, lowy, last_in, last_out)
    route(is_even("gx"), upx, lowx, Parts(tn0, tn1), tfx)
    route(is_even("gy"), upy, lowy, tny, tfy)


def element_sum(ref, faces):
    rows = []
    for y in range(LY):
        total = 0.0
        for at in range(0, faces, LY):
            first = (at + y) * B
            total = total + (ref[first : first + 8] + ref[first + 8 : first + 16] + ref[first + 16 : first + B])
        rows.append(row(total))
    return jnp.concatenate(rows, 0) + node_sum(ref[faces * B :])


def tile_of(ref, faces, f, a, x):
    at = f * CELLS + x * LY
    if a == B:
        return ref[faces * B + at : faces * B + at + LY, :]
    return ref[pl.ds(at * B + a, LY, stride=B), :]


def products_kernel(v0_ref, v1_ref, sums_ref, v1_hbm, sem):
    keep = pltpu.make_async_copy(v1_ref, v1_hbm, sem)
    keep.start()
    s0 = s1 = s00 = s01 = s11 = 0.0
    for f in range(F):
        for a in range(A):
            for x in range(LX):
                at = (f * A + a) * CELLS + x * LY
                v0 = v0_ref[at : at + LY, :]
                v1 = tile_of(v1_ref, F * CELLS, f, a, x)
                s0, s1, s00, s01, s11 = s0 + v0, s1 + v1, s00 + v0 * v0, s01 + v0 * v1, s11 + v1 * v1
    for k, s in enumerate((s0, s1, s00, s01, s11)):
        sums_ref[8 * k : 8 * k + 8] = s
    keep.wait()


def third_kernel(p_ref, v1_ref, rfx, rfy, rny, rn0, rn1, sn0, sn1, sfx, sny, sfy, sums_ref, k_ref, m_ref, w_ref,
                 v2_ref, p2_ref, upx_out, upy_out, loads_ref, mom_ref, ux, uy, last_in, last_out):
    upx, upy = upx_out.at[: A * LY], upy_out.at[: A * LX]
    upx_out[A * LY :] = jnp.zeros((upx_out.shape[0] - A * LY, LZ), f32)
    upy_out[A * LX :] = jnp.zeros((upy_out.shape[0] - A * LX, LZ), f32)
    assemble(p_ref, Parts(sn0, sn1), sfx, sny, sfy, Parts(rn0, rn1), rfx, rny, rfy, v2_ref, ux, uy)
    v1 = v1_ref[...]
    v2 = v2_ref[...]
    loads_ref[0:16] = sums_ref[0:16]
    loads_ref[16:24] = element_sum(v2_ref, F * CELLS)
    m3 = node_sum(v1 * v2)
    m4 = node_sum(v2 * v2)
    apply_operator(v2_ref, ux, uy, k_ref, m_ref, w_ref, p2_ref, upx, None, upy, None, last_in, last_out)
    loads_ref[24:32] = element_sum(p2_ref, F * CELLS)
    loads_ref[32:40] = element_sum(upx, LY)
    energy = node_sum(v2_ref[...] * p2_ref[...]) + node_sum(ux[...] * upx[...])
    tail = row(uy[...] * upy[...])
    tile = jnp.concatenate(
        [row(sums_ref[16 + 8 * k : 24 + 8 * k]) for k in range(3)]
        + [row(m3), row(m4), row(energy) + tail, jnp.zeros((2, LZ), f32)], 0,
    )
    for lanes in (64, 32, 16):
        tile = tile + pltpu.roll(tile, lanes, 1)
    lane = lax.broadcasted_iota(jnp.int32, (8, LZ), 1)
    moment = lax.broadcasted_iota(jnp.int32, (8, LZ), 0)
    packed = row(jnp.where(lax.div(lane, 16) == moment, tile, 0.0))
    pair = jnp.concatenate([packed, row(upy[...])] * 4, 0)
    for at in range(0, mom_ref.shape[0], 8):
        mom_ref[at : at + 8] = pair
    loads_ref[40:] = jnp.zeros((loads_ref.shape[0] - 40, LZ), f32)


def weigh_kernel(own, near, far, both, *outs, table):
    nx = len(table)
    q = lax.rem(lax.axis_index("gx"), 4)
    low, high = lax.rem(q, 2) == 0, q < 2
    one, two = jnp.where(low, 1, -1), jnp.where(high, 2, -2)
    sources = ((own, 0, (0,)), (near, one, (1, -1)), (far, two, (2, -2)), (both, one + two, (3, 1, -1, -3)))

    def pick(at, shift, span):
        value = jnp.float32(table[(at - span[0]) % nx])
        for s in span[1:]:
            value = jnp.where(shift == s, table[(at - s) % nx], value)
        return value

    for z, out in enumerate(outs):
        total = [0.0] * 4
        for ref, shift, span in sources:
            w = pick(4 * z, shift, span)
            for k in range(4):
                total[k] = total[k] + ref[k * 8 : k * 8 + 8] * w
            total[3] = total[3] + ref[32:40] * pick(4 * z - 1, shift, span)
        for k in range(4):
            out[k * 8 : k * 8 + 8] = total[k]


def two_sum(a, b):
    s = a + b
    t = s - a
    return s, (a - (s - t)) + (b - t)


def pair_add(a, b):
    s, e = two_sum(a[0], b[0])
    e = e + (a[1] + b[1])
    h = s + e
    return h, e - (h - s)


def split(a):
    t = a * 4097.0
    h = t - (t - a)
    return h, a - h


def pair_times(a, c):
    p = a[0] * c
    ah, al = split(a[0])
    ch, cl = split(c)
    return p, ((ah * ch - p) + ah * cl + al * ch) + al * cl + a[1] * c


def moments(got):
    zero = jnp.zeros((8, LZ), f32)
    pairs = [(got[at : at + 8], zero) for at in range(0, got.shape[0], 8)]
    while len(pairs) > 1:
        pairs = [pair_add(a, b) for a, b in zip(pairs[::2], pairs[1::2])]
    h, l = pairs[0]
    rows = [(h[r : r + 1], l[r : r + 1]) for r in (0, 2, 4, 6)]
    t = pair_add(pair_add(rows[0], rows[1]), pair_add(rows[2], rows[3]))
    level = [t] + [tuple(pltpu.roll(p, LZ - 16 * k, 1) for p in t) for k in range(1, 6)]
    inside = lax.broadcasted_iota(jnp.int32, (1, LZ), 1) < 16

    def total(value):
        return jnp.sum(jnp.where(inside, value, 0.0), axis=1, keepdims=True)

    c = total(level[1][0]) / total(level[0][0])
    minus = jnp.broadcast_to(-c, (1, LZ))
    heads = [level[0]]
    while len(level) > 1:
        level = [pair_add(up, pair_times(at, minus)) for at, up in zip(level, level[1:])]
        heads.append(level[0])
    return c, [total(p[0] + p[1]) for p in heads]


def conjugate_gradient(c, m):
    def dot(a, b):
        s = None
        for i, ai in enumerate(a):
            for j, bj in enumerate(b):
                t = ai * bj * m[i + j]
                s = t if s is None else s + t
        return s

    def add(a, b, factor):
        longer = []
        for i in range(max(len(a), len(b))):
            if i >= len(b):
                longer.append(a[i])
            elif i >= len(a):
                longer.append(factor * b[i])
            else:
                longer.append(a[i] + factor * b[i])
        return longer

    def times(a, shift):
        return [a[0] * shift] + [a[i] * shift + a[i - 1] for i in range(1, len(a))] + [a[-1]]

    def plain(a):
        out = [a[-1]]
        for coefficient in a[-2::-1]:
            out = times(out, -c)
            out[0] = out[0] + coefficient
        return out

    one = jnp.ones((1, 1), f32)
    iterate, residual, direction = [], [one], [one]
    norm = m[0]
    for step in range(ITERS):
        img = times(direction, c)
        alpha = norm / dot(direction, img)
        iterate = add(iterate, direction, alpha)
        residual = add(residual, img, -alpha)
        if step < ITERS - 1:
            norm_next = dot(residual, residual)
            direction = add(residual, direction, norm_next / norm)
            norm = norm_next
    return plain(iterate), plain(residual)


def residual_kernel(got_ref, inv_ref, rhs_hbm, v1_hbm, v2_ref, p2_ref, rx_ref, ry_ref,
                    part_ref, res_hbm, coef_ref, edge_ref, rhs_ref, v1_ref, res_ref, in_sems, out_sems, *, table, ny):
    fetches = []
    for f in range(F):
        pairs = (
            (rhs_hbm, rhs_ref, pl.ds(f * FACE, FACE)),
            (v1_hbm, v1_ref, pl.ds(f * CELLS * B, CELLS * B)),
            (v1_hbm, v1_ref, pl.ds(TAIL + f * CELLS, CELLS)),
        )
        fetches.append([pltpu.make_async_copy(src.at[r], dst.at[r], in_sems.at[3 * f + i]) for i, (src, dst, r) in enumerate(pairs)])
        for fetch in fetches[f]:
            fetch.start()
    x, d = conjugate_gradient(*moments(got_ref[...]))
    inv = inv_ref[0:1, 0:1]
    x = [t * inv for t in x]
    for k, t in enumerate(d):
        coef_ref[k : k + 1] = jnp.broadcast_to(t, (1, LZ))
    coef_ref[4:8] = jnp.zeros((4, LZ), f32)
    below = lax.rem(lax.axis_index("gy") + ny - 1, ny)
    me = lax.axis_index("gx")
    nx = len(table)
    edge = jnp.zeros((1, LZ), f32)
    for offset, weight in enumerate(table):
        slab = lax.rem(me + nx - offset, nx)
        edge = edge + got_ref[pl.ds(2 * (slab * ny + below) + 1, 1), :] * weight
    edge_ref[...] = jnp.concatenate([edge, jnp.zeros((LY - 1, LZ), f32)], 0)
    x = [jnp.broadcast_to(t, (LY, LZ)) for t in x]
    d = [jnp.broadcast_to(t, (LY, LZ)) for t in d]
    stores = []
    for f in range(F):
        for fetch in fetches[f]:
            fetch.wait()
        for a in range(A):
            for cell in range(LX):
                at = (f * A + a) * CELLS + cell * LY
                rows = slice(at, at + LY)
                v0 = rhs_ref[rows, :]
                v1, v2, img = (tile_of(ref, F * CELLS, f, a, cell) for ref in (v1_ref, v2_ref, p2_ref))
                if f == 0 and cell == 0:
                    img = img + tile_of(rx_ref, LY, 0, a, 0)
                part_ref[rows, :] = x[0] * v0 + x[1] * v1 + x[2] * v2
                res_ref[rows, :] = d[0] * v0 + d[1] * v1 + d[2] * v2 + d[3] * img
        if f == 1:
            add = d[3][0:1] * ry_ref[: A * LX]
            for cell in range(LX):
                first = pl.ds(FACE + cell * LY, B, stride=CELLS)
                res_ref[first, :] = res_ref[first, :] + add[cell * B : (cell + 1) * B]
            first = pl.ds(FACE + B * CELLS, LX, stride=LY)
            res_ref[first, :] = res_ref[first, :] + add[B * LX :]
        rows = pl.ds(f * FACE, FACE)
        stores.append(pltpu.make_async_copy(res_ref.at[rows], res_hbm.at[rows], out_sems.at[f]))
        stores[-1].start()
    for store in stores:
        store.wait()


def last_kernel(prolong_ref, coef_ref, edge_ref, c0, c1, c2, c3, part_ref, sol_hbm, coarse_ref, sol_ref, out_sems):
    d = [jnp.broadcast_to(coef_ref[k : k + 1], (LY, LZ)) for k in range(4)]
    circ = [c0[k * 8 : k * 8 + 8] + c1[k * 8 : k * 8 + 8] + c2[k * 8 : k * 8 + 8] + c3[k * 8 : k * 8 + 8] for k in range(4)]
    coarse = d[0] * circ[0] + d[1] * circ[1] + d[2] * circ[2] + d[3] * (circ[3] + edge_ref[...])
    coarse_ref[...] = coarse
    stores = []
    for f in range(F):
        for a in range(A):
            at = (f * A + a) * CELLS
            spread = coarse * prolong_ref[f, a]
            for cell in range(LX):
                rows = slice(at + cell * LY, at + (cell + 1) * LY)
                sol_ref[rows, :] = part_ref[rows, :] + spread
        rows = pl.ds(f * FACE, FACE)
        stores.append(pltpu.make_async_copy(sol_ref.at[rows], sol_hbm.at[rows], out_sems.at[f]))
        stores[-1].start()
    for store in stores:
        store.wait()


def jacobi_weights(n):
    coarse = np.zeros(n)
    load = np.zeros(n)
    load[0] = 1.0
    for _ in range(SWEEPS):
        coarse = (load + np.roll(coarse, 1) + np.roll(coarse, -1)) / 2.2
    return coarse / 75.0


def struct(*shape):
    return jax.ShapeDtypeStruct(shape, f32)


PARAMS = pltpu.CompilerParams(vmem_limit_bytes=16 * 1024 * 1024)


def shards(rhs, kappa, mass, stiffness, mass_matrix, prolong):
    nx, ny = lax.axis_size("gx"), lax.axis_size("gy")
    vx, vy = A * LY, A * LX
    rhs2 = rhs.reshape(ROWS, LZ)
    k2 = kappa.reshape(CELLS, LZ)
    m2 = mass.reshape(CELLS, LZ)
    sends = [struct(n, LZ) for n in PARTS] + [struct(vx, LZ), struct(vy, LZ), struct(vy, LZ)]
    upper = [pltpu.VMEM((vx, LZ), f32), pltpu.VMEM((vy, LZ), f32)] + [pltpu.VMEM((8 * LY, LZ), f32)] * 2
    edges = [pltpu.VMEM((vx, LZ), f32)] * 2 + [pltpu.VMEM((vy, LZ), f32)] * 2

    def call(kernel, name, ins, outs, scratch=(), **static):
        specs = [i[1] if isinstance(i, tuple) else VM for i in ins]
        ins = [i[0] if isinstance(i, tuple) else i for i in ins]

        def bound(*refs):
            kernel(*refs, **static)

        return pl.pallas_call(
            bound,
            out_shape=outs,
            in_specs=specs,
            out_specs=[ANY if isinstance(o, pl.MemoryRef) else VM for o in outs],
            scratch_shapes=list(scratch),
            compiler_params=PARAMS,
            name=name,
        )(*ins)

    def swap(s):
        *near, far_x, near_y, far_y = s
        far_x = far_swap(far_x, "gx")
        far_y = far_swap(far_y, "gy")
        near_y = near_swap(near_y, "gy")
        return [far_x, far_y, near_y] + [near_swap(part, "gx") for part in near]

    hbm = pltpu.with_memory_space_constraint(rhs, pltpu.HBM)
    fx, fy = call(
        edge_kernel, "edges", [(hbm, ANY)], [struct(A, LY, LZ), struct(A, LX, LZ)],
        [pltpu.SemaphoreType.DMA, pltpu.SemaphoreType.DMA],
    )
    hx = shifted(fx.reshape(vx, LZ), "gx", -1)
    hy = shifted(fy.reshape(vy, LZ), "gy", -1)
    w, inv = call(
        weight_kernel, "weights", [stiffness, mass_matrix],
        [jax.ShapeDtypeStruct((2 * OUT, 3 * IN), bf16), struct(8, LZ)],
    )

    p0, *s = call(
        first_kernel, "first", [rhs2, hx, hy, k2, m2, w], [struct(ROWS, LZ)] + sends, upper[2:] + edges,
    )
    r = swap(s)
    v1, p1, *s = call(
        second_kernel, "second", [p0, *r, *s, k2, m2, w],
        [struct(ROWS, LZ), struct(ROWS, LZ)] + sends, upper + edges,
    )
    r = swap(s)
    sums, v1_kept = call(
        products_kernel, "products", [rhs2, v1], [struct(40, LZ), pltpu.HBM((ROWS, LZ), f32)], [pltpu.SemaphoreType.DMA],
    )
    peers = nx * ny * 2
    v2, p2, upx, upy, loads, mom = call(
        third_kernel, "third", [p1, v1, *r, *s, sums, k2, m2, w],
        [struct(ROWS, LZ)] * 2 + [struct(peers + 8, LZ)] * 3 + [struct(peers, LZ)], upper,
    )
    table = [float(t) for t in jacobi_weights(nx)]
    group = [lax.ppermute(loads, "gx", [(i, i ^ b) for i in range(nx)]) for b in (1, 2, 3)]
    pieces = call(weigh_kernel, "weigh", [loads, *group], [struct(32, LZ)] * (nx // 4), table=table)
    coarse = [pieces[0]] + [shifted(p, "gx", 4 * z) for z, p in enumerate(pieces) if z]
    got = lax.all_to_all(mom.reshape(-1, 2, LZ), ("gx", "gy"), 0, 0, tiled=True).reshape(mom.shape)
    rx = shifted(upx, "gx", 1)
    ry = shifted(upy, "gy", 1)
    v0, v1_kept = (pltpu.with_memory_space_constraint(v, pltpu.HBM) for v in (rhs2, v1_kept))
    part, res, coef, edge = call(
        residual_kernel, "residual", [got, inv, (v0, ANY), (v1_kept, ANY), v2, p2, rx, ry],
        [struct(ROWS, LZ), pltpu.HBM((ROWS, LZ), f32), struct(8, LZ), struct(LY, LZ)],
        [pltpu.VMEM((ROWS, LZ), f32)] * 3 + [pltpu.SemaphoreType.DMA((9,)), pltpu.SemaphoreType.DMA((F,))], table=table, ny=ny,
    )
    sol, coarse = call(
        last_kernel, "last", [(prolong, SM), coef, edge, *coarse, part],
        [pltpu.HBM((ROWS, LZ), f32), struct(LY, LZ)], [pltpu.VMEM((ROWS, LZ), f32), pltpu.SemaphoreType.DMA((F,))],
    )
    return sol.reshape(rhs.shape), res.reshape(rhs.shape), coarse[None]


def solution(mesh):
    placed = (
        P(None, None, "gx", "gy", None),
        P("gx", "gy", None),
        P("gx", "gy", None),
        P(),
        P(),
        P(),
    )
    return jax.shard_map(
        shards,
        mesh=mesh,
        in_specs=placed,
        out_specs=(
            P(None, None, "gx", "gy", None),
            P(None, None, "gx", "gy", None),
            P("gx", "gy", None),
        ),
        check_vma=False,
    )
```

```python
import jax
import jax.numpy as jnp
import numpy as np
from jax import lax
from jax.experimental import pallas as pl
from jax.experimental.pallas import tpu as pltpu
from jax.sharding import PartitionSpec as P

ITERS = 3
SWEEPS = 8
F, A = 3, 25
B = 24
LAST = 6 * B
OUT, IN = LAST + 8, LAST + 16
LX, LY, LZ = 4, 8, 128
CELLS = LX * LY
FACE = A * CELLS
ROWS = F * FACE
LOADS = 40
TAIL = F * CELLS * B
f32, bf16 = jnp.float32, jnp.bfloat16
VM = pl.BlockSpec(memory_space=pltpu.VMEM)
SM = pl.BlockSpec(memory_space=pltpu.SMEM)
ANY = pl.BlockSpec(memory_space=pl.ANY)


PARTS = (100, 100)


class Parts:
    def __init__(self, *refs):
        self.refs = refs

    def __getitem__(self, _):
        return jnp.concatenate([ref[...] for ref in self.refs], 0)

    def __setitem__(self, _, value):
        at = 0
        for ref in self.refs:
            ref[...] = value[at : at + ref.shape[0]]
            at += ref.shape[0]


def shifted(value, axis, by):
    n = lax.axis_size(axis)
    return lax.ppermute(value, axis, [(i, (i + by) % n) for i in range(n)])


def near_swap(value, axis):
    n = lax.axis_size(axis)
    return lax.ppermute(value, axis, [(i, i ^ 1) for i in range(n)])


def far_swap(value, axis):
    n = lax.axis_size(axis)
    pairs = [(i, (i + 1) % n) if i % 2 else (i, (i - 1) % n) for i in range(n)]
    return lax.ppermute(value, axis, pairs)


def halves(v):
    hi = v.astype(bf16)
    lo = (v - hi.astype(f32)).astype(bf16)
    return hi, lo


def apply_operator(v_ref, ux_ref, uy_ref, k_ref, m_ref, w_ref, out_ref, up_x, low_x, up_y, low_y, last_in, last_out, by_nodes=False):
    w_all = w_ref[...]
    at_first = lax.broadcasted_iota(jnp.int32, (LY, LZ), 0) == 0
    last_in[LAST // B * LY :] = jnp.zeros((2 * LY, LZ), f32)

    def block(ref, at, pitch, i):
        if by_nodes:
            return ref[pl.ds(at * A + i, B, stride=pitch), :]
        return ref[(at + i) * B : (at + i + 1) * B, :]

    def face(f, x, y):
        if f == 0 and x == LX:
            return block(ux_ref, 0, LY, y)
        if f == 1 and y == LY:
            return block(uy_ref, 0, LX, x)
        return block(v_ref, f * CELLS, CELLS, x * LY + y)

    def last_rows(f, x):
        if x == LX:
            return ux_ref[B * LY :, :]
        at = (f * FACE + B * CELLS if by_nodes else TAIL + f * CELLS) + x * LY
        return v_ref[at : at + LY, :]

    def put(f, x, y, value):
        at = (f * CELLS + x * LY + y) * B
        out_ref[at : at + B, :] = value

    def put_last(f, x, value):
        at = TAIL + f * CELLS + x * LY
        out_ref[at : at + LY, :] = value

    filler = jnp.zeros((IN - OUT, LZ), f32)
    carry = last_carry = None
    for x in range(LX):
        z_last = last_rows(2, x)
        y_last = last_rows(1, x)
        above = uy_ref[B * LX + x : B * LX + x + 1, :]
        top = lax.broadcasted_iota(jnp.int32, (LY, LZ), 0) == LY - 1
        y_up = jnp.where(top, jnp.broadcast_to(above, (LY, LZ)), pltpu.roll(y_last, LY - 1, 0))
        for j, tile in enumerate((last_rows(0, x), y_last, z_last, last_rows(0, x + 1), y_up, pltpu.roll(z_last, LZ - 1, 1))):
            last_in[j * LY : (j + 1) * LY] = tile
        columns = []
        for y in range(LY):
            z = face(2, x, y)
            six = [face(0, x, y), face(0, x + 1, y), face(1, x, y), face(1, x, y + 1), z, pltpu.roll(z, LZ - 1, 1)]
            columns.append(jnp.concatenate(six + [last_in[pl.ds(y, 8, stride=LY), :], filler], 0))
        hi, lo = halves(jnp.concatenate(columns, 1))
        prod = jnp.dot(w_all, jnp.concatenate([hi, lo, hi], 0), preferred_element_type=f32)
        parts = []
        for y in range(LY):
            k = k_ref[x * LY + y : x * LY + y + 1, :]
            m = m_ref[x * LY + y : x * LY + y + 1, :]
            cols = slice(y * LZ, (y + 1) * LZ)
            w = prod[:OUT, cols] * k + prod[OUT:, cols] * m
            parts.append([w[b * B : (b + 1) * B] for b in range(6)])
            last_out[pl.ds(y, 8, stride=LY), :] = w[LAST:]
        for y in range(LY):
            wlx, wux, wly, wuy, wlz, wuz = parts[y]
            put(0, x, y, wlx if x == 0 else wlx + carry[y])
            put(1, x, y, wly if y == 0 else wly + parts[y - 1][3])
            put(2, x, y, wlz + pltpu.roll(wuz, 1, 1))
            if x == 0 and low_x is not None:
                low_x[y * B : (y + 1) * B] = wlx
            if x == LX - 1:
                up_x[y * B : (y + 1) * B] = wux
        tiles = [last_out[j * LY : (j + 1) * LY] for j in range(6)]
        put_last(0, x, tiles[0] if x == 0 else tiles[0] + last_carry)
        put_last(1, x, tiles[1] + jnp.where(at_first, 0.0, pltpu.roll(tiles[4], 1, 0)))
        put_last(2, x, tiles[2] + pltpu.roll(tiles[5], 1, 1))
        if x == 0 and low_x is not None:
            low_x[B * LY :] = tiles[0]
        if x == LX - 1:
            up_x[B * LY :] = tiles[3]
        if low_y is not None:
            low_y[x * B : (x + 1) * B] = parts[0][2]
            low_y[B * LX + x : B * LX + x + 1] = tiles[1][:1]
        up_y[x * B : (x + 1) * B] = parts[LY - 1][3]
        up_y[B * LX + x : B * LX + x + 1] = tiles[4][LY - 1 :]
        carry = [parts[y][1] for y in range(LY)]
        last_carry = tiles[3]


def is_even(axis):
    return lax.rem(lax.axis_index(axis), 2) == 0


def route(even, up, low, near, far):
    near[...] = jnp.where(even, up[...], low[...])
    far[...] = jnp.where(even, low[...], up[...])


def edge_kernel(rhs_ref, fx_ref, fy_ref, sem_x, sem_y):
    face_x = pltpu.make_async_copy(rhs_ref.at[0, :, 0], fx_ref, sem_x)
    face_y = pltpu.make_async_copy(rhs_ref.at[1, :, :, 0], fy_ref, sem_y)
    face_x.start()
    face_y.start()
    face_x.wait()
    face_y.wait()


def weight_kernel(s_ref, m_ref, w_ref, inv_ref):
    n = 6 * A

    def placing(rows, span):
        r = lax.broadcasted_iota(jnp.int32, (rows, n), 0)
        c = lax.broadcasted_iota(jnp.int32, (rows, n), 1)
        p = lax.rem(r, span)
        j = p - LAST
        node = jnp.where(p < LAST, lax.div(p, B) * A + lax.rem(p, B), (2 * lax.rem(j, 3) + lax.div(j, 3)) * A + B)
        return (node == c) & (p < n), lax.div(r, span)

    def ones(mask):
        return jnp.where(mask, 1.0, 0.0).astype(bf16)

    rows = ones(placing(OUT, OUT)[0])
    mask, third = placing(3 * IN, IN)
    columns = (ones(mask & (third < 2)), ones(mask & (third == 2)))
    diagonal = lax.broadcasted_iota(jnp.int32, (n, n), 0) == lax.broadcasted_iota(jnp.int32, (n, n), 1)

    def largest(v):
        return jnp.max(jnp.max(jnp.where(diagonal, v, 0.0), 0, keepdims=True), 1, keepdims=True)

    inv = 1.0 / (10.0 * largest(s_ref[...]) + 2.0 * largest(m_ref[...]))
    inv_ref[...] = jnp.broadcast_to(inv, (8, LZ))
    for i, ref in enumerate((s_ref, m_ref)):
        full = 0.0
        for part, place in zip(halves(ref[...] * inv), columns):
            moved = jnp.dot(rows, part, preferred_element_type=f32).astype(bf16)
            full = full + lax.dot_general(moved, place, (((1,), (1,)), ((), ())), preferred_element_type=f32)
        w_ref[i * OUT : (i + 1) * OUT] = full.astype(bf16)


def first_kernel(rhs_ref, hx_ref, hy_ref, k_ref, m_ref, w_ref,
                 p_ref, sn0, sn1, sfx, sny, sfy, last_in, last_out, upx, lowx, upy, lowy):
    apply_operator(rhs_ref, hx_ref, hy_ref, k_ref, m_ref, w_ref, p_ref, upx, lowx, upy, lowy, last_in, last_out, True)
    route(is_even("gx"), upx, lowx, Parts(sn0, sn1), sfx)
    route(is_even("gy"), upy, lowy, sny, sfy)


def assemble(p_ref, snx, sfx, sny, sfy, rnx, rfx, rny, rfy, v, ux, uy):
    even_x = is_even("gx")
    even_y = is_even("gy")
    v[...] = p_ref[...]
    below_x = jnp.where(even_x, rfx[...], rnx[...])
    v[: B * LY] = v[: B * LY] + below_x[: B * LY]
    v[TAIL : TAIL + LY] = v[TAIL : TAIL + LY] + below_x[B * LY :]
    below_y = jnp.where(even_y, rfy[...], rny[...])
    for x in range(LX):
        at = (CELLS + x * LY) * B
        v[at : at + B] = v[at : at + B] + below_y[x * B : (x + 1) * B]
        at = TAIL + CELLS + x * LY
        v[at : at + 1] = v[at : at + 1] + below_y[B * LX + x : B * LX + x + 1]
    ux[...] = jnp.where(even_x, snx[...] + rnx[...], sfx[...] + rfx[...])
    uy[...] = jnp.where(even_y, sny[...] + rny[...], sfy[...] + rfy[...])


def node_sum(value):
    return jnp.sum(value.reshape(-1, LY, LZ), 0)


def row(tile):
    return jnp.sum(tile, 0, keepdims=True)


def second_kernel(p_ref, rfx, rfy, rny, rn0, rn1, sn0, sn1, sfx, sny, sfy, k_ref, m_ref, w_ref,
                  v1_ref, p1_ref, tn0, tn1, tfx, tny, tfy, ux, uy, last_in, last_out, upx, lowx, upy, lowy):
    assemble(p_ref, Parts(sn0, sn1), sfx, sny, sfy, Parts(rn0, rn1), rfx, rny, rfy, v1_ref, ux, uy)
    apply_operator(v1_ref, ux, uy, k_ref, m_ref, w_ref, p1_ref, upx, lowx, upy, lowy, last_in, last_out)
    route(is_even("gx"), upx, lowx, Parts(tn0, tn1), tfx)
    route(is_even("gy"), upy, lowy, tny, tfy)


def element_sum(ref, faces):
    rows = []
    for y in range(LY):
        total = 0.0
        for at in range(0, faces, LY):
            first = (at + y) * B
            total = total + (ref[first : first + 8] + ref[first + 8 : first + 16] + ref[first + 16 : first + B])
        rows.append(row(total))
    return jnp.concatenate(rows, 0) + node_sum(ref[faces * B :])


def tile_of(ref, faces, f, a, x):
    at = f * CELLS + x * LY
    if a == B:
        return ref[faces * B + at : faces * B + at + LY, :]
    return ref[pl.ds(at * B + a, LY, stride=B), :]


def products_kernel(v0_ref, v1_ref, sums_ref, v1_hbm, sem):
    keep = pltpu.make_async_copy(v1_ref, v1_hbm, sem)
    keep.start()
    s0 = s1 = s00 = s01 = s11 = 0.0
    for f in range(F):
        for a in range(A):
            for x in range(LX):
                at = (f * A + a) * CELLS + x * LY
                v0 = v0_ref[at : at + LY, :]
                v1 = tile_of(v1_ref, F * CELLS, f, a, x)
                s0, s1, s00, s01, s11 = s0 + v0, s1 + v1, s00 + v0 * v0, s01 + v0 * v1, s11 + v1 * v1
    for k, s in enumerate((s0, s1, s00, s01, s11)):
        sums_ref[8 * k : 8 * k + 8] = s
    keep.wait()


def third_kernel(p_ref, v1_ref, rfx, rfy, rny, rn0, rn1, sn0, sn1, sfx, sny, sfy, sums_ref, k_ref, m_ref, w_ref,
                 v2_ref, p2_ref, upy, loads_ref, mom_ref, ux, uy, last_in, last_out):
    upx = loads_ref.at[LOADS : LOADS + A * LY]
    assemble(p_ref, Parts(sn0, sn1), sfx, sny, sfy, Parts(rn0, rn1), rfx, rny, rfy, v2_ref, ux, uy)
    v1 = v1_ref[...]
    v2 = v2_ref[...]
    loads_ref[0:16] = sums_ref[0:16]
    loads_ref[16:24] = element_sum(v2_ref, F * CELLS)
    m3 = node_sum(v1 * v2)
    m4 = node_sum(v2 * v2)
    apply_operator(v2_ref, ux, uy, k_ref, m_ref, w_ref, p2_ref, upx, None, upy, None, last_in, last_out)
    loads_ref[24:32] = element_sum(p2_ref, F * CELLS)
    loads_ref[32:40] = element_sum(upx, LY)
    energy = node_sum(v2_ref[...] * p2_ref[...]) + node_sum(ux[...] * upx[...])
    tail = row(uy[...] * upy[...])
    tile = jnp.concatenate(
        [row(sums_ref[16 + 8 * k : 24 + 8 * k]) for k in range(3)]
        + [row(m3), row(m4), row(energy) + tail, jnp.zeros((2, LZ), f32)], 0,
    )
    for lanes in (64, 32, 16):
        tile = tile + pltpu.roll(tile, lanes, 1)
    lane = lax.broadcasted_iota(jnp.int32, (8, LZ), 1)
    moment = lax.broadcasted_iota(jnp.int32, (8, LZ), 0)
    packed = row(jnp.where(lax.div(lane, 16) == moment, tile, 0.0))
    pair = jnp.concatenate([packed, row(upy[...])] * 4, 0)
    for at in range(0, mom_ref.shape[0], 8):
        mom_ref[at : at + 8] = pair
    used = LOADS + A * LY
    loads_ref[used:] = jnp.zeros((loads_ref.shape[0] - used, LZ), f32)


def weigh_kernel(own, below, above, second_above, *outs, table):
    nx = len(table)
    for z, out in enumerate(outs):
        total = [0.0] * 4
        for ref, at in ((own, 0), (below, -1), (above, 1), (second_above, 2)):
            for k in range(4):
                total[k] = total[k] + ref[k * 8 : k * 8 + 8] * table[(4 * z - at) % nx]
            total[3] = total[3] + ref[32:40] * table[(4 * z - at - 1) % nx]
        for k in range(4):
            out[k * 8 : k * 8 + 8] = total[k]


def two_sum(a, b):
    s = a + b
    t = s - a
    return s, (a - (s - t)) + (b - t)


def pair_add(a, b):
    s, e = two_sum(a[0], b[0])
    e = e + (a[1] + b[1])
    h = s + e
    return h, e - (h - s)


def split(a):
    t = a * 4097.0
    h = t - (t - a)
    return h, a - h


def pair_times(a, c):
    p = a[0] * c
    ah, al = split(a[0])
    ch, cl = split(c)
    return p, ((ah * ch - p) + ah * cl + al * ch) + al * cl + a[1] * c


def moments(got):
    zero = jnp.zeros((8, LZ), f32)
    pairs = [(got[at : at + 8], zero) for at in range(0, got.shape[0], 8)]
    while len(pairs) > 1:
        pairs = [pair_add(a, b) for a, b in zip(pairs[::2], pairs[1::2])]
    h, l = pairs[0]
    rows = [(h[r : r + 1], l[r : r + 1]) for r in (0, 2, 4, 6)]
    t = pair_add(pair_add(rows[0], rows[1]), pair_add(rows[2], rows[3]))
    level = [t] + [tuple(pltpu.roll(p, LZ - 16 * k, 1) for p in t) for k in range(1, 6)]
    inside = lax.broadcasted_iota(jnp.int32, (1, LZ), 1) < 16

    def total(value):
        return jnp.sum(jnp.where(inside, value, 0.0), axis=1, keepdims=True)

    c = total(level[1][0]) / total(level[0][0])
    minus = jnp.broadcast_to(-c, (1, LZ))
    heads = [level[0]]
    while len(level) > 1:
        level = [pair_add(up, pair_times(at, minus)) for at, up in zip(level, level[1:])]
        heads.append(level[0])
    return c, [total(p[0] + p[1]) for p in heads]


def conjugate_gradient(c, m):
    def dot(a, b):
        s = None
        for i, ai in enumerate(a):
            for j, bj in enumerate(b):
                t = ai * bj * m[i + j]
                s = t if s is None else s + t
        return s

    def add(a, b, factor):
        longer = []
        for i in range(max(len(a), len(b))):
            if i >= len(b):
                longer.append(a[i])
            elif i >= len(a):
                longer.append(factor * b[i])
            else:
                longer.append(a[i] + factor * b[i])
        return longer

    def times(a, shift):
        return [a[0] * shift] + [a[i] * shift + a[i - 1] for i in range(1, len(a))] + [a[-1]]

    def plain(a):
        out = [a[-1]]
        for coefficient in a[-2::-1]:
            out = times(out, -c)
            out[0] = out[0] + coefficient
        return out

    one = jnp.ones((1, 1), f32)
    iterate, residual, direction = [], [one], [one]
    norm = m[0]
    for step in range(ITERS):
        img = times(direction, c)
        alpha = norm / dot(direction, img)
        iterate = add(iterate, direction, alpha)
        residual = add(residual, img, -alpha)
        if step < ITERS - 1:
            norm_next = dot(residual, residual)
            direction = add(residual, direction, norm_next / norm)
            norm = norm_next
    return plain(iterate), plain(residual)


def coefficients_kernel(got_ref, inv_ref, rhs_hbm, v1_hbm, rhs_ref, v1_ref, coef_ref, edge_ref, sems, *, table, ny):
    fetches = [pltpu.make_async_copy(rhs_hbm, rhs_ref, sems.at[0]), pltpu.make_async_copy(v1_hbm, v1_ref, sems.at[1])]
    for fetch in fetches:
        fetch.start()
    x, d = conjugate_gradient(*moments(got_ref[...]))
    inv = inv_ref[0:1, 0:1]
    for k, t in enumerate([t * inv for t in x] + d):
        coef_ref[k : k + 1] = jnp.broadcast_to(t, (1, LZ))
    coef_ref[7:8] = jnp.zeros((1, LZ), f32)
    below = lax.rem(lax.axis_index("gy") + ny - 1, ny)
    me = lax.axis_index("gx")
    nx = len(table)
    edge = jnp.zeros((1, LZ), f32)
    for offset, weight in enumerate(table):
        slab = lax.rem(me + nx - offset, nx)
        edge = edge + got_ref[pl.ds(2 * (slab * ny + below) + 1, 1), :] * weight
    edge_ref[...] = jnp.concatenate([edge, jnp.zeros((LY - 1, LZ), f32)], 0)
    for fetch in fetches:
        fetch.wait()


def last_kernel(prolong_ref, coef_ref, edge_ref, c0, c1, c2, c3, rhs_ref, v1_ref, v2_ref, p2_ref, below_ref, ry_ref,
                sol_hbm, res_hbm, coarse_ref, sol_ref, res_ref, out_sems):
    rx_ref = below_ref.at[LOADS : LOADS + A * LY]
    coef = [jnp.broadcast_to(coef_ref[k : k + 1], (LY, LZ)) for k in range(7)]
    x, d = coef[:3], coef[3:]
    circ = [c0[k * 8 : k * 8 + 8] + c1[k * 8 : k * 8 + 8] + c2[k * 8 : k * 8 + 8] + c3[k * 8 : k * 8 + 8] for k in range(4)]
    coarse = d[0] * circ[0] + d[1] * circ[1] + d[2] * circ[2] + d[3] * (circ[3] + edge_ref[...])
    coarse_ref[...] = coarse
    stores = []
    for f in range(F):
        for a in range(A):
            at = (f * A + a) * CELLS
            spread = coarse * prolong_ref[f, a]
            for cell in range(LX):
                rows = slice(at + cell * LY, at + (cell + 1) * LY)
                v0 = rhs_ref[rows, :]
                v1, v2, img = (tile_of(ref, F * CELLS, f, a, cell) for ref in (v1_ref, v2_ref, p2_ref))
                if f == 0 and cell == 0:
                    img = img + tile_of(rx_ref, LY, 0, a, 0)
                sol_ref[rows, :] = x[0] * v0 + x[1] * v1 + x[2] * v2 + spread
                res_ref[rows, :] = d[0] * v0 + d[1] * v1 + d[2] * v2 + d[3] * img
        if f == 1:
            below = d[3][0:1] * ry_ref[...]
            for cell in range(LX):
                first = pl.ds(FACE + cell * LY, B, stride=CELLS)
                res_ref[first, :] = res_ref[first, :] + below[cell * B : (cell + 1) * B]
            first = pl.ds(FACE + B * CELLS, LX, stride=LY)
            res_ref[first, :] = res_ref[first, :] + below[B * LX :]
        rows = pl.ds(f * FACE, FACE)
        for i, (src, dst) in enumerate(((sol_ref, sol_hbm), (res_ref, res_hbm))):
            stores.append(pltpu.make_async_copy(src.at[rows], dst.at[rows], out_sems.at[2 * f + i]))
            stores[-1].start()
    for store in stores:
        store.wait()


def jacobi_weights(n):
    coarse = np.zeros(n)
    load = np.zeros(n)
    load[0] = 1.0
    for _ in range(SWEEPS):
        coarse = (load + np.roll(coarse, 1) + np.roll(coarse, -1)) / 2.2
    return coarse / 75.0


def struct(*shape):
    return jax.ShapeDtypeStruct(shape, f32)


PARAMS = pltpu.CompilerParams(vmem_limit_bytes=16 * 1024 * 1024)


def shards(rhs, kappa, mass, stiffness, mass_matrix, prolong):
    nx, ny = lax.axis_size("gx"), lax.axis_size("gy")
    vx, vy = A * LY, A * LX
    rhs2 = rhs.reshape(ROWS, LZ)
    k2 = kappa.reshape(CELLS, LZ)
    m2 = mass.reshape(CELLS, LZ)
    sends = [struct(n, LZ) for n in PARTS] + [struct(vx, LZ), struct(vy, LZ), struct(vy, LZ)]
    upper = [pltpu.VMEM((vx, LZ), f32), pltpu.VMEM((vy, LZ), f32)] + [pltpu.VMEM((8 * LY, LZ), f32)] * 2
    edges = [pltpu.VMEM((vx, LZ), f32)] * 2 + [pltpu.VMEM((vy, LZ), f32)] * 2

    def call(kernel, name, ins, outs, scratch=(), **static):
        specs = [i[1] if isinstance(i, tuple) else VM for i in ins]
        ins = [i[0] if isinstance(i, tuple) else i for i in ins]

        def bound(*refs):
            kernel(*refs, **static)

        return pl.pallas_call(
            bound,
            out_shape=outs,
            in_specs=specs,
            out_specs=[ANY if isinstance(o, pl.MemoryRef) else VM for o in outs],
            scratch_shapes=list(scratch),
            compiler_params=PARAMS,
            name=name,
        )(*ins)

    def swap(s):
        *near, far_x, near_y, far_y = s
        far_x = far_swap(far_x, "gx")
        far_y = far_swap(far_y, "gy")
        near_y = near_swap(near_y, "gy")
        return [far_x, far_y, near_y] + [near_swap(part, "gx") for part in near]

    hbm = pltpu.with_memory_space_constraint(rhs, pltpu.HBM)
    fx, fy = call(
        edge_kernel, "edges", [(hbm, ANY)], [struct(A, LY, LZ), struct(A, LX, LZ)],
        [pltpu.SemaphoreType.DMA, pltpu.SemaphoreType.DMA],
    )
    hx = shifted(fx.reshape(vx, LZ), "gx", -1)
    hy = shifted(fy.reshape(vy, LZ), "gy", -1)
    w, inv = call(
        weight_kernel, "weights", [stiffness, mass_matrix],
        [jax.ShapeDtypeStruct((2 * OUT, 3 * IN), bf16), struct(8, LZ)],
    )

    p0, *s = call(
        first_kernel, "first", [rhs2, hx, hy, k2, m2, w], [struct(ROWS, LZ)] + sends, upper[2:] + edges,
    )
    r = swap(s)
    v1, p1, *s = call(
        second_kernel, "second", [p0, *r, *s, k2, m2, w],
        [struct(ROWS, LZ), struct(ROWS, LZ)] + sends, upper + edges,
    )
    r = swap(s)
    sums, v1_kept = call(
        products_kernel, "products", [rhs2, v1], [struct(40, LZ), pltpu.HBM((ROWS, LZ), f32)], [pltpu.SemaphoreType.DMA],
    )
    peers = nx * ny * 2
    v2, p2, upy, loads, mom = call(
        third_kernel, "third", [p1, v1, *r, *s, sums, k2, m2, w],
        [struct(ROWS, LZ)] * 2 + [struct(vy, LZ), struct(max(peers + 8, LOADS + vx), LZ), struct(peers, LZ)], upper,
    )
    table = [float(t) for t in jacobi_weights(nx)]
    window = [shifted(loads, "gx", by) for by in (1, -1, -2)]
    pieces = call(weigh_kernel, "weigh", [loads, *window], [struct(32, LZ)] * (nx // 4), table=table)
    coarse = [pieces[0]] + [shifted(p, "gx", 4 * z) for z, p in enumerate(pieces) if z]
    got = lax.all_to_all(mom.reshape(-1, 2, LZ), ("gx", "gy"), 0, 0, tiled=True).reshape(mom.shape)
    ry = shifted(upy, "gy", 1)
    v0, v1_kept = (pltpu.with_memory_space_constraint(v, pltpu.HBM) for v in (rhs2, v1_kept))
    v0, v1, coef, edge = call(
        coefficients_kernel, "coefficients", [got, inv, (v0, ANY), (v1_kept, ANY)],
        [struct(ROWS, LZ)] * 2 + [struct(8, LZ), struct(LY, LZ)], [pltpu.SemaphoreType.DMA((2,))], table=table, ny=ny,
    )
    sol, res, coarse = call(
        last_kernel, "last", [(prolong, SM), coef, edge, *coarse, v0, v1, v2, p2, window[0], ry],
        [pltpu.HBM((ROWS, LZ), f32)] * 2 + [struct(LY, LZ)],
        [pltpu.VMEM((ROWS, LZ), f32)] * 2 + [pltpu.SemaphoreType.DMA((6,))],
    )
    return sol.reshape(rhs.shape), res.reshape(rhs.shape), coarse[None]


def solution(mesh):
    placed = (
        P(None, None, "gx", "gy", None),
        P("gx", "gy", None),
        P("gx", "gy", None),
        P(),
        P(),
        P(),
    )
    return jax.shard_map(
        shards,
        mesh=mesh,
        in_specs=placed,
        out_specs=(
            P(None, None, "gx", "gy", None),
            P(None, None, "gx", "gy", None),
            P("gx", "gy", None),
        ),
        check_vma=False,
    )
```

```python
import jax
import jax.numpy as jnp
import numpy as np
from jax import lax
from jax.experimental import pallas as pl
from jax.experimental.pallas import tpu as pltpu
from jax.sharding import PartitionSpec as P

ITERS = 3
SWEEPS = 8
F, A = 3, 25
B = 24
LAST = 6 * B
OUT, IN = LAST + 8, LAST + 16
LX, LY, LZ = 4, 8, 128
CELLS = LX * LY
FACE = A * CELLS
ROWS = F * FACE
HALF, SHORT = LZ // 2, LZ // 2 + 8
TAIL = F * CELLS * B
f32, bf16 = jnp.float32, jnp.bfloat16
VM = pl.BlockSpec(memory_space=pltpu.VMEM)
SM = pl.BlockSpec(memory_space=pltpu.SMEM)
ANY = pl.BlockSpec(memory_space=pl.ANY)


PARTS = (100, 100)


class Parts:
    def __init__(self, *refs):
        self.refs = refs

    def __getitem__(self, _):
        return jnp.concatenate([ref[...] for ref in self.refs], 0)

    def __setitem__(self, _, value):
        at = 0
        for ref in self.refs:
            ref[...] = value[at : at + ref.shape[0]]
            at += ref.shape[0]


def shifted(value, axis, by):
    n = lax.axis_size(axis)
    return lax.ppermute(value, axis, [(i, (i + by) % n) for i in range(n)])


def near_swap(value, axis):
    n = lax.axis_size(axis)
    return lax.ppermute(value, axis, [(i, i ^ 1) for i in range(n)])


def far_swap(value, axis):
    n = lax.axis_size(axis)
    pairs = [(i, (i + 1) % n) if i % 2 else (i, (i - 1) % n) for i in range(n)]
    return lax.ppermute(value, axis, pairs)


def halves(v):
    hi = v.astype(bf16)
    lo = (v - hi.astype(f32)).astype(bf16)
    return hi, lo


def apply_operator(v_ref, ux_ref, uy_ref, k_ref, m_ref, w_ref, out_ref, up_x, low_x, up_y, low_y, last_in, last_out, by_nodes=False):
    w_all = w_ref[...]
    at_first = lax.broadcasted_iota(jnp.int32, (LY, LZ), 0) == 0
    last_in[LAST // B * LY :] = jnp.zeros((2 * LY, LZ), f32)

    def block(ref, at, pitch, i):
        if by_nodes:
            return ref[pl.ds(at * A + i, B, stride=pitch), :]
        return ref[(at + i) * B : (at + i + 1) * B, :]

    def face(f, x, y):
        if f == 0 and x == LX:
            return block(ux_ref, 0, LY, y)
        if f == 1 and y == LY:
            return block(uy_ref, 0, LX, x)
        return block(v_ref, f * CELLS, CELLS, x * LY + y)

    def last_rows(f, x):
        if x == LX:
            return ux_ref[B * LY :, :]
        at = (f * FACE + B * CELLS if by_nodes else TAIL + f * CELLS) + x * LY
        return v_ref[at : at + LY, :]

    def put(f, x, y, value):
        at = (f * CELLS + x * LY + y) * B
        out_ref[at : at + B, :] = value

    def put_last(f, x, value):
        at = TAIL + f * CELLS + x * LY
        out_ref[at : at + LY, :] = value

    filler = jnp.zeros((IN - OUT, LZ), f32)
    carry = last_carry = None
    for x in range(LX):
        z_last = last_rows(2, x)
        y_last = last_rows(1, x)
        above = uy_ref[B * LX + x : B * LX + x + 1, :]
        top = lax.broadcasted_iota(jnp.int32, (LY, LZ), 0) == LY - 1
        y_up = jnp.where(top, jnp.broadcast_to(above, (LY, LZ)), pltpu.roll(y_last, LY - 1, 0))
        for j, tile in enumerate((last_rows(0, x), y_last, z_last, last_rows(0, x + 1), y_up, pltpu.roll(z_last, LZ - 1, 1))):
            last_in[j * LY : (j + 1) * LY] = tile
        columns = []
        for y in range(LY):
            z = face(2, x, y)
            six = [face(0, x, y), face(0, x + 1, y), face(1, x, y), face(1, x, y + 1), z, pltpu.roll(z, LZ - 1, 1)]
            columns.append(jnp.concatenate(six + [last_in[pl.ds(y, 8, stride=LY), :], filler], 0))
        hi, lo = halves(jnp.concatenate(columns, 1))
        prod = jnp.dot(w_all, jnp.concatenate([hi, lo, hi], 0), preferred_element_type=f32)
        parts = []
        for y in range(LY):
            k = k_ref[x * LY + y : x * LY + y + 1, :]
            m = m_ref[x * LY + y : x * LY + y + 1, :]
            cols = slice(y * LZ, (y + 1) * LZ)
            w = prod[:OUT, cols] * k + prod[OUT:, cols] * m
            parts.append([w[b * B : (b + 1) * B] for b in range(6)])
            last_out[pl.ds(y, 8, stride=LY), :] = w[LAST:]
        for y in range(LY):
            wlx, wux, wly, wuy, wlz, wuz = parts[y]
            put(0, x, y, wlx if x == 0 else wlx + carry[y])
            put(1, x, y, wly if y == 0 else wly + parts[y - 1][3])
            put(2, x, y, wlz + pltpu.roll(wuz, 1, 1))
            if x == 0 and low_x is not None:
                low_x[y * B : (y + 1) * B] = wlx
            if x == LX - 1:
                up_x[y * B : (y + 1) * B] = wux
        tiles = [last_out[j * LY : (j + 1) * LY] for j in range(6)]
        put_last(0, x, tiles[0] if x == 0 else tiles[0] + last_carry)
        put_last(1, x, tiles[1] + jnp.where(at_first, 0.0, pltpu.roll(tiles[4], 1, 0)))
        put_last(2, x, tiles[2] + pltpu.roll(tiles[5], 1, 1))
        if x == 0 and low_x is not None:
            low_x[B * LY :] = tiles[0]
        if x == LX - 1:
            up_x[B * LY :] = tiles[3]
        if low_y is not None:
            low_y[x * B : (x + 1) * B] = parts[0][2]
            low_y[B * LX + x : B * LX + x + 1] = tiles[1][:1]
        up_y[x * B : (x + 1) * B] = parts[LY - 1][3]
        up_y[B * LX + x : B * LX + x + 1] = tiles[4][LY - 1 :]
        carry = [parts[y][1] for y in range(LY)]
        last_carry = tiles[3]


def is_even(axis):
    return lax.rem(lax.axis_index(axis), 2) == 0


def route(even, up, low, near, far):
    near[...] = jnp.where(even, up[...], low[...])
    far[...] = jnp.where(even, low[...], up[...])


def edge_kernel(rhs_ref, fx_ref, fy_ref, sem_x, sem_y):
    face_x = pltpu.make_async_copy(rhs_ref.at[0, :, 0], fx_ref, sem_x)
    face_y = pltpu.make_async_copy(rhs_ref.at[1, :, :, 0], fy_ref, sem_y)
    face_x.start()
    face_y.start()
    face_x.wait()
    face_y.wait()


def weight_kernel(s_ref, m_ref, w_ref, inv_ref):
    n = 6 * A

    def placing(rows, span):
        r = lax.broadcasted_iota(jnp.int32, (rows, n), 0)
        c = lax.broadcasted_iota(jnp.int32, (rows, n), 1)
        p = lax.rem(r, span)
        j = p - LAST
        node = jnp.where(p < LAST, lax.div(p, B) * A + lax.rem(p, B), (2 * lax.rem(j, 3) + lax.div(j, 3)) * A + B)
        return (node == c) & (p < n), lax.div(r, span)

    def ones(mask):
        return jnp.where(mask, 1.0, 0.0).astype(bf16)

    rows = ones(placing(OUT, OUT)[0])
    mask, third = placing(3 * IN, IN)
    columns = (ones(mask & (third < 2)), ones(mask & (third == 2)))
    diagonal = lax.broadcasted_iota(jnp.int32, (n, n), 0) == lax.broadcasted_iota(jnp.int32, (n, n), 1)

    def largest(v):
        return jnp.max(jnp.max(jnp.where(diagonal, v, 0.0), 0, keepdims=True), 1, keepdims=True)

    inv = 1.0 / (10.0 * largest(s_ref[...]) + 2.0 * largest(m_ref[...]))
    inv_ref[...] = jnp.broadcast_to(inv, (8, LZ))
    for i, ref in enumerate((s_ref, m_ref)):
        full = 0.0
        for part, place in zip(halves(ref[...] * inv), columns):
            moved = jnp.dot(rows, part, preferred_element_type=f32).astype(bf16)
            full = full + lax.dot_general(moved, place, (((1,), (1,)), ((), ())), preferred_element_type=f32)
        w_ref[i * OUT : (i + 1) * OUT] = full.astype(bf16)


def first_kernel(rhs_ref, hx_ref, hy_ref, k_ref, m_ref, w_ref,
                 p_ref, sn0, sn1, sfx, sny, sfy, last_in, last_out, upx, lowx, upy, lowy):
    apply_operator(rhs_ref, hx_ref, hy_ref, k_ref, m_ref, w_ref, p_ref, upx, lowx, upy, lowy, last_in, last_out, True)
    route(is_even("gx"), upx, lowx, Parts(sn0, sn1), sfx)
    route(is_even("gy"), upy, lowy, sny, sfy)


def assemble(p_ref, snx, sfx, sny, sfy, rnx, rfx, rny, rfy, v, ux, uy):
    even_x = is_even("gx")
    even_y = is_even("gy")
    v[...] = p_ref[...]
    below_x = jnp.where(even_x, rfx[...], rnx[...])
    v[: B * LY] = v[: B * LY] + below_x[: B * LY]
    v[TAIL : TAIL + LY] = v[TAIL : TAIL + LY] + below_x[B * LY :]
    below_y = jnp.where(even_y, rfy[...], rny[...])
    for x in range(LX):
        at = (CELLS + x * LY) * B
        v[at : at + B] = v[at : at + B] + below_y[x * B : (x + 1) * B]
        at = TAIL + CELLS + x * LY
        v[at : at + 1] = v[at : at + 1] + below_y[B * LX + x : B * LX + x + 1]
    ux[...] = jnp.where(even_x, snx[...] + rnx[...], sfx[...] + rfx[...])
    uy[...] = jnp.where(even_y, sny[...] + rny[...], sfy[...] + rfy[...])


def node_sum(value):
    return jnp.sum(value.reshape(-1, LY, LZ), 0)


def row(tile):
    return jnp.sum(tile, 0, keepdims=True)


def second_kernel(p_ref, rfx, rfy, rny, rn0, rn1, sn0, sn1, sfx, sny, sfy, k_ref, m_ref, w_ref,
                  v1_ref, p1_ref, tn0, tn1, tfx, tny, tfy, ux, uy, last_in, last_out, upx, lowx, upy, lowy):
    assemble(p_ref, Parts(sn0, sn1), sfx, sny, sfy, Parts(rn0, rn1), rfx, rny, rfy, v1_ref, ux, uy)
    apply_operator(v1_ref, ux, uy, k_ref, m_ref, w_ref, p1_ref, upx, lowx, upy, lowy, last_in, last_out)
    route(is_even("gx"), upx, lowx, Parts(tn0, tn1), tfx)
    route(is_even("gy"), upy, lowy, tny, tfy)


def element_sum(ref, faces):
    rows = []
    for y in range(LY):
        total = 0.0
        for at in range(0, faces, LY):
            first = (at + y) * B
            total = total + (ref[first : first + 8] + ref[first + 8 : first + 16] + ref[first + 16 : first + B])
        rows.append(row(total))
    return jnp.concatenate(rows, 0) + node_sum(ref[faces * B :])


def tile_of(ref, faces, f, a, x):
    at = f * CELLS + x * LY
    if a == B:
        return ref[faces * B + at : faces * B + at + LY, :]
    return ref[pl.ds(at * B + a, LY, stride=B), :]


def products_kernel(v0_ref, v1_ref, sums_ref, v1_hbm, sem):
    keep = pltpu.make_async_copy(v1_ref, v1_hbm, sem)
    keep.start()
    s0 = s1 = s00 = s01 = s11 = 0.0
    for f in range(F):
        for a in range(A):
            for x in range(LX):
                at = (f * A + a) * CELLS + x * LY
                v0 = v0_ref[at : at + LY, :]
                v1 = tile_of(v1_ref, F * CELLS, f, a, x)
                s0, s1, s00, s01, s11 = s0 + v0, s1 + v1, s00 + v0 * v0, s01 + v0 * v1, s11 + v1 * v1
    for k, s in enumerate((s0, s1, s00, s01, s11)):
        sums_ref[8 * k : 8 * k + 8] = s
    keep.wait()


def third_kernel(p_ref, v1_ref, rfx, rfy, rny, rn0, rn1, sn0, sn1, sfx, sny, sfy, sums_ref, k_ref, m_ref, w_ref,
                 v2_ref, p2_ref, upx, upy, loads_ref, mom_ref, ux, uy, last_in, last_out):
    assemble(p_ref, Parts(sn0, sn1), sfx, sny, sfy, Parts(rn0, rn1), rfx, rny, rfy, v2_ref, ux, uy)
    v1 = v1_ref[...]
    v2 = v2_ref[...]
    loads_ref[0:16] = sums_ref[0:16]
    loads_ref[16:24] = element_sum(v2_ref, F * CELLS)
    m3 = node_sum(v1 * v2)
    m4 = node_sum(v2 * v2)
    apply_operator(v2_ref, ux, uy, k_ref, m_ref, w_ref, p2_ref, upx, None, upy, None, last_in, last_out)
    loads_ref[24:32] = element_sum(p2_ref, F * CELLS)
    loads_ref[32:40] = element_sum(upx, LY)
    energy = node_sum(v2_ref[...] * p2_ref[...]) + node_sum(ux[...] * upx[...])
    tail = row(uy[...] * upy[...])
    tile = jnp.concatenate(
        [row(sums_ref[16 + 8 * k : 24 + 8 * k]) for k in range(3)]
        + [row(m3), row(m4), row(energy) + tail, jnp.zeros((2, LZ), f32)], 0,
    )
    lane = lax.broadcasted_iota(jnp.int32, (8, LZ), 1)
    moment = lax.broadcasted_iota(jnp.int32, (8, LZ), 0)
    sums = jnp.broadcast_to(jnp.sum(tile, axis=1, keepdims=True), (8, LZ))
    packed = row(jnp.where(lane == HALF + moment, sums, 0.0))
    edge = row(upy[...])
    pair = [jnp.where(lane[:1] < HALF, edge, packed), pltpu.roll(edge, HALF, 1)]
    pair = jnp.concatenate(pair * 4, 0)[:, :SHORT]
    for at in range(0, mom_ref.shape[0], 8):
        mom_ref[at : at + 8] = pair
    loads_ref[40:] = jnp.zeros((loads_ref.shape[0] - 40, LZ), f32)


def weigh_kernel(own, near, far, both, *outs, table):
    nx = len(table)
    q = lax.rem(lax.axis_index("gx"), 4)
    low, high = lax.rem(q, 2) == 0, q < 2
    one, two = jnp.where(low, 1, -1), jnp.where(high, 2, -2)
    sources = ((own, 0, (0,)), (near, one, (1, -1)), (far, two, (2, -2)), (both, one + two, (3, 1, -1, -3)))

    def pick(at, shift, span):
        value = jnp.float32(table[(at - span[0]) % nx])
        for s in span[1:]:
            value = jnp.where(shift == s, table[(at - s) % nx], value)
        return value

    for z, out in enumerate(outs):
        total = [0.0] * 4
        for ref, shift, span in sources:
            w = pick(4 * z, shift, span)
            for k in range(4):
                total[k] = total[k] + ref[k * 8 : k * 8 + 8] * w
            total[3] = total[3] + ref[32:40] * pick(4 * z - 1, shift, span)
        for k in range(4):
            out[k * 8 : k * 8 + 8] = total[k]


def two_sum(a, b):
    s = a + b
    t = s - a
    return s, (a - (s - t)) + (b - t)


def pair_add(a, b):
    s, e = two_sum(a[0], b[0])
    e = e + (a[1] + b[1])
    h = s + e
    return h, e - (h - s)


def split(a):
    t = a * 4097.0
    h = t - (t - a)
    return h, a - h


def pair_times(a, c):
    p = a[0] * c
    ah, al = split(a[0])
    ch, cl = split(c)
    return p, ((ah * ch - p) + ah * cl + al * ch) + al * cl + a[1] * c


def moments(got):
    zero = jnp.zeros((8, SHORT), f32)
    pairs = [(got[at : at + 8], zero) for at in range(0, got.shape[0], 8)]
    while len(pairs) > 1:
        pairs = [pair_add(a, b) for a, b in zip(pairs[::2], pairs[1::2])]
    h, l = pairs[0]
    rows = [(h[r : r + 1], l[r : r + 1]) for r in (0, 2, 4, 6)]
    t = pair_add(pair_add(rows[0], rows[1]), pair_add(rows[2], rows[3]))
    level = [tuple(p[:, HALF + k : HALF + k + 1] for p in t) for k in range(6)]
    c = level[1][0] / level[0][0]
    heads = [level[0]]
    while len(level) > 1:
        level = [pair_add(up, pair_times(at, -c)) for at, up in zip(level, level[1:])]
        heads.append(level[0])
    return c, [p[0] + p[1] for p in heads]


def conjugate_gradient(c, m):
    def dot(a, b):
        s = None
        for i, ai in enumerate(a):
            for j, bj in enumerate(b):
                t = ai * bj * m[i + j]
                s = t if s is None else s + t
        return s

    def add(a, b, factor):
        longer = []
        for i in range(max(len(a), len(b))):
            if i >= len(b):
                longer.append(a[i])
            elif i >= len(a):
                longer.append(factor * b[i])
            else:
                longer.append(a[i] + factor * b[i])
        return longer

    def times(a, shift):
        return [a[0] * shift] + [a[i] * shift + a[i - 1] for i in range(1, len(a))] + [a[-1]]

    def plain(a):
        out = [a[-1]]
        for coefficient in a[-2::-1]:
            out = times(out, -c)
            out[0] = out[0] + coefficient
        return out

    one = jnp.ones((1, 1), f32)
    iterate, residual, direction = [], [one], [one]
    norm = m[0]
    for step in range(ITERS):
        img = times(direction, c)
        alpha = norm / dot(direction, img)
        iterate = add(iterate, direction, alpha)
        residual = add(residual, img, -alpha)
        if step < ITERS - 1:
            norm_next = dot(residual, residual)
            direction = add(residual, direction, norm_next / norm)
            norm = norm_next
    return plain(iterate), plain(residual)


def coefficients_kernel(got_ref, inv_ref, rhs_hbm, v1_hbm, rhs_ref, v1_ref, coef_ref, edge_ref, sems, *, table, ny):
    fetches = [pltpu.make_async_copy(rhs_hbm, rhs_ref, sems.at[0]), pltpu.make_async_copy(v1_hbm, v1_ref, sems.at[1])]
    for fetch in fetches:
        fetch.start()
    x, d = conjugate_gradient(*moments(got_ref[...]))
    inv = inv_ref[0:1, 0:1]
    for k, t in enumerate([t * inv for t in x] + d):
        coef_ref[k : k + 1] = jnp.broadcast_to(t, (1, LZ))
    coef_ref[7:8] = jnp.zeros((1, LZ), f32)
    below = lax.rem(lax.axis_index("gy") + ny - 1, ny)
    me = lax.axis_index("gx")
    nx = len(table)
    edge = [jnp.zeros((1, SHORT), f32)] * 2
    for offset, weight in enumerate(table):
        slab = lax.rem(me + nx - offset, nx)
        edge = [e + got_ref[pl.ds(2 * (slab * ny + below) + i, 1), :] * weight for i, e in enumerate(edge)]
    edge = jnp.concatenate([e[:, :HALF] for e in edge], 1)
    edge_ref[...] = jnp.concatenate([edge, jnp.zeros((LY - 1, LZ), f32)], 0)
    for fetch in fetches:
        fetch.wait()


def last_kernel(prolong_ref, coef_ref, edge_ref, c0, c1, c2, c3, rhs_ref, v1_ref, v2_ref, p2_ref, rx_ref, ry_ref,
                sol_hbm, res_hbm, coarse_ref, sol_ref, res_ref, out_sems):
    coef = [jnp.broadcast_to(coef_ref[k : k + 1], (LY, LZ)) for k in range(7)]
    x, d = coef[:3], coef[3:]
    circ = [c0[k * 8 : k * 8 + 8] + c1[k * 8 : k * 8 + 8] + c2[k * 8 : k * 8 + 8] + c3[k * 8 : k * 8 + 8] for k in range(4)]
    coarse = d[0] * circ[0] + d[1] * circ[1] + d[2] * circ[2] + d[3] * (circ[3] + edge_ref[...])
    coarse_ref[...] = coarse
    stores = []
    for f in range(F):
        for a in range(A):
            at = (f * A + a) * CELLS
            spread = coarse * prolong_ref[f, a]
            for cell in range(LX):
                rows = slice(at + cell * LY, at + (cell + 1) * LY)
                v0 = rhs_ref[rows, :]
                v1, v2, img = (tile_of(ref, F * CELLS, f, a, cell) for ref in (v1_ref, v2_ref, p2_ref))
                if f == 0 and cell == 0:
                    img = img + tile_of(rx_ref, LY, 0, a, 0)
                sol_ref[rows, :] = x[0] * v0 + x[1] * v1 + x[2] * v2 + spread
                res_ref[rows, :] = d[0] * v0 + d[1] * v1 + d[2] * v2 + d[3] * img
        if f == 1:
            below = d[3][0:1] * ry_ref[...]
            for cell in range(LX):
                first = pl.ds(FACE + cell * LY, B, stride=CELLS)
                res_ref[first, :] = res_ref[first, :] + below[cell * B : (cell + 1) * B]
            first = pl.ds(FACE + B * CELLS, LX, stride=LY)
            res_ref[first, :] = res_ref[first, :] + below[B * LX :]
        rows = pl.ds(f * FACE, FACE)
        for i, (src, dst) in enumerate(((sol_ref, sol_hbm), (res_ref, res_hbm))):
            stores.append(pltpu.make_async_copy(src.at[rows], dst.at[rows], out_sems.at[2 * f + i]))
            stores[-1].start()
    for store in stores:
        store.wait()


def jacobi_weights(n):
    coarse = np.zeros(n)
    load = np.zeros(n)
    load[0] = 1.0
    for _ in range(SWEEPS):
        coarse = (load + np.roll(coarse, 1) + np.roll(coarse, -1)) / 2.2
    return coarse / 75.0


def struct(*shape):
    return jax.ShapeDtypeStruct(shape, f32)


PARAMS = pltpu.CompilerParams(vmem_limit_bytes=16 * 1024 * 1024)


def shards(rhs, kappa, mass, stiffness, mass_matrix, prolong):
    nx, ny = lax.axis_size("gx"), lax.axis_size("gy")
    vx, vy = A * LY, A * LX
    rhs2 = rhs.reshape(ROWS, LZ)
    k2 = kappa.reshape(CELLS, LZ)
    m2 = mass.reshape(CELLS, LZ)
    sends = [struct(n, LZ) for n in PARTS] + [struct(vx, LZ), struct(vy, LZ), struct(vy, LZ)]
    upper = [pltpu.VMEM((vx, LZ), f32), pltpu.VMEM((vy, LZ), f32)] + [pltpu.VMEM((8 * LY, LZ), f32)] * 2
    edges = [pltpu.VMEM((vx, LZ), f32)] * 2 + [pltpu.VMEM((vy, LZ), f32)] * 2

    def call(kernel, name, ins, outs, scratch=(), **static):
        specs = [i[1] if isinstance(i, tuple) else VM for i in ins]
        ins = [i[0] if isinstance(i, tuple) else i for i in ins]

        def bound(*refs):
            kernel(*refs, **static)

        return pl.pallas_call(
            bound,
            out_shape=outs,
            in_specs=specs,
            out_specs=[ANY if isinstance(o, pl.MemoryRef) else VM for o in outs],
            scratch_shapes=list(scratch),
            compiler_params=PARAMS,
            name=name,
        )(*ins)

    def swap(s):
        *near, far_x, near_y, far_y = s
        far_x = far_swap(far_x, "gx")
        far_y = far_swap(far_y, "gy")
        near_y = near_swap(near_y, "gy")
        return [far_x, far_y, near_y] + [near_swap(part, "gx") for part in near]

    hbm = pltpu.with_memory_space_constraint(rhs, pltpu.HBM)
    fx, fy = call(
        edge_kernel, "edges", [(hbm, ANY)], [struct(A, LY, LZ), struct(A, LX, LZ)],
        [pltpu.SemaphoreType.DMA, pltpu.SemaphoreType.DMA],
    )
    hx = shifted(fx.reshape(vx, LZ), "gx", -1)
    hy = shifted(fy.reshape(vy, LZ), "gy", -1)
    w, inv = call(
        weight_kernel, "weights", [stiffness, mass_matrix],
        [jax.ShapeDtypeStruct((2 * OUT, 3 * IN), bf16), struct(8, LZ)],
    )

    p0, *s = call(
        first_kernel, "first", [rhs2, hx, hy, k2, m2, w], [struct(ROWS, LZ)] + sends, upper[2:] + edges,
    )
    r = swap(s)
    v1, p1, *s = call(
        second_kernel, "second", [p0, *r, *s, k2, m2, w],
        [struct(ROWS, LZ), struct(ROWS, LZ)] + sends, upper + edges,
    )
    r = swap(s)
    sums, v1_kept = call(
        products_kernel, "products", [rhs2, v1], [struct(40, LZ), pltpu.HBM((ROWS, LZ), f32)], [pltpu.SemaphoreType.DMA],
    )
    peers = nx * ny * 2
    v2, p2, upx, upy, loads, mom = call(
        third_kernel, "third", [p1, v1, *r, *s, sums, k2, m2, w],
        [struct(ROWS, LZ)] * 2 + [struct(vx, LZ), struct(vy, LZ), struct(152, LZ), struct(peers, SHORT)], upper,
    )
    table = [float(t) for t in jacobi_weights(nx)]
    group = [lax.ppermute(loads, "gx", [(i, i ^ b) for i in range(nx)]) for b in (1, 2, 3)]
    pieces = call(weigh_kernel, "weigh", [loads, *group], [struct(32, LZ)] * (nx // 4), table=table)
    coarse = [pieces[0]] + [shifted(p, "gx", 4 * z) for z, p in enumerate(pieces) if z]
    got = lax.all_to_all(mom.reshape(-1, 2, SHORT), ("gx", "gy"), 0, 0, tiled=True).reshape(mom.shape)
    rx = shifted(upx, "gx", 1)
    ry = shifted(upy, "gy", 1)
    v0, v1_kept = (pltpu.with_memory_space_constraint(v, pltpu.HBM) for v in (rhs2, v1_kept))
    v0, v1, coef, edge = call(
        coefficients_kernel, "coefficients", [got, inv, (v0, ANY), (v1_kept, ANY)],
        [struct(ROWS, LZ)] * 2 + [struct(8, LZ), struct(LY, LZ)], [pltpu.SemaphoreType.DMA((2,))], table=table, ny=ny,
    )
    sol, res, coarse = call(
        last_kernel, "last", [(prolong, SM), coef, edge, *coarse, v0, v1, v2, p2, rx, ry],
        [pltpu.HBM((ROWS, LZ), f32)] * 2 + [struct(LY, LZ)],
        [pltpu.VMEM((ROWS, LZ), f32)] * 2 + [pltpu.SemaphoreType.DMA((6,))],
    )
    return sol.reshape(rhs.shape), res.reshape(rhs.shape), coarse[None]


def solution(mesh):
    placed = (
        P(None, None, "gx", "gy", None),
        P("gx", "gy", None),
        P("gx", "gy", None),
        P(),
        P(),
        P(),
    )
    return jax.shard_map(
        shards,
        mesh=mesh,
        in_specs=placed,
        out_specs=(
            P(None, None, "gx", "gy", None),
            P(None, None, "gx", "gy", None),
            P("gx", "gy", None),
        ),
        check_vma=False,
    )
```

```python
import jax
import jax.numpy as jnp
import numpy as np
from jax import lax
from jax.experimental import pallas as pl
from jax.experimental.pallas import tpu as pltpu
from jax.sharding import PartitionSpec as P

ITERS = 3
SWEEPS = 8
F, A = 3, 25
B = 24
LAST = 6 * B
OUT, IN = LAST + 8, LAST + 16
LX, LY, LZ = 4, 8, 128
CELLS = LX * LY
FACE = A * CELLS
ROWS = F * FACE
TAIL = F * CELLS * B
f32, bf16 = jnp.float32, jnp.bfloat16
VM = pl.BlockSpec(memory_space=pltpu.VMEM)
SM = pl.BlockSpec(memory_space=pltpu.SMEM)
ANY = pl.BlockSpec(memory_space=pl.ANY)


PARTS = (100, 100)


class Parts:
    def __init__(self, *refs):
        self.refs = refs

    def __getitem__(self, _):
        return jnp.concatenate([ref[...] for ref in self.refs], 0)

    def __setitem__(self, _, value):
        at = 0
        for ref in self.refs:
            ref[...] = value[at : at + ref.shape[0]]
            at += ref.shape[0]


def shifted(value, axis, by):
    n = lax.axis_size(axis)
    return lax.ppermute(value, axis, [(i, (i + by) % n) for i in range(n)])


def near_swap(value, axis):
    n = lax.axis_size(axis)
    return lax.ppermute(value, axis, [(i, i ^ 1) for i in range(n)])


def far_swap(value, axis):
    n = lax.axis_size(axis)
    pairs = [(i, (i + 1) % n) if i % 2 else (i, (i - 1) % n) for i in range(n)]
    return lax.ppermute(value, axis, pairs)


def halves(v):
    hi = v.astype(bf16)
    lo = (v - hi.astype(f32)).astype(bf16)
    return hi, lo


def apply_operator(v_ref, ux_ref, uy_ref, k_ref, m_ref, w_ref, out_ref, up_x, low_x, up_y, low_y, last_in, last_out, by_nodes=False):
    w_all = w_ref[...]
    at_first = lax.broadcasted_iota(jnp.int32, (LY, LZ), 0) == 0
    last_in[LAST // B * LY :] = jnp.zeros((2 * LY, LZ), f32)

    def block(ref, at, pitch, i):
        if by_nodes:
            return ref[pl.ds(at * A + i, B, stride=pitch), :]
        return ref[(at + i) * B : (at + i + 1) * B, :]

    def face(f, x, y):
        if f == 0 and x == LX:
            return block(ux_ref, 0, LY, y)
        if f == 1 and y == LY:
            return block(uy_ref, 0, LX, x)
        return block(v_ref, f * CELLS, CELLS, x * LY + y)

    def last_rows(f, x):
        if x == LX:
            return ux_ref[B * LY :, :]
        at = (f * FACE + B * CELLS if by_nodes else TAIL + f * CELLS) + x * LY
        return v_ref[at : at + LY, :]

    def put(f, x, y, value):
        at = (f * CELLS + x * LY + y) * B
        out_ref[at : at + B, :] = value

    def put_last(f, x, value):
        at = TAIL + f * CELLS + x * LY
        out_ref[at : at + LY, :] = value

    filler = jnp.zeros((IN - OUT, LZ), f32)
    carry = last_carry = None
    for x in range(LX):
        z_last = last_rows(2, x)
        y_last = last_rows(1, x)
        above = uy_ref[B * LX + x : B * LX + x + 1, :]
        top = lax.broadcasted_iota(jnp.int32, (LY, LZ), 0) == LY - 1
        y_up = jnp.where(top, jnp.broadcast_to(above, (LY, LZ)), pltpu.roll(y_last, LY - 1, 0))
        for j, tile in enumerate((last_rows(0, x), y_last, z_last, last_rows(0, x + 1), y_up, pltpu.roll(z_last, LZ - 1, 1))):
            last_in[j * LY : (j + 1) * LY] = tile
        columns = []
        for y in range(LY):
            z = face(2, x, y)
            six = [face(0, x, y), face(0, x + 1, y), face(1, x, y), face(1, x, y + 1), z, pltpu.roll(z, LZ - 1, 1)]
            columns.append(jnp.concatenate(six + [last_in[pl.ds(y, 8, stride=LY), :], filler], 0))
        hi, lo = halves(jnp.concatenate(columns, 1))
        prod = jnp.dot(w_all, jnp.concatenate([hi, lo, hi], 0), preferred_element_type=f32)
        parts = []
        for y in range(LY):
            k = k_ref[x * LY + y : x * LY + y + 1, :]
            m = m_ref[x * LY + y : x * LY + y + 1, :]
            cols = slice(y * LZ, (y + 1) * LZ)
            w = prod[:OUT, cols] * k + prod[OUT:, cols] * m
            parts.append([w[b * B : (b + 1) * B] for b in range(6)])
            last_out[pl.ds(y, 8, stride=LY), :] = w[LAST:]
        for y in range(LY):
            wlx, wux, wly, wuy, wlz, wuz = parts[y]
            put(0, x, y, wlx if x == 0 else wlx + carry[y])
            put(1, x, y, wly if y == 0 else wly + parts[y - 1][3])
            put(2, x, y, wlz + pltpu.roll(wuz, 1, 1))
            if x == 0 and low_x is not None:
                low_x[y * B : (y + 1) * B] = wlx
            if x == LX - 1:
                up_x[y * B : (y + 1) * B] = wux
        tiles = [last_out[j * LY : (j + 1) * LY] for j in range(6)]
        put_last(0, x, tiles[0] if x == 0 else tiles[0] + last_carry)
        put_last(1, x, tiles[1] + jnp.where(at_first, 0.0, pltpu.roll(tiles[4], 1, 0)))
        put_last(2, x, tiles[2] + pltpu.roll(tiles[5], 1, 1))
        if x == 0 and low_x is not None:
            low_x[B * LY :] = tiles[0]
        if x == LX - 1:
            up_x[B * LY :] = tiles[3]
        if low_y is not None:
            low_y[x * B : (x + 1) * B] = parts[0][2]
            low_y[B * LX + x : B * LX + x + 1] = tiles[1][:1]
        up_y[x * B : (x + 1) * B] = parts[LY - 1][3]
        up_y[B * LX + x : B * LX + x + 1] = tiles[4][LY - 1 :]
        carry = [parts[y][1] for y in range(LY)]
        last_carry = tiles[3]


def is_even(axis):
    return lax.rem(lax.axis_index(axis), 2) == 0


def route(even, up, low, near, far):
    near[...] = jnp.where(even, up[...], low[...])
    far[...] = jnp.where(even, low[...], up[...])


def edge_kernel(rhs_ref, fx_ref, fy_ref, sem_x, sem_y):
    face_x = pltpu.make_async_copy(rhs_ref.at[0, :, 0], fx_ref, sem_x)
    face_y = pltpu.make_async_copy(rhs_ref.at[1, :, :, 0], fy_ref, sem_y)
    face_x.start()
    face_y.start()
    face_x.wait()
    face_y.wait()


def weight_kernel(s_ref, m_ref, w_ref, inv_ref):
    n = 6 * A

    def placing(rows, span):
        r = lax.broadcasted_iota(jnp.int32, (rows, n), 0)
        c = lax.broadcasted_iota(jnp.int32, (rows, n), 1)
        p = lax.rem(r, span)
        j = p - LAST
        node = jnp.where(p < LAST, lax.div(p, B) * A + lax.rem(p, B), (2 * lax.rem(j, 3) + lax.div(j, 3)) * A + B)
        return (node == c) & (p < n), lax.div(r, span)

    def ones(mask):
        return jnp.where(mask, 1.0, 0.0).astype(bf16)

    rows = ones(placing(OUT, OUT)[0])
    mask, third = placing(3 * IN, IN)
    columns = (ones(mask & (third < 2)), ones(mask & (third == 2)))
    diagonal = lax.broadcasted_iota(jnp.int32, (n, n), 0) == lax.broadcasted_iota(jnp.int32, (n, n), 1)

    def largest(v):
        return jnp.max(jnp.max(jnp.where(diagonal, v, 0.0), 0, keepdims=True), 1, keepdims=True)

    inv = 1.0 / (10.0 * largest(s_ref[...]) + 2.0 * largest(m_ref[...]))
    inv_ref[...] = jnp.broadcast_to(inv, (8, LZ))
    for i, ref in enumerate((s_ref, m_ref)):
        full = 0.0
        for part, place in zip(halves(ref[...] * inv), columns):
            moved = jnp.dot(rows, part, preferred_element_type=f32).astype(bf16)
            full = full + lax.dot_general(moved, place, (((1,), (1,)), ((), ())), preferred_element_type=f32)
        w_ref[i * OUT : (i + 1) * OUT] = full.astype(bf16)


def first_kernel(rhs_ref, hx_ref, hy_ref, k_ref, m_ref, w_ref,
                 p_ref, sn0, sn1, sfx, sny, sfy, last_in, last_out, upx, lowx, upy, lowy):
    apply_operator(rhs_ref, hx_ref, hy_ref, k_ref, m_ref, w_ref, p_ref, upx, lowx, upy, lowy, last_in, last_out, True)
    route(is_even("gx"), upx, lowx, Parts(sn0, sn1), sfx)
    route(is_even("gy"), upy, lowy, sny, sfy)


def assemble(p_ref, snx, sfx, sny, sfy, rnx, rfx, rny, rfy, v, ux, uy):
    even_x = is_even("gx")
    even_y = is_even("gy")
    v[...] = p_ref[...]
    below_x = jnp.where(even_x, rfx[...], rnx[...])
    v[: B * LY] = v[: B * LY] + below_x[: B * LY]
    v[TAIL : TAIL + LY] = v[TAIL : TAIL + LY] + below_x[B * LY :]
    below_y = jnp.where(even_y, rfy[...], rny[...])
    for x in range(LX):
        at = (CELLS + x * LY) * B
        v[at : at + B] = v[at : at + B] + below_y[x * B : (x + 1) * B]
        at = TAIL + CELLS + x * LY
        v[at : at + 1] = v[at : at + 1] + below_y[B * LX + x : B * LX + x + 1]
    ux[...] = jnp.where(even_x, snx[...] + rnx[...], sfx[...] + rfx[...])
    uy[...] = jnp.where(even_y, sny[...] + rny[...], sfy[...] + rfy[...])


def node_sum(value):
    return jnp.sum(value.reshape(-1, LY, LZ), 0)


def row(tile):
    return jnp.sum(tile, 0, keepdims=True)


def second_kernel(p_ref, rfx, rfy, rny, rn0, rn1, sn0, sn1, sfx, sny, sfy, k_ref, m_ref, w_ref,
                  v1_ref, p1_ref, tn0, tn1, tfx, tny, tfy, ux, uy, upx, upy, last_in, last_out, lowx, lowy):
    assemble(p_ref, Parts(sn0, sn1), sfx, sny, sfy, Parts(rn0, rn1), rfx, rny, rfy, v1_ref, ux, uy)
    apply_operator(v1_ref, ux, uy, k_ref, m_ref, w_ref, p1_ref, upx, lowx, upy, lowy, last_in, last_out)
    route(is_even("gx"), upx, lowx, Parts(tn0, tn1), tfx)
    route(is_even("gy"), upy, lowy, tny, tfy)


def element_sum(ref, faces):
    rows = []
    for y in range(LY):
        total = 0.0
        for at in range(0, faces, LY):
            first = (at + y) * B
            total = total + (ref[first : first + 8] + ref[first + 8 : first + 16] + ref[first + 16 : first + B])
        rows.append(row(total))
    return jnp.concatenate(rows, 0) + node_sum(ref[faces * B :])


def tile_of(ref, faces, f, a, x):
    at = f * CELLS + x * LY
    if a == B:
        return ref[faces * B + at : faces * B + at + LY, :]
    return ref[pl.ds(at * B + a, LY, stride=B), :]


def products_kernel(v0_ref, v1_ref, p1_ref, ux, uy, upx, upy, sums_ref, v1_hbm, sem):
    keep = pltpu.make_async_copy(v1_ref, v1_hbm, sem)
    keep.start()
    s0 = s1 = s00 = s01 = s11 = 0.0
    for f in range(F):
        for a in range(A):
            for x in range(LX):
                at = (f * A + a) * CELLS + x * LY
                v0 = v0_ref[at : at + LY, :]
                v1 = tile_of(v1_ref, F * CELLS, f, a, x)
                s0, s1, s00, s01, s11 = s0 + v0, s1 + v1, s00 + v0 * v0, s01 + v0 * v1, s11 + v1 * v1
    for k, s in enumerate((s0, s1, s00, s01, s11)):
        sums_ref[8 * k : 8 * k + 8] = s
    energy = node_sum(v1_ref[...] * p1_ref[...]) + node_sum(ux[...] * upx[...])
    sums_ref[40:48] = energy
    sums_ref[40:41] = sums_ref[40:41] + row(uy[...] * upy[...])
    keep.wait()


def third_kernel(p_ref, rfx, rfy, rny, rn0, rn1, sn0, sn1, sfx, sny, sfy, sums_ref, k_ref, m_ref, w_ref,
                 v2_ref, p2_ref, upx, upy, loads_ref, mom_ref, ux, uy, last_in, last_out):
    assemble(p_ref, Parts(sn0, sn1), sfx, sny, sfy, Parts(rn0, rn1), rfx, rny, rfy, v2_ref, ux, uy)
    v2 = v2_ref[...]
    loads_ref[0:16] = sums_ref[0:16]
    loads_ref[16:24] = element_sum(v2_ref, F * CELLS)
    m4 = node_sum(v2 * v2)
    apply_operator(v2_ref, ux, uy, k_ref, m_ref, w_ref, p2_ref, upx, None, upy, None, last_in, last_out)
    loads_ref[24:32] = element_sum(p2_ref, F * CELLS)
    loads_ref[32:40] = element_sum(upx, LY)
    energy = node_sum(v2_ref[...] * p2_ref[...]) + node_sum(ux[...] * upx[...])
    tail = row(uy[...] * upy[...])
    tile = jnp.concatenate(
        [row(sums_ref[16 + 8 * k : 24 + 8 * k]) for k in range(4)]
        + [row(m4), row(energy) + tail, jnp.zeros((2, LZ), f32)], 0,
    )
    lane = lax.broadcasted_iota(jnp.int32, (8, LZ), 1)
    moment = lax.broadcasted_iota(jnp.int32, (8, LZ), 0)
    sums = jnp.broadcast_to(jnp.sum(tile, axis=1, keepdims=True), (8, LZ))
    packed = row(jnp.where(lane == 16 * moment, sums, 0.0))
    pair = jnp.concatenate([packed, row(upy[...])] * 4, 0)
    for at in range(0, mom_ref.shape[0], 8):
        mom_ref[at : at + 8] = pair
    loads_ref[40:] = jnp.zeros((loads_ref.shape[0] - 40, LZ), f32)


def weigh_kernel(own, near, far, both, *outs, table):
    nx = len(table)
    q = lax.rem(lax.axis_index("gx"), 4)
    low, high = lax.rem(q, 2) == 0, q < 2
    one, two = jnp.where(low, 1, -1), jnp.where(high, 2, -2)
    sources = ((own, 0, (0,)), (near, one, (1, -1)), (far, two, (2, -2)), (both, one + two, (3, 1, -1, -3)))

    def pick(at, shift, span):
        value = jnp.float32(table[(at - span[0]) % nx])
        for s in span[1:]:
            value = jnp.where(shift == s, table[(at - s) % nx], value)
        return value

    for z, out in enumerate(outs):
        total = [0.0] * 4
        for ref, shift, span in sources:
            w = pick(4 * z, shift, span)
            for k in range(4):
                total[k] = total[k] + ref[k * 8 : k * 8 + 8] * w
            total[3] = total[3] + ref[32:40] * pick(4 * z - 1, shift, span)
        for k in range(4):
            out[k * 8 : k * 8 + 8] = total[k]


def two_sum(a, b):
    s = a + b
    t = s - a
    return s, (a - (s - t)) + (b - t)


def pair_add(a, b):
    s, e = two_sum(a[0], b[0])
    e = e + (a[1] + b[1])
    h = s + e
    return h, e - (h - s)


def split(a):
    t = a * 4097.0
    h = t - (t - a)
    return h, a - h


def pair_times(a, c):
    p = a[0] * c
    ah, al = split(a[0])
    ch, cl = split(c)
    return p, ((ah * ch - p) + ah * cl + al * ch) + al * cl + a[1] * c


def moments(got):
    zero = jnp.zeros((8, LZ), f32)
    pairs = [(got[at : at + 8], zero) for at in range(0, got.shape[0], 8)]
    while len(pairs) > 1:
        pairs = [pair_add(a, b) for a, b in zip(pairs[::2], pairs[1::2])]
    h, l = pairs[0]
    rows = [(h[r : r + 1], l[r : r + 1]) for r in (0, 2, 4, 6)]
    t = pair_add(pair_add(rows[0], rows[1]), pair_add(rows[2], rows[3]))
    level = [t] + [tuple(pltpu.roll(p, LZ - 16 * k, 1) for p in t) for k in range(1, 6)]
    inside = lax.broadcasted_iota(jnp.int32, (1, LZ), 1) < 16

    def total(value):
        return jnp.sum(jnp.where(inside, value, 0.0), axis=1, keepdims=True)

    c = total(level[1][0]) / total(level[0][0])
    minus = jnp.broadcast_to(-c, (1, LZ))
    heads = [level[0]]
    while len(level) > 1:
        level = [pair_add(up, pair_times(at, minus)) for at, up in zip(level, level[1:])]
        heads.append(level[0])
    return c, [total(p[0] + p[1]) for p in heads]


def conjugate_gradient(c, m):
    def dot(a, b):
        s = None
        for i, ai in enumerate(a):
            for j, bj in enumerate(b):
                t = ai * bj * m[i + j]
                s = t if s is None else s + t
        return s

    def add(a, b, factor):
        longer = []
        for i in range(max(len(a), len(b))):
            if i >= len(b):
                longer.append(a[i])
            elif i >= len(a):
                longer.append(factor * b[i])
            else:
                longer.append(a[i] + factor * b[i])
        return longer

    def times(a, shift):
        return [a[0] * shift] + [a[i] * shift + a[i - 1] for i in range(1, len(a))] + [a[-1]]

    def plain(a):
        out = [a[-1]]
        for coefficient in a[-2::-1]:
            out = times(out, -c)
            out[0] = out[0] + coefficient
        return out

    one = jnp.ones((1, 1), f32)
    iterate, residual, direction = [], [one], [one]
    norm = m[0]
    for step in range(ITERS):
        img = times(direction, c)
        alpha = norm / dot(direction, img)
        iterate = add(iterate, direction, alpha)
        residual = add(residual, img, -alpha)
        if step < ITERS - 1:
            norm_next = dot(residual, residual)
            direction = add(residual, direction, norm_next / norm)
            norm = norm_next
    return plain(iterate), plain(residual)


def coefficients_kernel(got_ref, inv_ref, rhs_hbm, v1_hbm, rhs_ref, v1_ref, coef_ref, edge_ref, sems, *, table, ny):
    fetches = [pltpu.make_async_copy(rhs_hbm, rhs_ref, sems.at[0]), pltpu.make_async_copy(v1_hbm, v1_ref, sems.at[1])]
    for fetch in fetches:
        fetch.start()
    x, d = conjugate_gradient(*moments(got_ref[...]))
    inv = inv_ref[0:1, 0:1]
    for k, t in enumerate([t * inv for t in x] + d):
        coef_ref[k : k + 1] = jnp.broadcast_to(t, (1, LZ))
    coef_ref[7:8] = jnp.zeros((1, LZ), f32)
    below = lax.rem(lax.axis_index("gy") + ny - 1, ny)
    me = lax.axis_index("gx")
    nx = len(table)
    edge = jnp.zeros((1, LZ), f32)
    for offset, weight in enumerate(table):
        slab = lax.rem(me + nx - offset, nx)
        edge = edge + got_ref[pl.ds(2 * (slab * ny + below) + 1, 1), :] * weight
    edge_ref[...] = jnp.concatenate([edge, jnp.zeros((LY - 1, LZ), f32)], 0)
    for fetch in fetches:
        fetch.wait()


def last_kernel(prolong_ref, coef_ref, edge_ref, c0, c1, c2, c3, rhs_ref, v1_ref, v2_ref, p2_ref, rx_ref, ry_ref,
                sol_hbm, res_hbm, coarse_ref, sol_ref, res_ref, out_sems):
    coef = [jnp.broadcast_to(coef_ref[k : k + 1], (LY, LZ)) for k in range(7)]
    x, d = coef[:3], coef[3:]
    circ = [c0[k * 8 : k * 8 + 8] + c1[k * 8 : k * 8 + 8] + c2[k * 8 : k * 8 + 8] + c3[k * 8 : k * 8 + 8] for k in range(4)]
    coarse = d[0] * circ[0] + d[1] * circ[1] + d[2] * circ[2] + d[3] * (circ[3] + edge_ref[...])
    coarse_ref[...] = coarse
    stores = []
    for f in range(F):
        for a in range(A):
            at = (f * A + a) * CELLS
            spread = coarse * prolong_ref[f, a]
            for cell in range(LX):
                rows = slice(at + cell * LY, at + (cell + 1) * LY)
                v0 = rhs_ref[rows, :]
                v1, v2, img = (tile_of(ref, F * CELLS, f, a, cell) for ref in (v1_ref, v2_ref, p2_ref))
                if f == 0 and cell == 0:
                    img = img + tile_of(rx_ref, LY, 0, a, 0)
                sol_ref[rows, :] = x[0] * v0 + x[1] * v1 + x[2] * v2 + spread
                res_ref[rows, :] = d[0] * v0 + d[1] * v1 + d[2] * v2 + d[3] * img
        if f == 1:
            below = d[3][0:1] * ry_ref[...]
            for cell in range(LX):
                first = pl.ds(FACE + cell * LY, B, stride=CELLS)
                res_ref[first, :] = res_ref[first, :] + below[cell * B : (cell + 1) * B]
            first = pl.ds(FACE + B * CELLS, LX, stride=LY)
            res_ref[first, :] = res_ref[first, :] + below[B * LX :]
        rows = pl.ds(f * FACE, FACE)
        for i, (src, dst) in enumerate(((sol_ref, sol_hbm), (res_ref, res_hbm))):
            stores.append(pltpu.make_async_copy(src.at[rows], dst.at[rows], out_sems.at[2 * f + i]))
            stores[-1].start()
    for store in stores:
        store.wait()


def jacobi_weights(n):
    coarse = np.zeros(n)
    load = np.zeros(n)
    load[0] = 1.0
    for _ in range(SWEEPS):
        coarse = (load + np.roll(coarse, 1) + np.roll(coarse, -1)) / 2.2
    return coarse / 75.0


def struct(*shape):
    return jax.ShapeDtypeStruct(shape, f32)


PARAMS = pltpu.CompilerParams(vmem_limit_bytes=16 * 1024 * 1024)


def shards(rhs, kappa, mass, stiffness, mass_matrix, prolong):
    nx, ny = lax.axis_size("gx"), lax.axis_size("gy")
    vx, vy = A * LY, A * LX
    rhs2 = rhs.reshape(ROWS, LZ)
    k2 = kappa.reshape(CELLS, LZ)
    m2 = mass.reshape(CELLS, LZ)
    sends = [struct(n, LZ) for n in PARTS] + [struct(vx, LZ), struct(vy, LZ), struct(vy, LZ)]
    upper = [pltpu.VMEM((vx, LZ), f32), pltpu.VMEM((vy, LZ), f32)] + [pltpu.VMEM((8 * LY, LZ), f32)] * 2
    edges = [pltpu.VMEM((vx, LZ), f32)] * 2 + [pltpu.VMEM((vy, LZ), f32)] * 2

    def call(kernel, name, ins, outs, scratch=(), **static):
        specs = [i[1] if isinstance(i, tuple) else VM for i in ins]
        ins = [i[0] if isinstance(i, tuple) else i for i in ins]

        def bound(*refs):
            kernel(*refs, **static)

        return pl.pallas_call(
            bound,
            out_shape=outs,
            in_specs=specs,
            out_specs=[ANY if isinstance(o, pl.MemoryRef) else VM for o in outs],
            scratch_shapes=list(scratch),
            compiler_params=PARAMS,
            name=name,
        )(*ins)

    def swap(s):
        *near, far_x, near_y, far_y = s
        far_x = far_swap(far_x, "gx")
        far_y = far_swap(far_y, "gy")
        near_y = near_swap(near_y, "gy")
        return [far_x, far_y, near_y] + [near_swap(part, "gx") for part in near]

    hbm = pltpu.with_memory_space_constraint(rhs, pltpu.HBM)
    fx, fy = call(
        edge_kernel, "edges", [(hbm, ANY)], [struct(A, LY, LZ), struct(A, LX, LZ)],
        [pltpu.SemaphoreType.DMA, pltpu.SemaphoreType.DMA],
    )
    hx = shifted(fx.reshape(vx, LZ), "gx", -1)
    hy = shifted(fy.reshape(vy, LZ), "gy", -1)
    w, inv = call(
        weight_kernel, "weights", [stiffness, mass_matrix],
        [jax.ShapeDtypeStruct((2 * OUT, 3 * IN), bf16), struct(8, LZ)],
    )

    p0, *s = call(
        first_kernel, "first", [rhs2, hx, hy, k2, m2, w], [struct(ROWS, LZ)] + sends, upper[2:] + edges,
    )
    r = swap(s)
    v1, p1, *s, ux1, uy1, upx1, upy1 = call(
        second_kernel, "second", [p0, *r, *s, k2, m2, w],
        [struct(ROWS, LZ), struct(ROWS, LZ)] + sends + [struct(vx, LZ), struct(vy, LZ)] * 2, upper[2:] + [edges[1], edges[3]],
    )
    r = swap(s)
    sums, v1_kept = call(
        products_kernel, "products", [rhs2, v1, p1, ux1, uy1, upx1, upy1], [struct(48, LZ), pltpu.HBM((ROWS, LZ), f32)], [pltpu.SemaphoreType.DMA],
    )
    peers = nx * ny * 2
    v2, p2, upx, upy, loads, mom = call(
        third_kernel, "third", [p1, *r, *s, sums, k2, m2, w],
        [struct(ROWS, LZ)] * 2 + [struct(vx, LZ), struct(vy, LZ), struct(peers + 8, LZ), struct(peers, LZ)], upper,
    )
    table = [float(t) for t in jacobi_weights(nx)]
    group = [lax.ppermute(loads, "gx", [(i, i ^ b) for i in range(nx)]) for b in (1, 2, 3)]
    pieces = call(weigh_kernel, "weigh", [loads, *group], [struct(32, LZ)] * (nx // 4), table=table)
    coarse = [pieces[0]] + [shifted(p, "gx", 4 * z) for z, p in enumerate(pieces) if z]
    got = lax.all_to_all(mom.reshape(-1, 2, LZ), ("gx", "gy"), 0, 0, tiled=True).reshape(mom.shape)
    rx = shifted(upx, "gx", 1)
    ry = shifted(upy, "gy", 1)
    v0, v1_kept = (pltpu.with_memory_space_constraint(v, pltpu.HBM) for v in (rhs2, v1_kept))
    v0, v1, coef, edge = call(
        coefficients_kernel, "coefficients", [got, inv, (v0, ANY), (v1_kept, ANY)],
        [struct(ROWS, LZ)] * 2 + [struct(8, LZ), struct(LY, LZ)], [pltpu.SemaphoreType.DMA((2,))], table=table, ny=ny,
    )
    sol, res, coarse = call(
        last_kernel, "last", [(prolong, SM), coef, edge, *coarse, v0, v1, v2, p2, rx, ry],
        [pltpu.HBM((ROWS, LZ), f32)] * 2 + [struct(LY, LZ)],
        [pltpu.VMEM((ROWS, LZ), f32)] * 2 + [pltpu.SemaphoreType.DMA((6,))],
    )
    return sol.reshape(rhs.shape), res.reshape(rhs.shape), coarse[None]


def solution(mesh):
    placed = (
        P(None, None, "gx", "gy", None),
        P("gx", "gy", None),
        P("gx", "gy", None),
        P(),
        P(),
        P(),
    )
    return jax.shard_map(
        shards,
        mesh=mesh,
        in_specs=placed,
        out_specs=(
            P(None, None, "gx", "gy", None),
            P(None, None, "gx", "gy", None),
            P("gx", "gy", None),
        ),
        check_vma=False,
    )
```

```python
import jax
import jax.numpy as jnp
import numpy as np
from jax import lax
from jax.experimental import pallas as pl
from jax.experimental.pallas import tpu as pltpu
from jax.sharding import PartitionSpec as P

ITERS = 3
SWEEPS = 8
F, A = 3, 25
B = 24
LAST = 6 * B
OUT, IN = LAST + 8, LAST + 16
LX, LY, LZ = 4, 8, 128
CELLS = LX * LY
FACE = A * CELLS
ROWS = F * FACE
TAIL = F * CELLS * B
f32, bf16 = jnp.float32, jnp.bfloat16
VM = pl.BlockSpec(memory_space=pltpu.VMEM)
SM = pl.BlockSpec(memory_space=pltpu.SMEM)
ANY = pl.BlockSpec(memory_space=pl.ANY)


PARTS = (100, 100)


class Parts:
    def __init__(self, *refs):
        self.refs = refs

    def __getitem__(self, _):
        return jnp.concatenate([ref[...] for ref in self.refs], 0)

    def __setitem__(self, _, value):
        at = 0
        for ref in self.refs:
            ref[...] = value[at : at + ref.shape[0]]
            at += ref.shape[0]


def shifted(value, axis, by):
    n = lax.axis_size(axis)
    return lax.ppermute(value, axis, [(i, (i + by) % n) for i in range(n)])


def near_swap(value, axis):
    n = lax.axis_size(axis)
    return lax.ppermute(value, axis, [(i, i ^ 1) for i in range(n)])


def far_swap(value, axis):
    n = lax.axis_size(axis)
    pairs = [(i, (i + 1) % n) if i % 2 else (i, (i - 1) % n) for i in range(n)]
    return lax.ppermute(value, axis, pairs)


def halves(v):
    hi = v.astype(bf16)
    lo = (v - hi.astype(f32)).astype(bf16)
    return hi, lo


def apply_operator(v_ref, ux_ref, uy_ref, k_ref, m_ref, w_ref, out_ref, up_x, low_x, up_y, low_y, last_in, last_out, by_nodes=False):
    w_all = w_ref[...]
    at_first = lax.broadcasted_iota(jnp.int32, (LY, LZ), 0) == 0
    last_in[LAST // B * LY :] = jnp.zeros((2 * LY, LZ), f32)

    def block(ref, at, pitch, i):
        if by_nodes:
            return ref[pl.ds(at * A + i, B, stride=pitch), :]
        return ref[(at + i) * B : (at + i + 1) * B, :]

    def face(f, x, y):
        if f == 0 and x == LX:
            return block(ux_ref, 0, LY, y)
        if f == 1 and y == LY:
            return block(uy_ref, 0, LX, x)
        return block(v_ref, f * CELLS, CELLS, x * LY + y)

    def last_rows(f, x):
        if x == LX:
            return ux_ref[B * LY :, :]
        at = (f * FACE + B * CELLS if by_nodes else TAIL + f * CELLS) + x * LY
        return v_ref[at : at + LY, :]

    def put(f, x, y, value):
        at = (f * CELLS + x * LY + y) * B
        out_ref[at : at + B, :] = value

    def put_last(f, x, value):
        at = TAIL + f * CELLS + x * LY
        out_ref[at : at + LY, :] = value

    filler = jnp.zeros((IN - OUT, LZ), f32)
    carry = last_carry = None
    for x in range(LX):
        z_last = last_rows(2, x)
        y_last = last_rows(1, x)
        above = uy_ref[B * LX + x : B * LX + x + 1, :]
        top = lax.broadcasted_iota(jnp.int32, (LY, LZ), 0) == LY - 1
        y_up = jnp.where(top, jnp.broadcast_to(above, (LY, LZ)), pltpu.roll(y_last, LY - 1, 0))
        for j, tile in enumerate((last_rows(0, x), y_last, z_last, last_rows(0, x + 1), y_up, pltpu.roll(z_last, LZ - 1, 1))):
            last_in[j * LY : (j + 1) * LY] = tile
        columns = []
        for y in range(LY):
            z = face(2, x, y)
            six = [face(0, x, y), face(0, x + 1, y), face(1, x, y), face(1, x, y + 1), z, pltpu.roll(z, LZ - 1, 1)]
            columns.append(jnp.concatenate(six + [last_in[pl.ds(y, 8, stride=LY), :], filler], 0))
        hi, lo = halves(jnp.concatenate(columns, 1))
        prod = jnp.dot(w_all, jnp.concatenate([hi, lo, hi], 0), preferred_element_type=f32)
        parts = []
        for y in range(LY):
            k = k_ref[x * LY + y : x * LY + y + 1, :]
            m = m_ref[x * LY + y : x * LY + y + 1, :]
            cols = slice(y * LZ, (y + 1) * LZ)
            w = prod[:OUT, cols] * k + prod[OUT:, cols] * m
            parts.append([w[b * B : (b + 1) * B] for b in range(6)])
            last_out[pl.ds(y, 8, stride=LY), :] = w[LAST:]
        for y in range(LY):
            wlx, wux, wly, wuy, wlz, wuz = parts[y]
            put(0, x, y, wlx if x == 0 else wlx + carry[y])
            put(1, x, y, wly if y == 0 else wly + parts[y - 1][3])
            put(2, x, y, wlz + pltpu.roll(wuz, 1, 1))
            if x == 0 and low_x is not None:
                low_x[y * B : (y + 1) * B] = wlx
            if x == LX - 1:
                up_x[y * B : (y + 1) * B] = wux
        tiles = [last_out[j * LY : (j + 1) * LY] for j in range(6)]
        put_last(0, x, tiles[0] if x == 0 else tiles[0] + last_carry)
        put_last(1, x, tiles[1] + jnp.where(at_first, 0.0, pltpu.roll(tiles[4], 1, 0)))
        put_last(2, x, tiles[2] + pltpu.roll(tiles[5], 1, 1))
        if x == 0 and low_x is not None:
            low_x[B * LY :] = tiles[0]
        if x == LX - 1:
            up_x[B * LY :] = tiles[3]
        if low_y is not None:
            low_y[x * B : (x + 1) * B] = parts[0][2]
            low_y[B * LX + x : B * LX + x + 1] = tiles[1][:1]
        up_y[x * B : (x + 1) * B] = parts[LY - 1][3]
        up_y[B * LX + x : B * LX + x + 1] = tiles[4][LY - 1 :]
        carry = [parts[y][1] for y in range(LY)]
        last_carry = tiles[3]


def is_even(axis):
    return lax.rem(lax.axis_index(axis), 2) == 0


def route(even, up, low, near, far):
    near[...] = jnp.where(even, up[...], low[...])
    far[...] = jnp.where(even, low[...], up[...])


def edge_kernel(rhs_ref, fx_ref, fy_ref, sem_x, sem_y):
    face_x = pltpu.make_async_copy(rhs_ref.at[0, :, 0], fx_ref, sem_x)
    face_y = pltpu.make_async_copy(rhs_ref.at[1, :, :, 0], fy_ref, sem_y)
    face_x.start()
    face_y.start()
    face_x.wait()
    face_y.wait()


def weight_kernel(s_ref, m_ref, w_ref, inv_ref):
    n = 6 * A

    def placing(rows, span):
        r = lax.broadcasted_iota(jnp.int32, (rows, n), 0)
        c = lax.broadcasted_iota(jnp.int32, (rows, n), 1)
        p = lax.rem(r, span)
        j = p - LAST
        node = jnp.where(p < LAST, lax.div(p, B) * A + lax.rem(p, B), (2 * lax.rem(j, 3) + lax.div(j, 3)) * A + B)
        return (node == c) & (p < n), lax.div(r, span)

    def ones(mask):
        return jnp.where(mask, 1.0, 0.0).astype(bf16)

    rows = ones(placing(OUT, OUT)[0])
    mask, third = placing(3 * IN, IN)
    columns = (ones(mask & (third < 2)), ones(mask & (third == 2)))
    diagonal = lax.broadcasted_iota(jnp.int32, (n, n), 0) == lax.broadcasted_iota(jnp.int32, (n, n), 1)

    def largest(v):
        return jnp.max(jnp.max(jnp.where(diagonal, v, 0.0), 0, keepdims=True), 1, keepdims=True)

    inv = 1.0 / (10.0 * largest(s_ref[...]) + 2.0 * largest(m_ref[...]))
    inv_ref[...] = jnp.broadcast_to(inv, (8, LZ))
    for i, ref in enumerate((s_ref, m_ref)):
        full = 0.0
        for part, place in zip(halves(ref[...] * inv), columns):
            moved = jnp.dot(rows, part, preferred_element_type=f32).astype(bf16)
            full = full + lax.dot_general(moved, place, (((1,), (1,)), ((), ())), preferred_element_type=f32)
        w_ref[i * OUT : (i + 1) * OUT] = full.astype(bf16)


def first_kernel(rhs_ref, hx_ref, hy_ref, k_ref, m_ref, w_ref,
                 p_ref, sn0, sn1, sfx, sny, sfy, last_in, last_out, upx, lowx, upy, lowy):
    apply_operator(rhs_ref, hx_ref, hy_ref, k_ref, m_ref, w_ref, p_ref, upx, lowx, upy, lowy, last_in, last_out, True)
    route(is_even("gx"), upx, lowx, Parts(sn0, sn1), sfx)
    route(is_even("gy"), upy, lowy, sny, sfy)


def assemble(p_ref, snx, sfx, sny, sfy, rnx, rfx, rny, rfy, v, ux, uy):
    even_x = is_even("gx")
    even_y = is_even("gy")
    v[...] = p_ref[...]
    below_x = jnp.where(even_x, rfx[...], rnx[...])
    v[: B * LY] = v[: B * LY] + below_x[: B * LY]
    v[TAIL : TAIL + LY] = v[TAIL : TAIL + LY] + below_x[B * LY :]
    below_y = jnp.where(even_y, rfy[...], rny[...])
    for x in range(LX):
        at = (CELLS + x * LY) * B
        v[at : at + B] = v[at : at + B] + below_y[x * B : (x + 1) * B]
        at = TAIL + CELLS + x * LY
        v[at : at + 1] = v[at : at + 1] + below_y[B * LX + x : B * LX + x + 1]
    ux[...] = jnp.where(even_x, snx[...] + rnx[...], sfx[...] + rfx[...])
    uy[...] = jnp.where(even_y, sny[...] + rny[...], sfy[...] + rfy[...])


def node_sum(value):
    return jnp.sum(value.reshape(-1, LY, LZ), 0)


def row(tile):
    return jnp.sum(tile, 0, keepdims=True)


def second_kernel(p_ref, rfx, rfy, rny, rn0, rn1, sn0, sn1, sfx, sny, sfy, k_ref, m_ref, w_ref,
                  v1_ref, p1_ref, tn0, tn1, tfx, tny, tfy, ux, uy, last_in, last_out, upx, lowx, upy, lowy):
    assemble(p_ref, Parts(sn0, sn1), sfx, sny, sfy, Parts(rn0, rn1), rfx, rny, rfy, v1_ref, ux, uy)
    apply_operator(v1_ref, ux, uy, k_ref, m_ref, w_ref, p1_ref, upx, lowx, upy, lowy, last_in, last_out)
    route(is_even("gx"), upx, lowx, Parts(tn0, tn1), tfx)
    route(is_even("gy"), upy, lowy, tny, tfy)


def element_sum(ref, faces):
    rows = []
    for y in range(LY):
        total = 0.0
        for at in range(0, faces, LY):
            first = (at + y) * B
            total = total + (ref[first : first + 8] + ref[first + 8 : first + 16] + ref[first + 16 : first + B])
        rows.append(row(total))
    return jnp.concatenate(rows, 0) + node_sum(ref[faces * B :])


def tile_of(ref, faces, f, a, x):
    at = f * CELLS + x * LY
    if a == B:
        return ref[faces * B + at : faces * B + at + LY, :]
    return ref[pl.ds(at * B + a, LY, stride=B), :]


def products_kernel(v0_ref, v1_ref, sums_ref, v1_hbm, sem):
    keep = pltpu.make_async_copy(v1_ref, v1_hbm, sem)
    keep.start()
    s0 = s1 = s00 = s01 = s11 = 0.0
    for f in range(F):
        for a in range(A):
            for x in range(LX):
                at = (f * A + a) * CELLS + x * LY
                v0 = v0_ref[at : at + LY, :]
                v1 = tile_of(v1_ref, F * CELLS, f, a, x)
                s0, s1, s00, s01, s11 = s0 + v0, s1 + v1, s00 + v0 * v0, s01 + v0 * v1, s11 + v1 * v1
    for k, s in enumerate((s0, s1, s00, s01, s11)):
        sums_ref[8 * k : 8 * k + 8] = s
    keep.wait()


def third_kernel(p_ref, v1_ref, rfx, rfy, rny, rn0, rn1, sn0, sn1, sfx, sny, sfy, sums_ref, k_ref, m_ref, w_ref,
                 v2_ref, p2_ref, upx, upy, loads_ref, mom_ref, ux, uy, last_in, last_out):
    assemble(p_ref, Parts(sn0, sn1), sfx, sny, sfy, Parts(rn0, rn1), rfx, rny, rfy, v2_ref, ux, uy)
    v1 = v1_ref[...]
    v2 = v2_ref[...]
    loads_ref[0:16] = sums_ref[0:16]
    loads_ref[16:24] = element_sum(v2_ref, F * CELLS)
    m3 = node_sum(v1 * v2)
    m4 = node_sum(v2 * v2)
    apply_operator(v2_ref, ux, uy, k_ref, m_ref, w_ref, p2_ref, upx, None, upy, None, last_in, last_out)
    loads_ref[24:32] = element_sum(p2_ref, F * CELLS)
    loads_ref[32:40] = element_sum(upx, LY)
    energy = node_sum(v2_ref[...] * p2_ref[...]) + node_sum(ux[...] * upx[...])
    tail = row(uy[...] * upy[...])
    tile = jnp.concatenate(
        [row(sums_ref[16 + 8 * k : 24 + 8 * k]) for k in range(3)]
        + [row(m3), row(m4), row(energy) + tail, jnp.zeros((2, LZ), f32)], 0,
    )
    for lanes in (64, 32, 16):
        tile = tile + pltpu.roll(tile, lanes, 1)
    lane = lax.broadcasted_iota(jnp.int32, (8, LZ), 1)
    moment = lax.broadcasted_iota(jnp.int32, (8, LZ), 0)
    packed = row(jnp.where(lax.div(lane, 16) == moment, tile, 0.0))
    pair = jnp.concatenate([packed, row(upy[...])] * 4, 0)
    for at in range(0, mom_ref.shape[0], 8):
        mom_ref[at : at + 8] = pair
    loads_ref[40:] = jnp.zeros((loads_ref.shape[0] - 40, LZ), f32)


def weigh_kernel(own, near, far, both, *outs, table):
    nx = len(table)
    q = lax.rem(lax.axis_index("gx"), 4)
    low, high = lax.rem(q, 2) == 0, q < 2
    one, two = jnp.where(low, 1, -1), jnp.where(high, 2, -2)
    sources = ((own, 0, (0,)), (near, one, (1, -1)), (far, two, (2, -2)), (both, one + two, (3, 1, -1, -3)))

    def pick(at, shift, span):
        value = jnp.float32(table[(at - span[0]) % nx])
        for s in span[1:]:
            value = jnp.where(shift == s, table[(at - s) % nx], value)
        return value

    for z, out in enumerate(outs):
        total = [0.0] * 4
        for ref, shift, span in sources:
            w = pick(4 * z, shift, span)
            for k in range(4):
                total[k] = total[k] + ref[k * 8 : k * 8 + 8] * w
            total[3] = total[3] + ref[32:40] * pick(4 * z - 1, shift, span)
        for k in range(4):
            out[k * 8 : k * 8 + 8] = total[k]


def two_sum(a, b):
    s = a + b
    t = s - a
    return s, (a - (s - t)) + (b - t)


def pair_add(a, b):
    s, e = two_sum(a[0], b[0])
    e = e + (a[1] + b[1])
    h = s + e
    return h, e - (h - s)


def split(a):
    t = a * 4097.0
    h = t - (t - a)
    return h, a - h


def pair_times(a, c):
    p = a[0] * c
    ah, al = split(a[0])
    ch, cl = split(c)
    return p, ((ah * ch - p) + ah * cl + al * ch) + al * cl + a[1] * c


def moments(got):
    zero = jnp.zeros((8, LZ), f32)
    pairs = [(got[at : at + 8], zero) for at in range(0, got.shape[0], 8)]
    while len(pairs) > 1:
        pairs = [pair_add(a, b) for a, b in zip(pairs[::2], pairs[1::2])]
    h, l = pairs[0]
    rows = [(h[r : r + 1], l[r : r + 1]) for r in (0, 2, 4, 6)]
    t = pair_add(pair_add(rows[0], rows[1]), pair_add(rows[2], rows[3]))
    level = [t] + [tuple(pltpu.roll(p, LZ - 16 * k, 1) for p in t) for k in range(1, 6)]
    inside = lax.broadcasted_iota(jnp.int32, (1, LZ), 1) < 16

    def total(value):
        return jnp.sum(jnp.where(inside, value, 0.0), axis=1, keepdims=True)

    c = total(level[1][0]) / total(level[0][0])
    minus = jnp.broadcast_to(-c, (1, LZ))
    heads = [level[0]]
    while len(level) > 1:
        level = [pair_add(up, pair_times(at, minus)) for at, up in zip(level, level[1:])]
        heads.append(level[0])
    return c, [total(p[0] + p[1]) for p in heads]


def conjugate_gradient(c, m):
    def dot(a, b):
        s = None
        for i, ai in enumerate(a):
            for j, bj in enumerate(b):
                t = ai * bj * m[i + j]
                s = t if s is None else s + t
        return s

    def add(a, b, factor):
        longer = []
        for i in range(max(len(a), len(b))):
            if i >= len(b):
                longer.append(a[i])
            elif i >= len(a):
                longer.append(factor * b[i])
            else:
                longer.append(a[i] + factor * b[i])
        return longer

    def times(a, shift):
        return [a[0] * shift] + [a[i] * shift + a[i - 1] for i in range(1, len(a))] + [a[-1]]

    def plain(a):
        out = [a[-1]]
        for coefficient in a[-2::-1]:
            out = times(out, -c)
            out[0] = out[0] + coefficient
        return out

    one = jnp.ones((1, 1), f32)
    iterate, residual, direction = [], [one], [one]
    norm = m[0]
    for step in range(ITERS):
        img = times(direction, c)
        alpha = norm / dot(direction, img)
        iterate = add(iterate, direction, alpha)
        residual = add(residual, img, -alpha)
        if step < ITERS - 1:
            norm_next = dot(residual, residual)
            direction = add(residual, direction, norm_next / norm)
            norm = norm_next
    return plain(iterate), plain(residual)


def coefficients_kernel(got_ref, inv_ref, rhs_hbm, v1_hbm, rhs_ref, v1_ref, coef_ref, edge_ref, sems, *, table, ny):
    fetches = [pltpu.make_async_copy(rhs_hbm, rhs_ref, sems.at[0]), pltpu.make_async_copy(v1_hbm, v1_ref, sems.at[1])]
    for fetch in fetches:
        fetch.start()
    x, d = conjugate_gradient(*moments(got_ref[...]))
    inv = inv_ref[0:1, 0:1]
    for k, t in enumerate([t * inv for t in x] + d):
        coef_ref[k : k + 1] = jnp.broadcast_to(t, (1, LZ))
    coef_ref[7:8] = jnp.zeros((1, LZ), f32)
    below = lax.rem(lax.axis_index("gy") + ny - 1, ny)
    me = lax.axis_index("gx")
    nx = len(table)
    edge = jnp.zeros((1, LZ), f32)
    for offset, weight in enumerate(table):
        slab = lax.rem(me + nx - offset, nx)
        edge = edge + got_ref[pl.ds(2 * (slab * ny + below) + 1, 1), :] * weight
    edge_ref[...] = jnp.concatenate([edge, jnp.zeros((LY - 1, LZ), f32)], 0)
    for fetch in fetches:
        fetch.wait()


def last_kernel(prolong_ref, coef_ref, edge_ref, c0, c1, c2, c3, rhs_ref, v1_ref, v2_ref, p2_ref, rx_ref, ry_ref,
                sol_hbm, res_hbm, coarse_ref, sol_ref, res_ref, out_sems):
    coef = [jnp.broadcast_to(coef_ref[k : k + 1], (LY, LZ)) for k in range(7)]
    x, d = coef[:3], coef[3:]
    circ = [c0[k * 8 : k * 8 + 8] + c1[k * 8 : k * 8 + 8] + c2[k * 8 : k * 8 + 8] + c3[k * 8 : k * 8 + 8] for k in range(4)]
    coarse = d[0] * circ[0] + d[1] * circ[1] + d[2] * circ[2] + d[3] * (circ[3] + edge_ref[...])
    coarse_ref[...] = coarse
    stores = []
    for part, (begin, end) in enumerate(((0, 8), (8, A), (A, 2 * A), (2 * A, 3 * A))):
        for f, a in (divmod(n, A) for n in range(begin, end)):
            at = (f * A + a) * CELLS
            spread = coarse * prolong_ref[f, a]
            for cell in range(LX):
                rows = slice(at + cell * LY, at + (cell + 1) * LY)
                v0 = rhs_ref[rows, :]
                v1, v2, img = (tile_of(ref, F * CELLS, f, a, cell) for ref in (v1_ref, v2_ref, p2_ref))
                if f == 0 and cell == 0:
                    img = img + tile_of(rx_ref, LY, 0, a, 0)
                sol_ref[rows, :] = x[0] * v0 + x[1] * v1 + x[2] * v2 + spread
                res_ref[rows, :] = d[0] * v0 + d[1] * v1 + d[2] * v2 + d[3] * img
        if begin == A:
            below = d[3][0:1] * ry_ref[...]
            for cell in range(LX):
                first = pl.ds(FACE + cell * LY, B, stride=CELLS)
                res_ref[first, :] = res_ref[first, :] + below[cell * B : (cell + 1) * B]
            first = pl.ds(FACE + B * CELLS, LX, stride=LY)
            res_ref[first, :] = res_ref[first, :] + below[B * LX :]
        rows = pl.ds(begin * CELLS, (end - begin) * CELLS)
        for i, (src, dst) in enumerate(((sol_ref, sol_hbm), (res_ref, res_hbm))):
            stores.append(pltpu.make_async_copy(src.at[rows], dst.at[rows], out_sems.at[2 * part + i]))
            stores[-1].start()
    for store in stores:
        store.wait()


def jacobi_weights(n):
    coarse = np.zeros(n)
    load = np.zeros(n)
    load[0] = 1.0
    for _ in range(SWEEPS):
        coarse = (load + np.roll(coarse, 1) + np.roll(coarse, -1)) / 2.2
    return coarse / 75.0


def struct(*shape):
    return jax.ShapeDtypeStruct(shape, f32)


PARAMS = pltpu.CompilerParams(vmem_limit_bytes=16 * 1024 * 1024)


def shards(rhs, kappa, mass, stiffness, mass_matrix, prolong):
    nx, ny = lax.axis_size("gx"), lax.axis_size("gy")
    vx, vy = A * LY, A * LX
    rhs2 = rhs.reshape(ROWS, LZ)
    k2 = kappa.reshape(CELLS, LZ)
    m2 = mass.reshape(CELLS, LZ)
    sends = [struct(n, LZ) for n in PARTS] + [struct(vx, LZ), struct(vy, LZ), struct(vy, LZ)]
    upper = [pltpu.VMEM((vx, LZ), f32), pltpu.VMEM((vy, LZ), f32)] + [pltpu.VMEM((8 * LY, LZ), f32)] * 2
    edges = [pltpu.VMEM((vx, LZ), f32)] * 2 + [pltpu.VMEM((vy, LZ), f32)] * 2

    def call(kernel, name, ins, outs, scratch=(), **static):
        specs = [i[1] if isinstance(i, tuple) else VM for i in ins]
        ins = [i[0] if isinstance(i, tuple) else i for i in ins]

        def bound(*refs):
            kernel(*refs, **static)

        return pl.pallas_call(
            bound,
            out_shape=outs,
            in_specs=specs,
            out_specs=[ANY if isinstance(o, pl.MemoryRef) else VM for o in outs],
            scratch_shapes=list(scratch),
            compiler_params=PARAMS,
            name=name,
        )(*ins)

    def swap(s):
        *near, far_x, near_y, far_y = s
        far_x = far_swap(far_x, "gx")
        far_y = far_swap(far_y, "gy")
        near_y = near_swap(near_y, "gy")
        return [far_x, far_y, near_y] + [near_swap(part, "gx") for part in near]

    hbm = pltpu.with_memory_space_constraint(rhs, pltpu.HBM)
    fx, fy = call(
        edge_kernel, "edges", [(hbm, ANY)], [struct(A, LY, LZ), struct(A, LX, LZ)],
        [pltpu.SemaphoreType.DMA, pltpu.SemaphoreType.DMA],
    )
    hx = shifted(fx.reshape(vx, LZ), "gx", -1)
    hy = shifted(fy.reshape(vy, LZ), "gy", -1)
    w, inv = call(
        weight_kernel, "weights", [stiffness, mass_matrix],
        [jax.ShapeDtypeStruct((2 * OUT, 3 * IN), bf16), struct(8, LZ)],
    )

    p0, *s = call(
        first_kernel, "first", [rhs2, hx, hy, k2, m2, w], [struct(ROWS, LZ)] + sends, upper[2:] + edges,
    )
    r = swap(s)
    v1, p1, *s = call(
        second_kernel, "second", [p0, *r, *s, k2, m2, w],
        [struct(ROWS, LZ), struct(ROWS, LZ)] + sends, upper + edges,
    )
    r = swap(s)
    sums, v1_kept = call(
        products_kernel, "products", [rhs2, v1], [struct(40, LZ), pltpu.HBM((ROWS, LZ), f32)], [pltpu.SemaphoreType.DMA],
    )
    peers = nx * ny * 2
    v2, p2, upx, upy, loads, mom = call(
        third_kernel, "third", [p1, v1, *r, *s, sums, k2, m2, w],
        [struct(ROWS, LZ)] * 2 + [struct(vx, LZ), struct(vy, LZ), struct(peers + 8, LZ), struct(peers, LZ)], upper,
    )
    table = [float(t) for t in jacobi_weights(nx)]
    group = [lax.ppermute(loads, "gx", [(i, i ^ b) for i in range(nx)]) for b in (1, 2, 3)]
    pieces = call(weigh_kernel, "weigh", [loads, *group], [struct(32, LZ)] * (nx // 4), table=table)
    coarse = [pieces[0]] + [shifted(p, "gx", 4 * z) for z, p in enumerate(pieces) if z]
    got = lax.all_to_all(mom.reshape(-1, 2, LZ), ("gx", "gy"), 0, 0, tiled=True).reshape(mom.shape)
    rx = shifted(upx, "gx", 1)
    ry = shifted(upy, "gy", 1)
    v0, v1_kept = (pltpu.with_memory_space_constraint(v, pltpu.HBM) for v in (rhs2, v1_kept))
    v0, v1, coef, edge = call(
        coefficients_kernel, "coefficients", [got, inv, (v0, ANY), (v1_kept, ANY)],
        [struct(ROWS, LZ)] * 2 + [struct(8, LZ), struct(LY, LZ)], [pltpu.SemaphoreType.DMA((2,))], table=table, ny=ny,
    )
    sol, res, coarse = call(
        last_kernel, "last", [(prolong, SM), coef, edge, *coarse, v0, v1, v2, p2, rx, ry],
        [pltpu.HBM((ROWS, LZ), f32)] * 2 + [struct(LY, LZ)],
        [pltpu.VMEM((ROWS, LZ), f32)] * 2 + [pltpu.SemaphoreType.DMA((8,))],
    )
    return sol.reshape(rhs.shape), res.reshape(rhs.shape), coarse[None]


def solution(mesh):
    placed = (
        P(None, None, "gx", "gy", None),
        P("gx", "gy", None),
        P("gx", "gy", None),
        P(),
        P(),
        P(),
    )
    return jax.shard_map(
        shards,
        mesh=mesh,
        in_specs=placed,
        out_specs=(
            P(None, None, "gx", "gy", None),
            P(None, None, "gx", "gy", None),
            P("gx", "gy", None),
        ),
        check_vma=False,
    )
```
